128 devices in a mesh: blk: 4 (over x), tok: 32 (over y, z, core).
Axes of the slice: x: 4, y: 4, z: 4, core: 2. Of those that a mesh axis runs over, the one named last changes fastest.
Arguments:
- inputs: bfloat16 [16384, 2048], P(('blk', 'tok')), may hold values from -6 to 6
- mix_scale: bfloat16 [2048], P('tok'), may hold values from 0.5 to 1.5
- branch_mat: bfloat16 [2048, 2560], P('tok', 'blk'), may hold values from -0.125 to 0.125
- input_mat: bfloat16 [2048, 2560], P('tok', 'blk'), may hold values from -0.125 to 0.125
- conv_taps: bfloat16 [4, 2560], P(None, ('blk', 'tok')), may hold values from -3 to 3
- conv_shift: bfloat16 [2560], P(('blk', 'tok')), may hold values from -2 to 2
- rate_mat: bfloat16 [16, 160, 160], P('blk', 'tok'), may hold values from -0.5 to 0.5
- rate_shift: bfloat16 [2560], P(('blk', 'tok')), may hold values from -2 to 2
- entry_mat: bfloat16 [16, 160, 160], P('blk', 'tok'), may hold values from -0.5 to 0.5
- entry_shift: bfloat16 [2560], P(('blk', 'tok')), may hold values from -2 to 2
- decay_logit: bfloat16 [2560], P(('blk', 'tok')), may hold values from 5 to 14
- out_mat: bfloat16 [2560, 2048], P('blk', 'tok'), may hold values from -0.25 to 0.25
- feed_scale: bfloat16 [2048], P('tok'), may hold values from 0.5 to 1.5
- gate_mat: bfloat16 [2048, 6144], P('tok', 'blk'), may hold values from -0.125 to 0.125
- up_mat: bfloat16 [2048, 6144], P('tok', 'blk'), may hold values from -0.125 to 0.125
- down_mat: bfloat16 [6144, 2048], P('blk', 'tok'), may hold values from -0.15625 to 0.15625
- lengths: int32 [5], replicated, may hold values from 1024 to 8192, as said below
- cotangent: bfloat16 [16384, 2048], P(('blk', 'tok')), may hold values from -6 to 6
Outputs:
- layer_out: bfloat16 [16384, 2048], P(('blk', 'tok'))
- inputs_grad: bfloat16 [16384, 2048], P(('blk', 'tok'))
- mix_scale_grad: float32 [2048], P('tok')
- branch_mat_grad: float32 [2048, 2560], P('tok', 'blk')
- input_mat_grad: float32 [2048, 2560], P('tok', 'blk')
- conv_taps_grad: float32 [4, 2560], P(None, ('blk', 'tok'))
- conv_shift_grad: float32 [2560], P(('blk', 'tok'))
- rate_mat_grad: float32 [16, 160, 160], P('blk', 'tok')
- rate_shift_grad: float32 [2560], P(('blk', 'tok'))
- entry_mat_grad: float32 [16, 160, 160], P('blk', 'tok')
- entry_shift_grad: float32 [2560], P(('blk', 'tok'))
- decay_logit_grad: float32 [2560], P(('blk', 'tok'))
- out_mat_grad: float32 [2560, 2048], P('blk', 'tok')
- feed_scale_grad: float32 [2048], P('tok')
- gate_mat_grad: float32 [2048, 6144], P('tok', 'blk')
- up_mat_grad: float32 [2048, 6144], P('tok', 'blk')
- down_mat_grad: float32 [6144, 2048], P('blk', 'tok')
The draws below stay inside these ranges and needn't reach their ends.
Inputs may be any that keep to these rules, and one draw needn't show every extreme that they name: `lengths`: token counts of the items laid end to end in this order; they sum to 16384, and one item has exactly 8192 tokens.
All inputs are finite; a program needn't handle non-finite values.
Results may differ from the reference program's by a relative error of at most 0.023.
Values may be sent and summed in bfloat16 or wider, within the bound.
No kernel may reach another device: no remote copies, remote signals or barrier semaphores. Data moves between devices by JAX's collectives and lax.ppermute only.
A program may use at most 192 MiB of HBM per device.

```python
import jax
import jax.numpy as jnp
from jax import lax

D = 2048
H = 16
BW = 160
R = 2560
F = 6144
CONV = 4
TOKENS = 16384
SHORTS = 4
ITEMS = 5
LEAST = 1024


def draw_lengths(key, part):
    key = jax.random.fold_in(key, 7)
    spare_tokens = TOKENS // 2 - SHORTS * LEAST
    cut_points = jnp.sort(jax.random.randint(jax.random.fold_in(key, 1), (SHORTS - 1,), 0, spare_tokens + 1))
    bounds = jnp.concatenate([jnp.zeros((1,), jnp.int32), cut_points.astype(jnp.int32), jnp.full((1,), spare_tokens, jnp.int32)])
    shares = bounds[1:] - bounds[:-1]
    if SHORTS > 1:
        shares = shares.at[1].add(shares[0]).at[0].set(0)
    item_lengths = jnp.concatenate([jnp.full((1,), TOKENS // 2, jnp.int32), LEAST + shares])
    shuffle = jax.random.permutation(jax.random.fold_in(key, 2), ITEMS)
    return item_lengths[shuffle].astype(jnp.int32)


def block_scale(stream_key, dims, pieces, low, largest):
    level, own = 1.0, jax.random.fold_in(stream_key, 6)
    for dim, parts in pieces:
        heights = jnp.exp(jax.random.uniform(jax.random.fold_in(own, dim), (parts,), jnp.float32, low / len(pieces), largest / len(pieces)))
        level = level * jnp.repeat(heights, dims[dim] // parts).reshape([-1 if axis == dim else 1 for axis in range(len(dims))])
    return level


def scatter_about(key, dims, scale, most, cuts=(), held_as=jnp.bfloat16):
    array = scale * jax.random.normal(key, dims, jnp.float32)
    if cuts:
        array = array * block_scale(key, dims, cuts, -0.22, 0.18)
    return jnp.clip(array, -most, most).astype(held_as)


def setup_inputs(seed: int = 0) -> dict:
    key_of = jax.random.split(jax.random.key(seed), 19)
    inputs = scatter_about(key_of[0], (TOKENS, D), 1.0, 6.0, ((0, 128),))
    mix_scale = jnp.clip(1.0 + 0.1 * jax.random.normal(key_of[1], (D,), jnp.float32), 0.5, 1.5).astype(jnp.bfloat16)
    branch_mat = scatter_about(key_of[2], (D, R), D ** -0.5, 0.125, ((0, 32), (1, 4)))
    input_mat = scatter_about(key_of[3], (D, R), D ** -0.5, 0.125, ((0, 32), (1, 4)))
    conv_taps = scatter_about(key_of[4], (CONV, R), CONV ** -0.5, 3.0, ((1, 128),))
    conv_shift = scatter_about(key_of[5], (R,), 0.5, 2.0, ((0, 128),))
    rate_mat = scatter_about(key_of[6], (H, BW, BW), BW ** -0.5, 0.5, ((0, 4), (1, 32)))
    rate_shift = scatter_about(key_of[7], (R,), 0.5, 2.0, ((0, 128),))
    entry_mat = scatter_about(key_of[8], (H, BW, BW), BW ** -0.5, 0.5, ((0, 4), (1, 32)))
    entry_shift = scatter_about(key_of[9], (R,), 0.5, 2.0, ((0, 128),))
    decay_logit = jnp.clip(5.0 + 9.0 * jax.random.uniform(key_of[10], (R,), jnp.float32) ** block_scale(key_of[10], (R,), ((0, 128),), -0.2, 0.2), 5.0, 14.0).astype(jnp.bfloat16)
    out_mat = scatter_about(key_of[11], (R, D), (R // 4) ** -0.5, 0.25, ((0, 4), (1, 32)))
    feed_scale = jnp.clip(1.0 + 0.1 * jax.random.normal(key_of[12], (D,), jnp.float32), 0.5, 1.5).astype(jnp.bfloat16)
    gate_mat = scatter_about(key_of[13], (D, F), D ** -0.5, 0.125, ((0, 32), (1, 4)))
    up_mat = scatter_about(key_of[14], (D, F), D ** -0.5, 0.125, ((0, 32), (1, 4)))
    down_mat = scatter_about(key_of[15], (F, D), (F // 4) ** -0.5, 0.15625, ((0, 4), (1, 32)))
    lengths = draw_lengths(jax.random.fold_in(key_of[18], 71), 0)
    cotangent = scatter_about(key_of[17], (TOKENS, D), 1.0, 6.0, ((0, 128),))
    return {"inputs": inputs, "mix_scale": mix_scale, "branch_mat": branch_mat, "input_mat": input_mat, "conv_taps": conv_taps, "conv_shift": conv_shift, "rate_mat": rate_mat, "rate_shift": rate_shift, "entry_mat": entry_mat, "entry_shift": entry_shift, "decay_logit": decay_logit, "out_mat": out_mat, "feed_scale": feed_scale, "gate_mat": gate_mat, "up_mat": up_mat, "down_mat": down_mat, "lengths": lengths, "cotangent": cotangent}


@jax.custom_vjp
def low(v):
    return lax.optimization_barrier(v.astype(jnp.bfloat16)).astype(jnp.float32)

@jax.custom_vjp
def low_back(v):
    return v

def low_keep(v):
    return (low(v), None)

def low_pass(kept, grad):
    return (grad,)

def back_keep(v):
    return (v, None)

def back_low(kept, grad):
    return (low(grad),)
low.defvjp(low_keep, low_pass)
low_back.defvjp(back_keep, back_low)
eps_norm = 1e-06
decay_power = 8.0
highest = lax.Precision.HIGHEST

def product(former, latter):
    return jnp.dot(former, latter, precision=highest, preferred_element_type=jnp.float32)

def compose(former, latter):
    return (former[0] * latter[0], former[1] * latter[0] + latter[1])

def normalize(values, gains):
    factor = lax.rsqrt(lax.optimization_barrier(jnp.mean(values * values, axis=-1, keepdims=True)) + eps_norm)
    return values * factor * gains

def positions(lengths, total_tokens):
    tokens = jnp.arange(total_tokens, dtype=jnp.int32)
    item_ends = jnp.cumsum(lengths).astype(jnp.int32)
    starts = item_ends - lengths.astype(jnp.int32)
    opened = lax.optimization_barrier(jnp.max(jnp.where(starts[None, :] <= tokens[:, None], starts[None, :], 0), axis=1))
    return (tokens - opened)[:, None]

def forward(inputs, mix_scale, branch_mat, input_mat, conv_taps, conv_shift, rate_mat, rate_shift, entry_mat, entry_shift, decay_logit, out_mat, feed_scale, gate_mat, up_mat, down_mat, places):
    normed_one = low(normalize(inputs, mix_scale))
    gated_branch = jax.nn.gelu(low_back(product(normed_one, branch_mat)))
    conv_input = low(low_back(product(normed_one, input_mat)))
    convolved = conv_shift + conv_taps[0] * conv_input
    for tap_index in range(1, CONV):
        lagged = jnp.concatenate([jnp.zeros((tap_index, conv_input.shape[1]), jnp.float32), conv_input[:-tap_index]], axis=0)
        convolved = convolved + conv_taps[tap_index] * jnp.where(places >= tap_index, lagged, 0.0)
    grouped = convolved.reshape(-1, H, BW)
    rates = jax.nn.sigmoid(jnp.einsum('nhc,hcd->nhd', grouped, rate_mat, precision=highest).reshape(-1, R) + rate_shift)
    entries = jax.nn.sigmoid(jnp.einsum('nhc,hcd->nhd', grouped, entry_mat, precision=highest).reshape(-1, R) + entry_shift)
    log_keep = -decay_power * jax.nn.softplus(-decay_logit) * rates
    resets = places == 0
    keeps = jnp.where(resets, 0.0, jnp.exp(log_keep))
    scaling = jnp.where(resets, 1.0, jnp.sqrt(-jnp.expm1(2.0 * log_keep)))
    drives = entries * convolved * scaling
    states = lax.associative_scan(compose, (keeps, drives), axis=0)[1]
    mixture = low(states * gated_branch)
    middle = inputs + low_back(product(mixture, out_mat))
    normed_two = low(normalize(middle, feed_scale))
    gate_pre = low_back(product(normed_two, gate_mat))
    up_pre = low_back(product(normed_two, up_mat))
    hidden = low(jax.nn.gelu(gate_pre) * up_pre)
    return middle + low_back(product(hidden, down_mat))

def reference(inputs, mix_scale, branch_mat, input_mat, conv_taps, conv_shift, rate_mat, rate_shift, entry_mat, entry_shift, decay_logit, out_mat, feed_scale, gate_mat, up_mat, down_mat, lengths, cotangent):
    places = positions(lengths, inputs.shape[0])
    floats = tuple((member.astype(jnp.float32) for member in (inputs, mix_scale, branch_mat, input_mat, conv_taps, conv_shift, rate_mat, rate_shift, entry_mat, entry_shift, decay_logit, out_mat, feed_scale, gate_mat, up_mat, down_mat)))
    layer_out, pullback = jax.vjp(lambda *values: forward(*values, places), *floats)
    gradients = pullback(cotangent.astype(jnp.float32))
    return (layer_out.astype(jnp.bfloat16), gradients[0].astype(jnp.bfloat16), gradients[1], gradients[2], gradients[3], gradients[4], gradients[5], gradients[6], gradients[7], gradients[8], gradients[9], gradients[10], gradients[11], gradients[12], gradients[13], gradients[14], gradients[15])
```

```python
import jax
import jax.numpy as jnp
from jax import lax
from jax.experimental import pallas as pl
from jax.experimental.pallas import tpu as pltpu
from jax.sharding import PartitionSpec as P

CONV = 4
MEMBERS = 4
TOKS = 32
OWN = 128
HALO = 16

eps_norm = 1e-06
decay_power = 8.0
f32 = jnp.float32
bf16 = jnp.bfloat16


def hop_blk(values, distance):
    return lax.ppermute(
        values, "blk", [(i, (i + distance) % MEMBERS) for i in range(MEMBERS)]
    )


def hop_tok(values, axis, distance):
    route = []
    for y in range(4):
        for z in range(4):
            for c in range(2):
                if axis == "y":
                    to = ((y + distance) % 4, z, c)
                elif axis == "z":
                    to = (y, (z + distance) % 4, c)
                else:
                    to = (y, z, (c + distance) % 2)
                route.append((y * 8 + z * 2 + c, to[0] * 8 + to[1] * 2 + to[2]))
    return lax.ppermute(values, "tok", route)


def hop(values, axis, distance):
    if axis == "blk":
        return hop_blk(values, distance)
    return hop_tok(values, axis, distance)


def ring_gather(values, axis="blk"):
    half = values.shape[0] // 2
    before = hop(values, axis, 1)
    after = hop(values, axis, -1)
    far_head = hop(before[:half], axis, 1)
    far_tail = hop(after[half:], axis, -1)
    return [values, after, jnp.concatenate([far_head, far_tail]), before]


def narrow_sum(left, right):
    return (left.astype(f32) + right.astype(f32)).astype(bf16)


def ring_scatter(parts, axis="blk"):
    half = parts[2].shape[0] // 2
    head = hop(parts[2][:half].astype(bf16), axis, 1)
    tail = hop(parts[2][half:].astype(bf16), axis, -1)
    forth = jnp.concatenate([narrow_sum(parts[1][:half], head), parts[1][half:].astype(bf16)])
    back = jnp.concatenate([parts[3][:half].astype(bf16), narrow_sum(parts[3][half:], tail)])
    from_before = hop(forth, axis, 1)
    from_after = hop(back, axis, -1)
    return parts[0].astype(f32) + from_before.astype(f32) + from_after.astype(f32)


def turned(values, place):
    return [
        lax.dynamic_index_in_dim(values, (place + j) % 4, 0, keepdims=False) for j in range(4)
    ]


def weight_scatter(values, spot):
    y, z, c = spot
    columns = values.shape[1]
    half = columns // 2
    parts = values.reshape(4, 4, 2, 64, columns)
    mine = lax.dynamic_index_in_dim(parts, c, 2, keepdims=False)
    theirs = lax.dynamic_index_in_dim(parts, 1 - c, 2, keepdims=False)
    chip = narrow_sum(mine, hop(theirs, "core", 1))
    first = jnp.swapaxes(chip[..., :half], 0, 1).reshape(4, 256, half)
    second = chip[..., half:].reshape(4, 256, columns - half)
    first = ring_scatter(turned(first, z), "z").astype(bf16).reshape(4, 64, half)
    second = ring_scatter(turned(second, y), "y").astype(bf16).reshape(4, 64, columns - half)
    first = ring_scatter(turned(first, y), "y")
    second = ring_scatter(turned(second, z), "z")
    return jnp.concatenate([first, second], axis=1)


def small_gather(values):
    values = jnp.stack([values, hop(values, "core", 1)])
    for axis in ("z", "y"):
        values = jnp.stack([values] + [hop(values, axis, -d) for d in range(1, 4)])
    return values


def small_scatter(values, spot):
    y, z, c = spot
    parts = values.reshape((4, 4, 2) + values.shape[1:])
    mine = lax.dynamic_index_in_dim(parts, c, 2, keepdims=False)
    theirs = lax.dynamic_index_in_dim(parts, 1 - c, 2, keepdims=False)
    chip = mine + hop(theirs, "core", 1)
    for axis, place in (("y", y), ("z", z)):
        pieces = turned(chip, place)
        chip = pieces[0]
        for d in range(1, 4):
            chip = chip + hop(pieces[d], axis, d)
    return chip


def product(operand, weight, out=f32):
    return jnp.dot(operand, weight, preferred_element_type=f32).astype(out)


def product_back(operand, weight, out=f32):
    return lax.dot_general(
        operand, weight, (((1,), (1,)), ((), ())), preferred_element_type=f32
    ).astype(out)


def product_outer(operand, weight, out=bf16):
    return lax.dot_general(
        operand, weight, (((0,), (0,)), ((), ())), preferred_element_type=f32
    ).astype(out)


def norm_factor(values):
    return lax.rsqrt(jnp.mean(values * values, axis=1, keepdims=True) + eps_norm)


def normalize_back(gradient, values, factor, gains):
    weighted = gradient * gains
    return factor * weighted - values * (factor * factor * factor) * jnp.mean(
        weighted * values, axis=1, keepdims=True
    )


def sigmoid(values):
    return 1.0 / (1.0 + jnp.exp(-values))


def one_minus_exp(values):
    series = 1.0 + values * (1.0 / 8.0)
    for order in (7.0, 6.0, 5.0, 4.0, 3.0, 2.0):
        series = 1.0 + values * series * (1.0 / order)
    return jnp.where(values > -0.35, -values * series, 1.0 - jnp.exp(values))


def gelu_parts(values):
    root = 0.7978845608028654
    square = values * values
    bent = jnp.tanh(root * values * (1.0 + 0.044715 * square))
    half = 0.5 * (1.0 + bent)
    slope = half + 0.5 * values * (1.0 - bent * bent) * root * (1.0 + 3.0 * 0.044715 * square)
    return values * half, slope


def rows_at(start, size):
    return pl.ds(pl.multiple_of(start, size), size)


def conv_rows(ci_ref, slot, tile):
    base = slot * OWN + tile * HALO
    before = jnp.where(tile == 0, MEMBERS * OWN + slot * HALO, base - HALO)
    return jnp.concatenate(
        [ci_ref[rows_at(before, HALO), :].astype(f32), ci_ref[rows_at(base, HALO), :].astype(f32)],
        axis=0,
    )


def local_forward_kernel(
    ci_ref,
    place_ref,
    taps_ref,
    shift_ref,
    gates_ref,
    bias_ref,
    soft_ref,
    conv_ref,
    rate_ref,
    entry_ref,
    local_ref,
    cum_ref,
    edge_ref,
    pre_ref,
    high_ref,
    low_ref,
):
    channels = conv_ref.shape[1]

    for slot in range(MEMBERS):

        def convolve(tile, carry):
            base = slot * OWN + tile * HALO
            rows = conv_rows(ci_ref, slot, tile)
            places = place_ref[rows_at(base, HALO), :]
            total = shift_ref[...] + taps_ref[0:1, :] * rows[HALO:]
            for tap in range(1, CONV):
                lagged = pltpu.roll(rows, tap, 0)[HALO:]
                total = total + taps_ref[tap : tap + 1, :] * jnp.where(places >= tap, lagged, 0.0)
            conv_ref[rows_at(base, HALO), :] = total
            high = total.astype(bf16)
            high_ref[rows_at(base, HALO), :] = high
            low_ref[rows_at(base, HALO), :] = (total - high.astype(f32)).astype(bf16)
            return carry

        lax.fori_loop(0, OWN // HALO, convolve, 0)

    def gate(step, carry):
        columns = pl.ds(pl.multiple_of(step * 256, 256), 256)
        weight = gates_ref[:, columns]
        pre_ref[:, columns] = (
            jnp.dot(high_ref[...], weight, preferred_element_type=f32)
            + jnp.dot(low_ref[...], weight, preferred_element_type=f32)
            + bias_ref[:, columns]
        )
        return carry

    lax.fori_loop(0, 2 * channels // 256, gate, 0)

    row_ids = lax.broadcasted_iota(jnp.int32, (8, channels), 0)

    def scan(tile, carry):
        ends = []
        for slot in range(MEMBERS):
            base = slot * OWN + tile * 8
            rows = rows_at(base, 8)
            rates = sigmoid(pre_ref[rows, :channels])
            entries = sigmoid(pre_ref[rows, channels:])
            log_keep = -soft_ref[...] * rates
            resets = place_ref[rows, :] == 0
            keeps = jnp.where(resets, 0.0, jnp.exp(log_keep))
            scaling = jnp.where(resets, 1.0, jnp.sqrt(one_minus_exp(2.0 * log_keep)))
            value = entries * conv_ref[rows, :] * scaling
            coeff = keeps
            for distance in (1, 2, 4):
                reach = row_ids >= distance
                value = value + coeff * jnp.where(reach, pltpu.roll(value, distance, 0), 0.0)
                coeff = coeff * jnp.where(reach, pltpu.roll(coeff, distance, 0), 1.0)
            cum, state = carry[2 * slot], carry[2 * slot + 1]
            value = value + coeff * state
            coeff = coeff * cum
            rate_ref[rows, :] = rates
            entry_ref[rows, :] = entries
            local_ref[rows, :] = value
            cum_ref[rows, :] = coeff
            ends += [coeff[7:8], value[7:8]]
        return tuple(ends)

    start = (jnp.ones((1, channels), f32), jnp.zeros((1, channels), f32)) * MEMBERS
    ends = lax.fori_loop(0, OWN // 8, scan, start)
    edge_ref[...] = jnp.concatenate(ends[0::2] + ends[1::2], axis=0)


def place_of(spot_ref, tok):
    y, z, c = spot_ref[0], spot_ref[1], spot_ref[2]
    far_y = jnp.bitwise_and((tok >> 3) - y + 4, 3)
    far_z = jnp.bitwise_and(jnp.bitwise_and(tok >> 1, 3) - z + 4, 3)
    far_c = jnp.bitwise_xor(jnp.bitwise_and(tok, 1), c)
    return far_y * 8 + far_z * 2 + far_c


def mix_kernel(spot_ref, edges_ref, local_ref, cum_ref, branch_ref, state_ref, mixed_ref, carry_ref):
    channels = local_ref.shape[1]
    tok = spot_ref[3]

    def fold(at, pair):
        block = edges_ref[place_of(spot_ref, at)]
        return pair[0] * block[:4], block[:4] * pair[1] + block[4:]

    whole = (jnp.ones((4, channels), f32), jnp.zeros((4, channels), f32))
    prefix = lax.fori_loop(0, tok, fold, whole)
    total = lax.fori_loop(tok, TOKS, fold, prefix)
    current = jnp.zeros((1, channels), f32)
    carries = [None] * MEMBERS
    for _ in range(2):
        for slot in range(MEMBERS):
            one = slice(slot, slot + 1)
            carries[slot] = prefix[0][one] * current + prefix[1][one]
            current = total[0][one] * current + total[1][one]
    carry_ref[...] = jnp.concatenate(carries, axis=0)

    def apply(tile, token):
        for slot in range(MEMBERS):
            rows = rows_at(slot * OWN + tile * HALO, HALO)
            states = local_ref[rows, :] + cum_ref[rows, :] * carry_ref[slot : slot + 1, :]
            state_ref[rows, :] = states
            mixed_ref[rows, :] = (states * gelu_parts(branch_ref[rows, :])[0]).astype(bf16)
        return token

    lax.fori_loop(0, OWN // HALO, apply, 0)


def local_backward_kernel(
    grad_ref,
    branch_ref,
    state_ref,
    rate_ref,
    place_ref,
    soft_ref,
    bgrad_ref,
    sgrad_ref,
    local_ref,
    cum_ref,
    edge_ref,
):
    channels = grad_ref.shape[1]
    row_ids = lax.broadcasted_iota(jnp.int32, (8, channels), 0)

    def scan(step, carry):
        ends = []
        for slot in range(MEMBERS):
            pieces = {}
            base = slot * OWN + OWN - HALO - step * HALO
            cum, after = carry[2 * slot], carry[2 * slot + 1]
            slopes = []
            for part in (1, 0):
                rows = rows_at(base + 8 * part, 8)
                gated, slope = gelu_parts(branch_ref[rows, :])
                gradient = grad_ref[rows, :]
                slopes.append(slope * gradient * state_ref[rows, :])
                sgrad = gradient * gated
                keeps = jnp.where(
                    place_ref[rows, :] == 0, 0.0, jnp.exp(-soft_ref[...] * rate_ref[rows, :])
                )
                coeff = keeps
                value = keeps * sgrad
                for distance in (1, 2, 4):
                    reach = row_ids < 8 - distance
                    value = value + coeff * jnp.where(
                        reach, pltpu.roll(value, 8 - distance, 0), 0.0
                    )
                    coeff = coeff * jnp.where(reach, pltpu.roll(coeff, 8 - distance, 0), 1.0)
                value = value + coeff * after
                coeff = coeff * cum
                sgrad_ref[rows, :] = sgrad
                local_ref[rows, :] = value
                cum_ref[rows, :] = coeff
                cum, after = coeff[0:1], value[0:1]
            bgrad_ref[rows_at(base, HALO), :] = jnp.concatenate(
                [slopes[1], slopes[0]], axis=0
            ).astype(bf16)
            ends += [cum, after]
        return tuple(ends)

    start = (jnp.ones((1, channels), f32), jnp.zeros((1, channels), f32)) * MEMBERS
    ends = lax.fori_loop(0, OWN // HALO, scan, start)
    edge_ref[...] = jnp.concatenate(ends[0::2] + ends[1::2], axis=0)


def finish_backward_kernel(
    spot_ref,
    edges_ref,
    sgrad_ref,
    local_ref,
    cum_ref,
    state_ref,
    carry_ref,
    conv_ref,
    rate_ref,
    entry_ref,
    place_ref,
    soft_ref,
    ci_ref,
    taps_ref,
    gates_ref,
    pregrad_ref,
    igrad_ref,
    owed_ref,
    sums_ref,
    tapsum_ref,
    cgrad_ref,
    back_ref,
):
    channels = conv_ref.shape[1]
    tok = spot_ref[3]

    def fold(step, pair):
        block = edges_ref[place_of(spot_ref, TOKS - 1 - step)]
        return pair[0] * block[:4], block[:4] * pair[1] + block[4:]

    whole = (jnp.ones((4, channels), f32), jnp.zeros((4, channels), f32))
    prefix = lax.fori_loop(0, TOKS - 1 - tok, fold, whole)
    total = lax.fori_loop(TOKS - 1 - tok, TOKS, fold, prefix)
    current = jnp.zeros((1, channels), f32)
    carries = [None] * MEMBERS
    for _ in range(2):
        for slot in reversed(range(MEMBERS)):
            one = slice(slot, slot + 1)
            carries[slot] = prefix[0][one] * current + prefix[1][one]
            current = total[0][one] * current + total[1][one]
    back_ref[...] = jnp.concatenate(carries, axis=0)

    row_ids = lax.broadcasted_iota(jnp.int32, (8, channels), 0)
    zero = jnp.zeros((8, channels), f32)
    logit_sum, rate_sum, entry_sum = zero, zero, zero
    for slot in range(MEMBERS):

        def gate_grads(step, carry):
            later, logit_sum, rate_sum, entry_sum = carry
            base = slot * OWN + OWN - HALO - step * HALO
            low_rate, low_entry = [], []
            for part in (1, 0):
                first = base + 8 * part
                rows = rows_at(first, 8)
                held = local_ref[rows, :] + cum_ref[rows, :] * back_ref[slot : slot + 1, :]
                following = jnp.where(row_ids == 7, later, pltpu.roll(held, 7, 0))
                adjoint = sgrad_ref[rows, :] + following
                later = held[0:1]
                ahead = state_ref[rows_at(jnp.maximum(first - 8, 0), 8), :][7:8]
                at_start = first == slot * OWN
                ahead = jnp.where(at_start, carry_ref[slot : slot + 1, :], ahead)
                previous = jnp.where(row_ids == 0, ahead, pltpu.roll(state_ref[rows, :], 1, 0))
                rates, entries, conv = rate_ref[rows, :], entry_ref[rows, :], conv_ref[rows, :]
                resets = place_ref[rows, :] == 0
                log_keep = -soft_ref[...] * rates
                squared = jnp.exp(2.0 * log_keep)
                root = jnp.sqrt(one_minus_exp(2.0 * log_keep))
                scaling = jnp.where(resets, 1.0, root)
                turn = jnp.where(resets, 0.0, squared / root)
                weighed = adjoint * entries
                log_grad = held * previous - weighed * conv * turn
                rate_part = log_grad * rates
                logit_sum = logit_sum + rate_part
                rate_grad = -soft_ref[...] * rate_part * (1.0 - rates)
                direct = weighed * scaling
                entry_grad = direct * conv * (1.0 - entries)
                rate_sum = rate_sum + rate_grad
                entry_sum = entry_sum + entry_grad
                cgrad_ref[rows, :] = direct
                low_rate.append(rate_grad)
                low_entry.append(entry_grad)
            rows = rows_at(base, HALO)
            pregrad_ref[rows, :channels] = jnp.concatenate(low_rate[::-1], axis=0).astype(bf16)
            pregrad_ref[rows, channels:] = jnp.concatenate(low_entry[::-1], axis=0).astype(bf16)
            return later, logit_sum, rate_sum, entry_sum

        _, logit_sum, rate_sum, entry_sum = lax.fori_loop(
            0,
            OWN // HALO,
            gate_grads,
            (back_ref[slot : slot + 1, :], logit_sum, rate_sum, entry_sum),
        )

    def gate_back(step, carry):
        columns = pl.ds(pl.multiple_of(step * 128, 128), 128)
        cgrad_ref[:, columns] += jnp.dot(
            pregrad_ref[...], gates_ref[:, columns], preferred_element_type=f32
        )
        return carry

    lax.fori_loop(0, channels // 128, gate_back, 0)

    shift_sum = jnp.zeros((HALO, channels), f32)
    tap_sums = [shift_sum] * CONV
    for slot in range(MEMBERS):

        def spread(rows, places):
            return [rows] + [jnp.where(places >= tap, rows, 0.0) for tap in range(1, CONV)]

        def shifted_sum(current, following):
            total = taps_ref[0:1, :] * current[0]
            for tap in range(1, CONV):
                both = jnp.concatenate([current[tap], following[tap]], axis=0)
                total = total + taps_ref[tap : tap + 1, :] * pltpu.roll(both, 2 * HALO - tap, 0)[:HALO]
            return total

        def conv_back(tile, carry):
            shift_sum, tap_sums = carry
            base = slot * OWN + tile * HALO
            rows = rows_at(base, HALO)
            after = jnp.minimum(base + HALO, slot * OWN + OWN - HALO)
            next_rows = rows_at(after, HALO)
            last = jnp.where(tile == OWN // HALO - 1, 0.0, 1.0)
            grads = spread(cgrad_ref[rows, :], place_ref[rows, :])
            coming = spread(cgrad_ref[next_rows, :] * last, place_ref[next_rows, :])
            igrad_ref[rows, :] = shifted_sum(grads, coming)
            inputs = conv_rows(ci_ref, slot, tile)
            shift_sum = shift_sum + grads[0]
            sums = [tap_sums[0] + grads[0] * inputs[HALO:]]
            for tap in range(1, CONV):
                sums.append(tap_sums[tap] + grads[tap] * pltpu.roll(inputs, tap, 0)[HALO:])
            return shift_sum, sums

        shift_sum, tap_sums = lax.fori_loop(0, OWN // HALO, conv_back, (shift_sum, tap_sums))
        rows = rows_at(slot * OWN, HALO)
        first = spread(cgrad_ref[rows, :], place_ref[rows, :])
        owed_ref[slot * HALO : (slot + 1) * HALO, :] = shifted_sum(
            [jnp.zeros((HALO, channels), f32)] * CONV, first
        )

    def total_rows(values):
        return jnp.sum(values, axis=0, keepdims=True)

    sums_ref[...] = jnp.concatenate(
        [total_rows(v) for v in (shift_sum, rate_sum, entry_sum, logit_sum)], axis=0
    )
    tapsum_ref[...] = jnp.concatenate([total_rows(v) for v in tap_sums], axis=0)


def in_vmem(kernel, outs, scratch=(), scalars=0, count=1, flops=0, moved=0):
    vmem = pl.BlockSpec(memory_space=pltpu.VMEM)
    smem = pl.BlockSpec(memory_space=pltpu.SMEM)
    return pl.pallas_call(
        kernel,
        out_shape=[jax.ShapeDtypeStruct(shape, dtype) for shape, dtype in outs],
        in_specs=[smem] * scalars + [vmem] * count,
        out_specs=[vmem] * len(outs),
        scratch_shapes=[pltpu.VMEM(shape, dtype) for shape, dtype in scratch],
        compiler_params=pltpu.CompilerParams(vmem_limit_bytes=40 * 1024 * 1024),
        cost_estimate=pl.CostEstimate(flops=flops, bytes_accessed=moved, transcendentals=0),
    )


def per_device(
    inputs,
    mix_scale,
    branch_mat,
    input_mat,
    conv_taps,
    conv_shift,
    rate_mat,
    rate_shift,
    entry_mat,
    entry_shift,
    decay_logit,
    out_mat,
    feed_scale,
    gate_mat,
    up_mat,
    down_mat,
    lengths,
    cotangent,
):
    blk = lax.axis_index("blk")
    tok = lax.axis_index("tok")
    spot = (tok // 8, (tok // 2) % 4, tok % 2)
    spots = jnp.stack(list(spot) + [tok]).astype(jnp.int32)
    width = inputs.shape[1]
    channels = branch_mat.shape[1]
    hidden_units = gate_mat.shape[1]
    groups, _, block = rate_mat.shape
    slice_rows = branch_mat.shape[0]
    total_rows = MEMBERS * OWN

    smalls = [rate_mat, entry_mat, mix_scale, feed_scale, conv_taps, conv_shift]
    smalls += [rate_shift, entry_shift, decay_logit]
    flat = jnp.concatenate([member.reshape(-1) for member in smalls])
    flat = jnp.pad(flat, (0, slice_rows * 128 - flat.shape[0])).reshape(slice_rows, 128)
    mixer_all = lax.all_gather(
        jnp.concatenate([input_mat, branch_mat, out_mat.T, flat], axis=1), "tok", axis=0, tiled=True
    )
    feed_all = lax.all_gather(
        jnp.concatenate([gate_mat, up_mat, down_mat.T], axis=1), "tok", axis=0, tiled=True
    )
    input_all = mixer_all[:, :channels]
    branch_all = mixer_all[:, channels : 2 * channels]
    project_all = mixer_all[:, : 2 * channels]
    out_turned = mixer_all[:, 2 * channels : 3 * channels]
    gate_up_all = feed_all[:, : 2 * hidden_units]
    down_turned = feed_all[:, 2 * hidden_units :]
    small_all = mixer_all[:, 3 * channels :].reshape(TOKS, -1)
    cuts, at = [], 0
    for member in smalls:
        cuts.append(small_all[:, at : at + member.size].reshape((TOKS,) + member.shape))
        at += member.size
    rate_all = jnp.moveaxis(cuts[0], 0, 1).reshape(groups, block, block)
    entry_all = jnp.moveaxis(cuts[1], 0, 1).reshape(groups, block, block)
    mix_gain = cuts[2].reshape(1, -1).astype(f32)
    feed_gain = cuts[3].reshape(1, -1).astype(f32)
    taps = jnp.moveaxis(cuts[4], 0, 1).reshape(CONV, channels).astype(f32)
    shift, rate_bias, entry_bias, logits = [
        member.reshape(1, channels).astype(f32) for member in cuts[5:]
    ]
    bias = jnp.concatenate([rate_bias, entry_bias], axis=1)
    soft = decay_power * jax.nn.softplus(-logits)
    same = jnp.eye(groups, dtype=bf16)[:, None, :, None]

    def dense(mats):
        return (mats[:, :, None, :] * same).reshape(channels, channels)

    gates = jnp.concatenate([dense(rate_all), dense(entry_all)], axis=1)

    slots = (blk + jnp.arange(MEMBERS, dtype=jnp.int32)) % MEMBERS
    token_ids = (
        (slots * TOKS + tok)[:, None] * OWN + jnp.arange(OWN, dtype=jnp.int32)[None, :]
    ).reshape(-1)
    starts = jnp.cumsum(lengths) - lengths
    opened = jnp.max(jnp.where(starts[None, :] <= token_ids[:, None], starts[None, :], 0), axis=1)
    places = (token_ids - opened).reshape(total_rows, 1).astype(jnp.int32)

    devices = MEMBERS * TOKS
    tail = lax.ppermute(
        inputs[OWN - HALO :], ("blk", "tok"), [(i, (i + 1) % devices) for i in range(devices)]
    )
    rows_all = jnp.concatenate(ring_gather(inputs) + ring_gather(tail), axis=0)
    cotangent_all = jnp.concatenate(ring_gather(cotangent), axis=0)

    wide_values = rows_all.astype(f32)
    wide_one = (wide_values * norm_factor(wide_values) * mix_gain).astype(bf16)
    own_one = wide_one[:total_rows]
    conv_input = product(wide_one, input_all, bf16)
    branch = product(own_one, branch_all)
    state_shape = ((total_rows, channels), f32)
    conv, rates, entries, local, cum, edges = in_vmem(
        local_forward_kernel,
        [state_shape] * 5 + [((8, channels), f32)],
        [
            ((total_rows, 2 * channels), f32),
            ((total_rows, channels), bf16),
            ((total_rows, channels), bf16),
        ],
        count=7,
    )(conv_input, places, taps, shift, gates, bias, soft)
    all_edges = small_gather(edges).reshape(TOKS, 8, channels)
    states, mixture, carried = in_vmem(
        mix_kernel,
        [state_shape, ((total_rows, channels), bf16), ((MEMBERS, channels), f32)],
        scalars=1,
        count=4,
    )(spots, all_edges, local, cum, branch)

    def rows_of(values):
        return [values[j * OWN : (j + 1) * OWN] for j in range(MEMBERS)]

    own_values = inputs.astype(f32)
    middle = own_values + ring_scatter(rows_of(product_back(mixture, out_turned)))

    factor_two = norm_factor(middle)
    normed_two = (middle * factor_two * feed_gain).astype(bf16)
    wide_two = jnp.concatenate(ring_gather(normed_two), axis=0)
    gate_up = product(wide_two, gate_up_all)
    gate_pre, up_pre = gate_up[:, :hidden_units], gate_up[:, hidden_units:]
    hidden_grad = product(cotangent_all, down_turned)
    gate_act, gate_slope = gelu_parts(gate_pre)
    hidden = (gate_act * up_pre).astype(bf16)
    gate_grad = (gate_slope * hidden_grad * up_pre).astype(bf16)
    up_grad = (gate_act * hidden_grad).astype(bf16)
    both_grads = jnp.concatenate([gate_grad, up_grad], axis=1)
    two_shares = product_back(both_grads, gate_up_all)
    two_grad = ring_scatter(rows_of(two_shares))
    middle_grad = cotangent.astype(f32) + normalize_back(two_grad, middle, factor_two, feed_gain)
    layer_out = middle + ring_scatter(rows_of(product_back(hidden, down_turned)))
    grad_feed_scale = jnp.sum(two_grad * middle * factor_two, axis=0)
    grad_gate_up = lax.psum_scatter(
        product_outer(wide_two, both_grads), "tok", scatter_dimension=0, tiled=True
    )
    grad_down = lax.psum_scatter(
        product_outer(cotangent_all, hidden), "tok", scatter_dimension=0, tiled=True
    )

    middle_wide = jnp.concatenate(ring_gather(middle_grad.astype(bf16)), axis=0)
    mixture_grad = product(middle_wide, out_turned)
    branch_grad, sgrad, local_back, cum_back, back_edges = in_vmem(
        local_backward_kernel,
        [((total_rows, channels), bf16)] + [state_shape] * 3 + [((8, channels), f32)],
        count=6,
    )(mixture_grad, branch, states, rates, places, soft)
    all_back = small_gather(back_edges).reshape(TOKS, 8, channels)
    pregrads, igrad, owed, sums, tap_sums = in_vmem(
        finish_backward_kernel,
        [
            ((total_rows, 2 * channels), bf16),
            state_shape,
            ((MEMBERS * HALO, channels), f32),
            ((4, channels), f32),
            ((CONV, channels), f32),
        ],
        [((total_rows, channels), f32), ((MEMBERS, channels), f32)],
        scalars=1,
        count=14,
    )(
        spots,
        all_back,
        sgrad,
        local_back,
        cum_back,
        states,
        carried,
        conv,
        rates,
        entries,
        places,
        soft,
        conv_input,
        taps,
        gates.T,
    )
    returned = lax.ppermute(
        owed.reshape(MEMBERS, HALO, channels)[:, HALO - 3 :],
        "tok",
        [(i, (i - 1) % TOKS) for i in range(TOKS)],
    )
    turned_on = jnp.concatenate([returned[1:], returned[:1]], axis=0)
    landing = jnp.where(tok == TOKS - 1, turned_on, returned)
    input_grad = igrad.reshape(MEMBERS, OWN, channels) + jnp.pad(
        landing, ((0, 0), (OWN - 3, 0), (0, 0))
    )
    input_low = input_grad.reshape(total_rows, channels).astype(bf16)
    one_shares = product_back(input_low, input_all) + product_back(branch_grad, branch_all)
    one_grad = ring_scatter(rows_of(one_shares))
    factor_one = norm_factor(own_values)
    first_grad = normalize_back(one_grad, own_values, factor_one, mix_gain)
    inputs_grad = (middle_grad + first_grad).astype(bf16)
    grad_mix_scale = jnp.sum(one_grad * own_values * factor_one, axis=0)

    grad_early = weight_scatter(
        jnp.concatenate(
            [product_outer(own_one, branch_grad), product_outer(middle_wide, mixture)], axis=1
        ),
        spot,
    )
    grad_branch, grad_out = grad_early[:, :channels], grad_early[:, channels:]
    grad_input = weight_scatter(product_outer(own_one, input_low), spot)
    dense_grads = product_outer(conv.astype(bf16), pregrads, f32)
    columns = jnp.arange(2 * channels, dtype=jnp.int32) % channels // block
    gate_grads = sum(
        jnp.where(columns == h, dense_grads[h * block : (h + 1) * block], 0.0)
        for h in range(groups)
    )
    small_grads = [
        gate_grads.reshape(TOKS, -1),
        jnp.moveaxis(tap_sums.reshape(CONV, TOKS, -1), 1, 0).reshape(TOKS, -1),
        jnp.moveaxis(sums.reshape(4, TOKS, -1), 1, 0).reshape(TOKS, -1),
        grad_mix_scale.reshape(TOKS, -1),
        grad_feed_scale.reshape(TOKS, -1),
    ]
    settled = small_scatter(jnp.concatenate(small_grads, axis=1), spot)
    cuts, at = [], 0
    for member in small_grads:
        cuts.append(settled[at : at + member.shape[1]])
        at += member.shape[1]
    gate_own = jnp.transpose(cuts[0].reshape(block // TOKS, 2, groups, block), (1, 2, 0, 3))
    sums_own = cuts[2].reshape(4, -1)
    gains_own = jnp.concatenate(cuts[3:])
    gains_own = gains_own + hop_blk(gains_own, 1) + hop_blk(gains_own, -1) + hop_blk(gains_own, 2)
    own_logits = decay_logit.astype(f32)
    return (
        layer_out.astype(bf16),
        inputs_grad,
        gains_own[: width // TOKS],
        grad_branch,
        grad_input,
        cuts[1].reshape(CONV, -1),
        sums_own[0],
        gate_own[0],
        sums_own[1],
        gate_own[1],
        sums_own[2],
        sums_own[3] * decay_power * jax.nn.sigmoid(-own_logits),
        grad_out.T,
        gains_own[width // TOKS :],
        grad_gate_up[:, :hidden_units].astype(f32),
        grad_gate_up[:, hidden_units:].astype(f32),
        grad_down.T.astype(f32),
    )


def solution(mesh):
    in_specs = (
        P(("blk", "tok"), None),
        P("tok"),
        P("tok", "blk"),
        P("tok", "blk"),
        P(None, ("blk", "tok")),
        P(("blk", "tok")),
        P("blk", "tok", None),
        P(("blk", "tok")),
        P("blk", "tok", None),
        P(("blk", "tok")),
        P(("blk", "tok")),
        P("blk", "tok"),
        P("tok"),
        P("tok", "blk"),
        P("tok", "blk"),
        P("blk", "tok"),
        P(),
        P(("blk", "tok"), None),
    )
    out_specs = (
        P(("blk", "tok"), None),
        P(("blk", "tok"), None),
        P("tok"),
        P("tok", "blk"),
        P("tok", "blk"),
        P(None, ("blk", "tok")),
        P(("blk", "tok")),
        P("blk", "tok", None),
        P(("blk", "tok")),
        P("blk", "tok", None),
        P(("blk", "tok")),
        P(("blk", "tok")),
        P("blk", "tok"),
        P("tok"),
        P("tok", "blk"),
        P("tok", "blk"),
        P("blk", "tok"),
    )
    return jax.shard_map(
        per_device, mesh=mesh, in_specs=in_specs, out_specs=out_specs, check_vma=False
    )
```

```python
import functools

import jax
import jax.numpy as jnp
from jax import lax
from jax.experimental import pallas as pl
from jax.experimental.pallas import tpu as pltpu
from jax.sharding import PartitionSpec as P

CONV = 4
MEMBERS = 4
TOKS = 32
OWN = 128
HALO = 16

eps_norm = 1e-06
decay_power = 8.0
f32 = jnp.float32
bf16 = jnp.bfloat16


def hop_blk(values, distance):
    return lax.ppermute(
        values, "blk", [(i, (i + distance) % MEMBERS) for i in range(MEMBERS)]
    )


def hop_tok(values, axis, distance):
    route = []
    for y in range(4):
        for z in range(4):
            for c in range(2):
                if axis == "y":
                    to = ((y + distance) % 4, z, c)
                elif axis == "z":
                    to = (y, (z + distance) % 4, c)
                else:
                    to = (y, z, (c + distance) % 2)
                route.append((y * 8 + z * 2 + c, to[0] * 8 + to[1] * 2 + to[2]))
    return lax.ppermute(values, "tok", route)


def hop(values, axis, distance):
    if axis == "blk":
        return hop_blk(values, distance)
    return hop_tok(values, axis, distance)


def ring_gather(values, axis="blk"):
    half = values.shape[0] // 2
    before = hop(values, axis, 1)
    after = hop(values, axis, -1)
    far_head = hop(before[:half], axis, 1)
    far_tail = hop(after[half:], axis, -1)
    return [values, after, jnp.concatenate([far_head, far_tail]), before]


def narrow_sum(left, right):
    return (left.astype(f32) + right.astype(f32)).astype(bf16)


def ring_scatter(parts, axis="blk"):
    half = parts[2].shape[0] // 2
    head = hop(parts[2][:half].astype(bf16), axis, 1)
    tail = hop(parts[2][half:].astype(bf16), axis, -1)
    forth = jnp.concatenate([narrow_sum(parts[1][:half], head), parts[1][half:].astype(bf16)])
    back = jnp.concatenate([parts[3][:half].astype(bf16), narrow_sum(parts[3][half:], tail)])
    from_before = hop(forth, axis, 1)
    from_after = hop(back, axis, -1)
    return parts[0].astype(f32) + from_before.astype(f32) + from_after.astype(f32)


def pair_gather(first, second):
    before_one, after_one = hop_blk(first, 1), hop_blk(first, -1)
    before_two, after_two = hop_blk(second, 1), hop_blk(second, -1)
    far_one, far_two = hop_blk(before_one, 1), hop_blk(after_two, -1)
    return [first, after_one, far_one, before_one], [second, after_two, far_two, before_two]


def after(value, *others):
    return lax.optimization_barrier((value,) + others)[0]


def hop_sum(values, axis):
    return values + hop(values, axis, 1) + hop(values, axis, -1) + hop(values, axis, 2)


def direct_gather(values, axis="blk"):
    return [values] + [hop(values, axis, -d) for d in range(1, 4)]


def turned(values, place):
    return [
        lax.dynamic_index_in_dim(values, (place + j) % 4, 0, keepdims=False) for j in range(4)
    ]


def swap_sum(parts, core):
    mine = lax.dynamic_index_in_dim(parts, core, 1, keepdims=False)
    theirs = lax.dynamic_index_in_dim(parts, 1 - core, 1, keepdims=False)
    return narrow_sum(mine, hop(theirs, "core", 1))


def chip_sum(values, core):
    return swap_sum(values.reshape(16, 2, -1, values.shape[1]), core)


def chips_sum(values):
    cores = [[2 * i + c for i in range(16)] for c in range(2)]
    terms = lax.all_to_all(values, "tok", 0, 0, axis_index_groups=cores, tiled=True)
    return jnp.sum(terms.astype(f32), axis=0)


def small_gather(values):
    values = jnp.stack([values, hop(values, "core", 1)])
    for axis in ("z", "y"):
        values = jnp.stack(direct_gather(values, axis))
    return values


def product(operand, weight, out=f32):
    return jnp.dot(operand, weight, preferred_element_type=f32).astype(out)


def product_back(operand, weight, out=f32):
    return lax.dot_general(
        operand, weight, (((1,), (1,)), ((), ())), preferred_element_type=f32
    ).astype(out)


def product_outer(operand, weight, out=bf16):
    return lax.dot_general(
        operand, weight, (((0,), (0,)), ((), ())), preferred_element_type=f32
    ).astype(out)


def norm_factor(values):
    return lax.rsqrt(jnp.mean(values * values, axis=1, keepdims=True) + eps_norm)


def normalize_back(gradient, values, factor, gains):
    weighted = gradient * gains
    return factor * weighted - values * (factor * factor * factor) * jnp.mean(
        weighted * values, axis=1, keepdims=True
    )


def sigmoid(values):
    return 1.0 / (1.0 + jnp.exp(-values))


def one_minus_exp(values):
    series = 1.0 + values * (1.0 / 8.0)
    for order in (7.0, 6.0, 5.0, 4.0, 3.0, 2.0):
        series = 1.0 + values * series * (1.0 / order)
    return jnp.where(values > -0.35, -values * series, 1.0 - jnp.exp(values))


def gelu_parts(values):
    root = 0.7978845608028654
    square = values * values
    bent = jnp.tanh(root * values * (1.0 + 0.044715 * square))
    half = 0.5 * (1.0 + bent)
    slope = half + 0.5 * values * (1.0 - bent * bent) * root * (1.0 + 3.0 * 0.044715 * square)
    return values * half, slope


def rows_at(start, size):
    return pl.ds(pl.multiple_of(start, size), size)


def conv_rows(ci_ref, slot, tile):
    base = slot * OWN + tile * HALO
    before = jnp.where(tile == 0, MEMBERS * OWN + slot * HALO, base - HALO)
    return jnp.concatenate(
        [ci_ref[rows_at(before, HALO), :].astype(f32), ci_ref[rows_at(base, HALO), :].astype(f32)],
        axis=0,
    )


def local_forward_kernel(
    ci_ref,
    place_ref,
    taps_ref,
    shift_ref,
    gates_ref,
    bias_ref,
    soft_ref,
    conv_ref,
    rate_ref,
    entry_ref,
    local_ref,
    cum_ref,
    edge_ref,
    pre_ref,
    high_ref,
    low_ref,
):
    channels = conv_ref.shape[1]

    for slot in range(MEMBERS):

        def convolve(tile, carry):
            base = slot * OWN + tile * HALO
            rows = conv_rows(ci_ref, slot, tile)
            places = place_ref[rows_at(base, HALO), :]
            total = shift_ref[...] + taps_ref[0:1, :] * rows[HALO:]
            for tap in range(1, CONV):
                lagged = pltpu.roll(rows, tap, 0)[HALO:]
                total = total + taps_ref[tap : tap + 1, :] * jnp.where(places >= tap, lagged, 0.0)
            conv_ref[rows_at(base, HALO), :] = total
            high = total.astype(bf16)
            high_ref[rows_at(base, HALO), :] = high
            low_ref[rows_at(base, HALO), :] = (total - high.astype(f32)).astype(bf16)
            return carry

        lax.fori_loop(0, OWN // HALO, convolve, 0)

    def gate(step, carry):
        columns = pl.ds(pl.multiple_of(step * 256, 256), 256)
        weight = gates_ref[:, columns]
        pre_ref[:, columns] = (
            jnp.dot(high_ref[...], weight, preferred_element_type=f32)
            + jnp.dot(low_ref[...], weight, preferred_element_type=f32)
            + bias_ref[:, columns]
        )
        return carry

    lax.fori_loop(0, 2 * channels // 256, gate, 0)

    row_ids = lax.broadcasted_iota(jnp.int32, (8, channels), 0)

    def scan(tile, carry):
        ends = []
        for slot in range(MEMBERS):
            base = slot * OWN + tile * 8
            rows = rows_at(base, 8)
            rates = sigmoid(pre_ref[rows, :channels])
            entries = sigmoid(pre_ref[rows, channels:])
            log_keep = -soft_ref[...] * rates
            resets = place_ref[rows, :] == 0
            keeps = jnp.where(resets, 0.0, jnp.exp(log_keep))
            scaling = jnp.where(resets, 1.0, jnp.sqrt(one_minus_exp(2.0 * log_keep)))
            value = entries * conv_ref[rows, :] * scaling
            coeff = keeps
            for distance in (1, 2, 4):
                reach = row_ids >= distance
                value = value + coeff * jnp.where(reach, pltpu.roll(value, distance, 0), 0.0)
                coeff = coeff * jnp.where(reach, pltpu.roll(coeff, distance, 0), 1.0)
            cum, state = carry[2 * slot], carry[2 * slot + 1]
            value = value + coeff * state
            coeff = coeff * cum
            rate_ref[rows, :] = rates
            entry_ref[rows, :] = entries
            local_ref[rows, :] = value
            cum_ref[rows, :] = coeff
            ends += [coeff[7:8], value[7:8]]
        return tuple(ends)

    start = (jnp.ones((1, channels), f32), jnp.zeros((1, channels), f32)) * MEMBERS
    ends = lax.fori_loop(0, OWN // 8, scan, start)
    edge_ref[...] = jnp.concatenate(ends[0::2] + ends[1::2], axis=0)


def extended(pair, block):
    return pair[0] * block[:4], block[:4] * pair[1] + block[4:]


def whole_chain(channels):
    return jnp.ones((4, channels), f32), jnp.zeros((4, channels), f32)


def fold_near_kernel(backward, spot_ref, *refs):
    pieces, (total_ref, prefix_ref, held_ref) = refs[:4], refs[4:]
    z, c = spot_ref[2], spot_ref[3]
    for distance, piece in enumerate(pieces):
        held_ref[distance] = piece[...]
    chain = whole_chain(total_ref.shape[1])
    prefix = chain
    for place in reversed(range(8)) if backward else range(8):
        here = place == 2 * z + c
        prefix = tuple(jnp.where(here, new, old) for new, old in zip(chain, prefix))
        distance = jnp.bitwise_and(place // 2 - z + 4, 3)
        chain = extended(chain, held_ref[distance, jnp.bitwise_xor(place % 2, c)])
    total_ref[...] = jnp.concatenate(chain, axis=0)
    prefix_ref[...] = jnp.concatenate(prefix, axis=0)


def slot_carries(backward, spot_ref, pieces, prefix_ref, held_ref):
    y = spot_ref[1]
    channels = prefix_ref.shape[1]
    for distance, piece in enumerate(pieces):
        held_ref[distance] = piece[...]
    total = whole_chain(channels)
    prefix = total
    for place in reversed(range(4)) if backward else range(4):
        here = place == y
        prefix = tuple(jnp.where(here, new, old) for new, old in zip(total, prefix))
        total = extended(total, held_ref[jnp.bitwise_and(place - y + 4, 3)])
    prefix = extended(prefix, prefix_ref[...])
    current = jnp.zeros((1, channels), f32)
    carries = [None] * MEMBERS
    for _ in range(2):
        for slot in reversed(range(MEMBERS)) if backward else range(MEMBERS):
            one = slice(slot, slot + 1)
            carries[slot] = prefix[0][one] * current + prefix[1][one]
            current = total[0][one] * current + total[1][one]
    return carries


def mix_kernel(
    spot_ref,
    piece0,
    piece1,
    piece2,
    piece3,
    prefix_ref,
    local_ref,
    cum_ref,
    branch_ref,
    state_ref,
    mixed_ref,
    carry_ref,
    held_ref,
):
    pieces = (piece0, piece1, piece2, piece3)
    carries = slot_carries(False, spot_ref, pieces, prefix_ref, held_ref)
    carry_ref[...] = jnp.concatenate(carries, axis=0)

    def apply(tile, token):
        for slot in range(MEMBERS):
            rows = rows_at(slot * OWN + tile * HALO, HALO)
            states = local_ref[rows, :] + cum_ref[rows, :] * carry_ref[slot : slot + 1, :]
            state_ref[rows, :] = states
            mixed_ref[rows, :] = (states * gelu_parts(branch_ref[rows, :])[0]).astype(bf16)
        return token

    lax.fori_loop(0, OWN // HALO, apply, 0)


def local_backward_kernel(
    grad_ref,
    branch_ref,
    state_ref,
    rate_ref,
    place_ref,
    soft_ref,
    bgrad_ref,
    sgrad_ref,
    local_ref,
    cum_ref,
    edge_ref,
):
    channels = grad_ref.shape[1]
    row_ids = lax.broadcasted_iota(jnp.int32, (8, channels), 0)

    def scan(step, carry):
        ends = []
        for slot in range(MEMBERS):
            pieces = {}
            base = slot * OWN + OWN - HALO - step * HALO
            cum, after = carry[2 * slot], carry[2 * slot + 1]
            slopes = []
            for part in (1, 0):
                rows = rows_at(base + 8 * part, 8)
                gated, slope = gelu_parts(branch_ref[rows, :])
                gradient = grad_ref[rows, :]
                slopes.append(slope * gradient * state_ref[rows, :])
                sgrad = gradient * gated
                keeps = jnp.where(
                    place_ref[rows, :] == 0, 0.0, jnp.exp(-soft_ref[...] * rate_ref[rows, :])
                )
                coeff = keeps
                value = keeps * sgrad
                for distance in (1, 2, 4):
                    reach = row_ids < 8 - distance
                    value = value + coeff * jnp.where(
                        reach, pltpu.roll(value, 8 - distance, 0), 0.0
                    )
                    coeff = coeff * jnp.where(reach, pltpu.roll(coeff, 8 - distance, 0), 1.0)
                value = value + coeff * after
                coeff = coeff * cum
                sgrad_ref[rows, :] = sgrad
                local_ref[rows, :] = value
                cum_ref[rows, :] = coeff
                cum, after = coeff[0:1], value[0:1]
            bgrad_ref[rows_at(base, HALO), :] = jnp.concatenate(
                [slopes[1], slopes[0]], axis=0
            ).astype(bf16)
            ends += [cum, after]
        return tuple(ends)

    start = (jnp.ones((1, channels), f32), jnp.zeros((1, channels), f32)) * MEMBERS
    ends = lax.fori_loop(0, OWN // HALO, scan, start)
    edge_ref[...] = jnp.concatenate(ends[0::2] + ends[1::2], axis=0)


def finish_backward_kernel(
    spot_ref,
    piece0,
    piece1,
    piece2,
    piece3,
    prefix_ref,
    sgrad_ref,
    local_ref,
    cum_ref,
    state_ref,
    carry_ref,
    conv_ref,
    rate_ref,
    entry_ref,
    place_ref,
    soft_ref,
    ci_ref,
    taps_ref,
    gates_ref,
    pregrad_ref,
    igrad_ref,
    owed_ref,
    sums_ref,
    tapsum_ref,
    cgrad_ref,
    back_ref,
    held_ref,
):
    channels = conv_ref.shape[1]
    pieces = (piece0, piece1, piece2, piece3)
    carries = slot_carries(True, spot_ref, pieces, prefix_ref, held_ref)
    back_ref[...] = jnp.concatenate(carries, axis=0)

    row_ids = lax.broadcasted_iota(jnp.int32, (8, channels), 0)
    zero = jnp.zeros((8, channels), f32)
    logit_sum, rate_sum, entry_sum = zero, zero, zero
    for slot in range(MEMBERS):

        def gate_grads(step, carry):
            later, logit_sum, rate_sum, entry_sum = carry
            base = slot * OWN + OWN - HALO - step * HALO
            low_rate, low_entry = [], []
            for part in (1, 0):
                first = base + 8 * part
                rows = rows_at(first, 8)
                held = local_ref[rows, :] + cum_ref[rows, :] * back_ref[slot : slot + 1, :]
                following = jnp.where(row_ids == 7, later, pltpu.roll(held, 7, 0))
                adjoint = sgrad_ref[rows, :] + following
                later = held[0:1]
                ahead = state_ref[rows_at(jnp.maximum(first - 8, 0), 8), :][7:8]
                at_start = first == slot * OWN
                ahead = jnp.where(at_start, carry_ref[slot : slot + 1, :], ahead)
                previous = jnp.where(row_ids == 0, ahead, pltpu.roll(state_ref[rows, :], 1, 0))
                rates, entries, conv = rate_ref[rows, :], entry_ref[rows, :], conv_ref[rows, :]
                resets = place_ref[rows, :] == 0
                log_keep = -soft_ref[...] * rates
                squared = jnp.exp(2.0 * log_keep)
                root = jnp.sqrt(one_minus_exp(2.0 * log_keep))
                scaling = jnp.where(resets, 1.0, root)
                turn = jnp.where(resets, 0.0, squared / root)
                weighed = adjoint * entries
                log_grad = held * previous - weighed * conv * turn
                rate_part = log_grad * rates
                logit_sum = logit_sum + rate_part
                rate_grad = -soft_ref[...] * rate_part * (1.0 - rates)
                direct = weighed * scaling
                entry_grad = direct * conv * (1.0 - entries)
                rate_sum = rate_sum + rate_grad
                entry_sum = entry_sum + entry_grad
                cgrad_ref[rows, :] = direct
                low_rate.append(rate_grad)
                low_entry.append(entry_grad)
            rows = rows_at(base, HALO)
            pregrad_ref[rows, :channels] = jnp.concatenate(low_rate[::-1], axis=0).astype(bf16)
            pregrad_ref[rows, channels:] = jnp.concatenate(low_entry[::-1], axis=0).astype(bf16)
            return later, logit_sum, rate_sum, entry_sum

        _, logit_sum, rate_sum, entry_sum = lax.fori_loop(
            0,
            OWN // HALO,
            gate_grads,
            (back_ref[slot : slot + 1, :], logit_sum, rate_sum, entry_sum),
        )

    def gate_back(step, carry):
        columns = pl.ds(pl.multiple_of(step * 128, 128), 128)
        cgrad_ref[:, columns] += jnp.dot(
            pregrad_ref[...], gates_ref[:, columns], preferred_element_type=f32
        )
        return carry

    lax.fori_loop(0, channels // 128, gate_back, 0)

    shift_sum = jnp.zeros((HALO, channels), f32)
    tap_sums = [shift_sum] * CONV
    for slot in range(MEMBERS):

        def spread(rows, places):
            return [rows] + [jnp.where(places >= tap, rows, 0.0) for tap in range(1, CONV)]

        def shifted_sum(current, following):
            total = taps_ref[0:1, :] * current[0]
            for tap in range(1, CONV):
                both = jnp.concatenate([current[tap], following[tap]], axis=0)
                total = total + taps_ref[tap : tap + 1, :] * pltpu.roll(both, 2 * HALO - tap, 0)[:HALO]
            return total

        def conv_back(tile, carry):
            shift_sum, tap_sums = carry
            base = slot * OWN + tile * HALO
            rows = rows_at(base, HALO)
            after = jnp.minimum(base + HALO, slot * OWN + OWN - HALO)
            next_rows = rows_at(after, HALO)
            last = jnp.where(tile == OWN // HALO - 1, 0.0, 1.0)
            grads = spread(cgrad_ref[rows, :], place_ref[rows, :])
            coming = spread(cgrad_ref[next_rows, :] * last, place_ref[next_rows, :])
            igrad_ref[rows, :] = shifted_sum(grads, coming)
            inputs = conv_rows(ci_ref, slot, tile)
            shift_sum = shift_sum + grads[0]
            sums = [tap_sums[0] + grads[0] * inputs[HALO:]]
            for tap in range(1, CONV):
                sums.append(tap_sums[tap] + grads[tap] * pltpu.roll(inputs, tap, 0)[HALO:])
            return shift_sum, sums

        shift_sum, tap_sums = lax.fori_loop(0, OWN // HALO, conv_back, (shift_sum, tap_sums))
        rows = rows_at(slot * OWN, HALO)
        first = spread(cgrad_ref[rows, :], place_ref[rows, :])
        owed_ref[slot * HALO : (slot + 1) * HALO, :] = shifted_sum(
            [jnp.zeros((HALO, channels), f32)] * CONV, first
        )

    def total_rows(values):
        return jnp.sum(values, axis=0, keepdims=True)

    sums_ref[...] = jnp.concatenate(
        [total_rows(v) for v in (shift_sum, rate_sum, entry_sum, logit_sum)], axis=0
    )
    tapsum_ref[...] = jnp.concatenate([total_rows(v) for v in tap_sums], axis=0)


def in_vmem(kernel, outs, scratch=(), scalars=0, count=1, flops=0, moved=0):
    vmem = pl.BlockSpec(memory_space=pltpu.VMEM)
    smem = pl.BlockSpec(memory_space=pltpu.SMEM)
    return pl.pallas_call(
        kernel,
        out_shape=[jax.ShapeDtypeStruct(shape, dtype) for shape, dtype in outs],
        in_specs=[smem] * scalars + [vmem] * count,
        out_specs=[vmem] * len(outs),
        scratch_shapes=[pltpu.VMEM(shape, dtype) for shape, dtype in scratch],
        compiler_params=pltpu.CompilerParams(vmem_limit_bytes=40 * 1024 * 1024),
        cost_estimate=pl.CostEstimate(flops=flops, bytes_accessed=moved, transcendentals=0),
    )


def exchange_edges(edges, spots, backward):
    channels = edges.shape[1]
    near = jnp.stack([edges, hop(edges, "core", 1)])
    total, prefix = in_vmem(
        functools.partial(fold_near_kernel, backward),
        [((8, channels), f32)] * 2,
        [((4, 2, 8, channels), f32)],
        scalars=1,
        count=4,
    )(spots, *direct_gather(near, "z"))
    return direct_gather(total, "y") + [prefix]


def outer_kernel(lhs_one, lhs_two, rhs_one, rhs_two, rhs_three, out_ref):
    def settle(lhs, rhs):
        out_ref[...] = lax.dot_general(
            lhs[...], rhs[...], (((0,), (0,)), ((), ())), preferred_element_type=f32
        ).astype(bf16)

    for step, (lhs, rhs) in enumerate(
        ((lhs_one, rhs_one), (lhs_one, rhs_two), (lhs_two, rhs_three))
    ):
        pl.when(pl.program_id(0) == step)(functools.partial(settle, lhs, rhs))


def feed_outer(lhs_one, lhs_two, rhs):
    rows, features = lhs_one.shape
    columns = rhs[0].shape[1]
    height = 256
    whole = pl.BlockSpec((rows, columns), lambda j, i: (0, 0))
    return pl.pallas_call(
        outer_kernel,
        grid=(3, features // height),
        in_specs=[
            pl.BlockSpec((rows, height), lambda j, i: (0, jnp.where(j < 2, i, 0))),
            pl.BlockSpec((rows, height), lambda j, i: (0, jnp.where(j < 2, 0, i))),
            whole,
            whole,
            whole,
        ],
        out_specs=pl.BlockSpec((height, columns), lambda j, i: (i, j)),
        out_shape=jax.ShapeDtypeStruct((features, 3 * columns), bf16),
        compiler_params=pltpu.CompilerParams(vmem_limit_bytes=40 * 1024 * 1024),
        cost_estimate=pl.CostEstimate(
            flops=6 * rows * features * columns,
            bytes_accessed=6 * features * columns,
            transcendentals=0,
        ),
    )(lhs_one, lhs_two, *rhs)


def per_device(
    inputs,
    mix_scale,
    branch_mat,
    input_mat,
    conv_taps,
    conv_shift,
    rate_mat,
    rate_shift,
    entry_mat,
    entry_shift,
    decay_logit,
    out_mat,
    feed_scale,
    gate_mat,
    up_mat,
    down_mat,
    lengths,
    cotangent,
):
    blk = lax.axis_index("blk")
    tok = lax.axis_index("tok")
    spot = (tok // 8, (tok // 2) % 4, tok % 2)
    spots = jnp.stack([tok] + list(spot)).astype(jnp.int32)
    width = inputs.shape[1]
    channels = branch_mat.shape[1]
    hidden_units = gate_mat.shape[1]
    groups, _, block = rate_mat.shape
    slice_rows = branch_mat.shape[0]
    total_rows = MEMBERS * OWN

    smalls = [rate_mat, entry_mat, mix_scale, feed_scale, conv_taps, conv_shift]
    smalls += [rate_shift, entry_shift, decay_logit]
    flat = jnp.concatenate([member.reshape(-1) for member in smalls])
    flat = jnp.pad(flat, (0, slice_rows * 128 - flat.shape[0])).reshape(slice_rows, 128)
    near = small_gather(flat)
    for axis, place in ((2, spot[2]), (1, spot[1]), (0, spot[0])):
        near = jnp.roll(near, place, axis)
    small_all = near.reshape(TOKS, -1)
    mixer_all = lax.all_gather(
        jnp.concatenate([input_mat, branch_mat, out_mat.T], axis=1), "tok", axis=0, tiled=True
    )
    feed_all = lax.all_gather(
        jnp.concatenate([gate_mat, up_mat, down_mat.T], axis=1), "tok", axis=0, tiled=True
    )
    input_all = mixer_all[:, :channels]
    branch_all = mixer_all[:, channels : 2 * channels]
    project_all = mixer_all[:, : 2 * channels]
    out_turned = mixer_all[:, 2 * channels : 3 * channels]
    gate_up_all = feed_all[:, : 2 * hidden_units]
    down_turned = feed_all[:, 2 * hidden_units :]
    cuts, at = [], 0
    for member in smalls:
        cuts.append(small_all[:, at : at + member.size].reshape((TOKS,) + member.shape))
        at += member.size
    rate_all = jnp.moveaxis(cuts[0], 0, 1).reshape(groups, block, block)
    entry_all = jnp.moveaxis(cuts[1], 0, 1).reshape(groups, block, block)
    mix_gain = cuts[2].reshape(1, -1).astype(f32)
    feed_gain = cuts[3].reshape(1, -1).astype(f32)
    taps = jnp.moveaxis(cuts[4], 0, 1).reshape(CONV, channels).astype(f32)
    shift, rate_bias, entry_bias, logits = [
        member.reshape(1, channels).astype(f32) for member in cuts[5:]
    ]
    bias = jnp.concatenate([rate_bias, entry_bias], axis=1)
    soft = decay_power * jax.nn.softplus(-logits)
    same = jnp.eye(groups, dtype=bf16)[:, None, :, None]

    def dense(mats):
        return (mats[:, :, None, :] * same).reshape(channels, channels)

    gates = jnp.concatenate([dense(rate_all), dense(entry_all)], axis=1)

    slots = (blk + jnp.arange(MEMBERS, dtype=jnp.int32)) % MEMBERS
    token_ids = (
        (slots * TOKS + tok)[:, None] * OWN + jnp.arange(OWN, dtype=jnp.int32)[None, :]
    ).reshape(-1)
    starts = jnp.cumsum(lengths) - lengths
    opened = jnp.max(jnp.where(starts[None, :] <= token_ids[:, None], starts[None, :], 0), axis=1)
    places = (token_ids - opened).reshape(total_rows, 1).astype(jnp.int32)

    devices = MEMBERS * TOKS
    tail = lax.ppermute(
        inputs[OWN - HALO :], ("blk", "tok"), [(i, (i + 1) % devices) for i in range(devices)]
    )
    input_blocks, cotangent_blocks = pair_gather(inputs, cotangent)
    rows_all = jnp.concatenate(input_blocks + direct_gather(tail), axis=0)
    cotangent_all = jnp.concatenate(cotangent_blocks, axis=0)

    wide_values = rows_all.astype(f32)
    wide_one = (wide_values * norm_factor(wide_values) * mix_gain).astype(bf16)
    own_one = wide_one[:total_rows]
    conv_input = product(wide_one, input_all, bf16)
    branch = product(own_one, branch_all)
    state_shape = ((total_rows, channels), f32)
    conv, rates, entries, local, cum, edges = in_vmem(
        local_forward_kernel,
        [state_shape] * 5 + [((8, channels), f32)],
        [
            ((total_rows, 2 * channels), f32),
            ((total_rows, channels), bf16),
            ((total_rows, channels), bf16),
        ],
        count=7,
    )(conv_input, places, taps, shift, gates, bias, soft)
    chains = exchange_edges(edges, spots, False)
    states, mixture, carried = in_vmem(
        mix_kernel,
        [state_shape, ((total_rows, channels), bf16), ((MEMBERS, channels), f32)],
        [((4, 8, channels), f32)],
        scalars=1,
        count=8,
    )(spots, *chains, local, cum, branch)

    def rows_of(values):
        return [values[j * OWN : (j + 1) * OWN] for j in range(MEMBERS)]

    own_values = inputs.astype(f32)
    middle = own_values + ring_scatter(rows_of(product_back(mixture, out_turned)))

    factor_two = norm_factor(middle)
    normed_two = (middle * factor_two * feed_gain).astype(bf16)
    wide_two = jnp.concatenate(ring_gather(normed_two), axis=0)
    hidden_grad = product(after(cotangent_all, mixture), down_turned)
    gate_up = product(after(wide_two, hidden_grad), gate_up_all)
    gate_pre, up_pre = gate_up[:, :hidden_units], gate_up[:, hidden_units:]
    gate_act, gate_slope = gelu_parts(gate_pre)
    hidden = (gate_act * up_pre).astype(bf16)
    gate_grad = (gate_slope * hidden_grad * up_pre).astype(bf16)
    up_grad = (gate_act * hidden_grad).astype(bf16)
    both_grads = jnp.concatenate([gate_grad, up_grad], axis=1)
    two_shares = product_back(both_grads, gate_up_all)
    two_grad = ring_scatter(rows_of(two_shares))
    middle_grad = cotangent.astype(f32) + normalize_back(two_grad, middle, factor_two, feed_gain)
    grad_feed_scale = jnp.sum(two_grad * middle * factor_two, axis=0)
    feed_grads = lax.psum_scatter(
        feed_outer(wide_two, cotangent_all, after((gate_grad, up_grad, hidden), two_shares)),
        "tok",
        scatter_dimension=0,
        tiled=True,
    )
    layer_shares = product_back(after(hidden, two_shares), down_turned, bf16)

    middle_wide = jnp.concatenate(ring_gather(middle_grad.astype(bf16)), axis=0)
    mixture_grad = product(middle_wide, out_turned)
    branch_grad, sgrad, local_back, cum_back, back_edges = in_vmem(
        local_backward_kernel,
        [((total_rows, channels), bf16)] + [state_shape] * 3 + [((8, channels), f32)],
        count=6,
    )(mixture_grad, branch, states, rates, places, soft)
    chains_back = exchange_edges(back_edges, spots, True)
    branch_shares = product_back(after(branch_grad, back_edges), branch_all)
    grad_branch = product_outer(own_one, after(branch_grad, back_edges))
    grad_out = product_outer(middle_wide, after(mixture, back_edges))
    pregrads, igrad, owed, sums, tap_sums = in_vmem(
        finish_backward_kernel,
        [
            ((total_rows, 2 * channels), bf16),
            state_shape,
            ((MEMBERS * HALO, channels), f32),
            ((4, channels), f32),
            ((CONV, channels), f32),
        ],
        [
            ((total_rows, channels), f32),
            ((MEMBERS, channels), f32),
            ((4, 8, channels), f32),
        ],
        scalars=1,
        count=18,
    )(
        spots,
        *chains_back,
        after(sgrad, branch_shares),
        local_back,
        cum_back,
        states,
        carried,
        conv,
        rates,
        entries,
        places,
        soft,
        conv_input,
        taps,
        gates.T,
    )
    returned = lax.ppermute(
        owed.reshape(MEMBERS, HALO, channels)[:, HALO - 3 :],
        "tok",
        [(i, (i - 1) % TOKS) for i in range(TOKS)],
    )
    turned_on = jnp.concatenate([returned[1:], returned[:1]], axis=0)
    landing = jnp.where(tok == TOKS - 1, turned_on, returned)
    input_grad = igrad.reshape(MEMBERS, OWN, channels) + jnp.pad(
        landing, ((0, 0), (OWN - 3, 0), (0, 0))
    )
    input_low = input_grad.reshape(total_rows, channels).astype(bf16)
    one_shares = product_back(input_low, input_all) + branch_shares
    one_grad = ring_scatter(rows_of(one_shares))
    layer_out = middle + ring_scatter(rows_of(after(layer_shares, one_grad)))
    factor_one = norm_factor(own_values)
    first_grad = normalize_back(one_grad, own_values, factor_one, mix_gain)
    inputs_grad = (middle_grad + first_grad).astype(bf16)
    grad_mix_scale = jnp.sum(
        one_shares * wide_values[:total_rows] * norm_factor(wide_values[:total_rows]), axis=0
    )

    mixer_grads = chips_sum(
        jnp.concatenate([chip_sum(grad_out, spot[2]), chip_sum(grad_branch, spot[2])], axis=1)
    )
    grad_out, grad_branch = mixer_grads[:slice_rows], mixer_grads[slice_rows:]
    grad_input = product_outer(own_one, after(input_low, mixer_grads))
    dense_grads = product_outer(conv.astype(bf16), pregrads, f32)
    columns = jnp.arange(2 * channels, dtype=jnp.int32) % channels // block
    gate_grads = sum(
        jnp.where(columns == h, dense_grads[h * block : (h + 1) * block], 0.0)
        for h in range(groups)
    )
    small_grads = [
        gate_grads.reshape(TOKS, -1),
        jnp.moveaxis(tap_sums.reshape(CONV, TOKS, -1), 1, 0).reshape(TOKS, -1),
        jnp.moveaxis(sums.reshape(4, TOKS, -1), 1, 0).reshape(TOKS, -1),
        grad_mix_scale.reshape(TOKS, -1),
        grad_feed_scale.reshape(TOKS, -1),
    ]
    small_rows = jnp.concatenate(small_grads, axis=1).astype(bf16)
    small_rows = jnp.pad(small_rows, ((0, 0), (0, HALO * channels - small_rows.shape[1])))
    last_rows = jnp.concatenate(
        [
            grad_input.reshape(16, 2, slice_rows, channels),
            small_rows.reshape(16, 2, HALO, channels),
        ],
        axis=2,
    )
    last_rows = chips_sum(swap_sum(last_rows, spot[2]))
    grad_input, settled = last_rows[:slice_rows], last_rows[slice_rows:].reshape(-1)
    cuts, at = [], 0
    for member in small_grads:
        cuts.append(settled[at : at + member.shape[1]])
        at += member.shape[1]
    gate_own = jnp.transpose(cuts[0].reshape(block // TOKS, 2, groups, block), (1, 2, 0, 3))
    sums_own = cuts[2].reshape(4, -1)
    gains_own = jnp.concatenate(cuts[3:])
    gains_own = hop_sum(gains_own, "blk")
    own_logits = decay_logit.astype(f32)
    return (
        layer_out.astype(bf16),
        inputs_grad,
        gains_own[: width // TOKS],
        grad_branch,
        grad_input,
        cuts[1].reshape(CONV, -1),
        sums_own[0],
        gate_own[0],
        sums_own[1],
        gate_own[1],
        sums_own[2],
        sums_own[3] * decay_power * jax.nn.sigmoid(-own_logits),
        grad_out.T,
        gains_own[width // TOKS :],
        feed_grads[:, :hidden_units].astype(f32),
        feed_grads[:, hidden_units : 2 * hidden_units].astype(f32),
        feed_grads[:, 2 * hidden_units :].T.astype(f32),
    )


def solution(mesh):
    in_specs = (
        P(("blk", "tok"), None),
        P("tok"),
        P("tok", "blk"),
        P("tok", "blk"),
        P(None, ("blk", "tok")),
        P(("blk", "tok")),
        P("blk", "tok", None),
        P(("blk", "tok")),
        P("blk", "tok", None),
        P(("blk", "tok")),
        P(("blk", "tok")),
        P("blk", "tok"),
        P("tok"),
        P("tok", "blk"),
        P("tok", "blk"),
        P("blk", "tok"),
        P(),
        P(("blk", "tok"), None),
    )
    out_specs = (
        P(("blk", "tok"), None),
        P(("blk", "tok"), None),
        P("tok"),
        P("tok", "blk"),
        P("tok", "blk"),
        P(None, ("blk", "tok")),
        P(("blk", "tok")),
        P("blk", "tok", None),
        P(("blk", "tok")),
        P("blk", "tok", None),
        P(("blk", "tok")),
        P(("blk", "tok")),
        P("blk", "tok"),
        P("tok"),
        P("tok", "blk"),
        P("tok", "blk"),
        P("blk", "tok"),
    )
    return jax.shard_map(
        per_device, mesh=mesh, in_specs=in_specs, out_specs=out_specs, check_vma=False
    )
```

```python
import functools

import jax
import jax.numpy as jnp
from jax import lax
from jax.experimental import pallas as pl
from jax.experimental.pallas import tpu as pltpu
from jax.sharding import PartitionSpec as P

CONV = 4
MEMBERS = 4
TOKS = 32
OWN = 128
HALO = 16
SMALL = 24
FIRST = 104

eps_norm = 1e-06
decay_power = 8.0
f32 = jnp.float32
bf16 = jnp.bfloat16


def hop_blk(values, distance):
    return lax.ppermute(
        values, "blk", [(i, (i + distance) % MEMBERS) for i in range(MEMBERS)]
    )


def hop_tok(values, axis, distance):
    route = []
    for y in range(4):
        for z in range(4):
            for c in range(2):
                if axis == "y":
                    to = ((y + distance) % 4, z, c)
                elif axis == "z":
                    to = (y, (z + distance) % 4, c)
                else:
                    to = (y, z, (c + distance) % 2)
                route.append((y * 8 + z * 2 + c, to[0] * 8 + to[1] * 2 + to[2]))
    return lax.ppermute(values, "tok", route)


def hop(values, axis, distance):
    if axis == "blk":
        return hop_blk(values, distance)
    return hop_tok(values, axis, distance)


def hop_apart(values, distance, axis="blk"):
    route = []
    for b in range(MEMBERS):
        for t in range(TOKS):
            step = distance if t % 2 == 0 else -distance
            place = {"blk": b, "y": t // 8, "z": t // 2 % 4}
            place[axis] = (place[axis] + step) % 4
            to = place["blk"] * TOKS + place["y"] * 8 + place["z"] * 2 + t % 2
            route.append((b * TOKS + t, to))
    return lax.ppermute(values, ("blk", "tok"), route)


def either(core, first, second):
    return jnp.where(core == 0, first, second)


def ring_gather(values, core):
    behind = hop_apart(values, 1)
    ahead = hop_apart(values, -1)
    far = hop_apart(behind, 1)
    return [values, either(core, ahead, behind), far, either(core, behind, ahead)]


def ring_open(parts, core, axis="blk"):
    return hop_apart(parts[2].astype(bf16), 1, axis), ring_near(parts, core, axis)


def ring_near(parts, core, axis="blk"):
    return hop_apart(either(core, parts[3], parts[1]).astype(bf16), -1, axis)


def ring_pass(parts, far, core, axis="blk"):
    onward = either(core, parts[1], parts[3]).astype(f32) + far.astype(f32)
    return hop_apart(onward.astype(bf16), 1, axis)


def ring_close(parts, near, joined):
    return parts[0].astype(f32) + near.astype(f32) + joined.astype(f32)


def ring_scatter(parts, core, axis="blk"):
    far, near = ring_open(parts, core, axis)
    return ring_close(parts, near, ring_pass(parts, far, core, axis))


def direct_scatter(parts, axis):
    total = parts[0].astype(f32)
    for distance in range(1, 4):
        total = total + hop(parts[distance], axis, distance).astype(f32)
    return total


def narrow_sum(left, right):
    return (left.astype(f32) + right.astype(f32)).astype(bf16)


def after(value, *others):
    return lax.optimization_barrier((value,) + others)[0]


def hop_sum(values, axis):
    return values + hop(values, axis, 1) + hop(values, axis, -1) + hop(values, axis, 2)


def direct_gather(values, axis="blk"):
    return [values] + [hop(values, axis, -d) for d in range(1, 4)]


def turned(values, place, axis=0):
    return [
        lax.dynamic_index_in_dim(values, (place + j) % 4, axis, keepdims=False) for j in range(4)
    ]


def swap_sum(parts, core):
    mine = lax.dynamic_index_in_dim(parts, core, 1, keepdims=False)
    theirs = lax.dynamic_index_in_dim(parts, 1 - core, 1, keepdims=False)
    return narrow_sum(mine, hop(theirs, "core", 1))


def chip_sum(values, core):
    return swap_sum(values.reshape(16, 2, -1, values.shape[1]), core)


def chips_sum(values):
    cores = [[2 * i + c for i in range(16)] for c in range(2)]
    terms = lax.all_to_all(values, "tok", 0, 0, axis_index_groups=cores, tiled=True)
    return jnp.sum(terms.astype(f32), axis=0)


def together(*values):
    return lax.optimization_barrier(values)


def small_gather(values, before_last):
    values = jnp.stack([values, hop(values, "core", 1)])
    values = jnp.stack(direct_gather(values, "z"))
    return jnp.stack(direct_gather(after(values, *before_last), "y"))


def product(operand, weight, out=f32):
    return jnp.dot(operand, weight, preferred_element_type=f32).astype(out)


def product_back(operand, weight, out=f32):
    return lax.dot_general(
        operand, weight, (((1,), (1,)), ((), ())), preferred_element_type=f32
    ).astype(out)


def product_outer(operand, weight, out=bf16):
    return lax.dot_general(
        operand, weight, (((0,), (0,)), ((), ())), preferred_element_type=f32
    ).astype(out)


def norm_factor(values):
    return lax.rsqrt(jnp.mean(values * values, axis=1, keepdims=True) + eps_norm)


def normalize_back(gradient, values, factor, gains):
    weighted = gradient * gains
    return factor * weighted - values * (factor * factor * factor) * jnp.mean(
        weighted * values, axis=1, keepdims=True
    )


def sigmoid(values):
    return 1.0 / (1.0 + jnp.exp(-values))


def one_minus_exp(values):
    series = 1.0 + values * (1.0 / 6.0)
    for order in (5.0, 4.0, 3.0, 2.0):
        series = 1.0 + values * series * (1.0 / order)
    return jnp.where(values > -0.1, -values * series, 1.0 - jnp.exp(values))


def inverse_root(values):
    return lax.rsqrt(jnp.maximum(values, 1e-37))


def gelu_parts(values):
    root = 0.7978845608028654
    square = values * values
    bent = jnp.tanh(root * values * (1.0 + 0.044715 * square))
    half = 0.5 * (1.0 + bent)
    slope = half + 0.5 * values * (1.0 - bent * bent) * root * (1.0 + 3.0 * 0.044715 * square)
    return values * half, slope


def rows_at(start, size):
    return pl.ds(pl.multiple_of(start, size), size)


def conv_rows(ci_ref, slot, tile):
    base = slot * OWN + tile * HALO
    before = jnp.where(tile == 0, MEMBERS * OWN + slot * HALO, base - HALO)
    return jnp.concatenate(
        [ci_ref[rows_at(before, HALO), :].astype(f32), ci_ref[rows_at(base, HALO), :].astype(f32)],
        axis=0,
    )


def local_forward_kernel(
    ci_ref,
    place_ref,
    taps_ref,
    shift_ref,
    blocks_ref,
    bias_ref,
    soft_ref,
    conv_ref,
    rate_ref,
    entry_ref,
    local_ref,
    cum_ref,
    edge_ref,
    gates_ref,
    pre_ref,
    high_ref,
):
    channels = conv_ref.shape[1]
    block = blocks_ref.shape[0]
    width = 2 * channels
    columns = lax.broadcasted_iota(jnp.int32, (HALO, width), 1)
    columns = jnp.where(columns >= channels, columns - channels, columns)
    for group in range(channels // block):
        inside = (columns >= group * block) & (columns < (group + 1) * block)

        def spread_gates(step, carry):
            rows = blocks_ref[rows_at(step * HALO, HALO), :].astype(f32)
            gates_ref[rows_at(group * block + step * HALO, HALO), :] = jnp.where(
                inside, rows, 0.0
            ).astype(bf16)
            return carry

        lax.fori_loop(0, block // HALO, spread_gates, 0)

    for slot in range(MEMBERS):

        def convolve(tile, carry):
            base = slot * OWN + tile * HALO
            rows = conv_rows(ci_ref, slot, tile)
            places = place_ref[rows_at(base, HALO), :]
            total = shift_ref[...] + taps_ref[0:1, :] * rows[HALO:]
            for tap in range(1, CONV):
                lagged = pltpu.roll(rows, tap, 0)[HALO:]
                total = total + taps_ref[tap : tap + 1, :] * jnp.where(places >= tap, lagged, 0.0)
            conv_ref[rows_at(base, HALO), :] = total
            high_ref[rows_at(base, HALO), :] = total.astype(bf16)
            return carry

        lax.fori_loop(0, OWN // HALO, convolve, 0)

    def gate(step, carry):
        columns = pl.ds(pl.multiple_of(step * 256, 256), 256)
        weight = gates_ref[:, columns]
        pre_ref[:, columns] = (
            jnp.dot(high_ref[...], weight, preferred_element_type=f32) + bias_ref[:, columns]
        )
        return carry

    lax.fori_loop(0, 2 * channels // 256, gate, 0)

    row_ids = lax.broadcasted_iota(jnp.int32, (8, channels), 0)

    def scan(tile, carry):
        ends = []
        for slot in range(MEMBERS):
            base = slot * OWN + tile * 8
            rows = rows_at(base, 8)
            rates = sigmoid(pre_ref[rows, :channels])
            entries = 0.5 * jnp.tanh(0.5 * pre_ref[rows, channels:]) + 0.5
            log_keep = -soft_ref[...] * rates
            resets = place_ref[rows, :] == 0
            keeps = jnp.where(resets, 0.0, jnp.exp(log_keep))
            squared = one_minus_exp(2.0 * log_keep)
            scaling = jnp.where(resets, 1.0, squared * inverse_root(squared))
            value = entries * conv_ref[rows, :] * scaling
            coeff = keeps
            for distance in (1, 2, 4):
                reach = row_ids >= distance
                value = value + coeff * jnp.where(reach, pltpu.roll(value, distance, 0), 0.0)
                coeff = coeff * jnp.where(reach, pltpu.roll(coeff, distance, 0), 1.0)
            cum, state = carry[2 * slot], carry[2 * slot + 1]
            value = value + coeff * state
            coeff = coeff * cum
            rate_ref[rows, :] = rates
            entry_ref[rows, :] = entries
            local_ref[rows, :] = value
            cum_ref[rows, :] = coeff
            ends += [coeff[7:8], value[7:8]]
        return tuple(ends)

    start = (jnp.ones((1, channels), f32), jnp.zeros((1, channels), f32)) * MEMBERS
    ends = lax.fori_loop(0, OWN // 8, scan, start)
    edge_ref[...] = jnp.concatenate(ends[0::2] + ends[1::2], axis=0)


def extended(pair, block):
    return pair[0] * block[:4], block[:4] * pair[1] + block[4:]


def whole_chain(channels):
    return jnp.ones((4, channels), f32), jnp.zeros((4, channels), f32)


def fold_near_kernel(backward, spot_ref, *refs):
    pieces, (total_ref, prefix_ref, held_ref) = refs[:4], refs[4:]
    z, c = spot_ref[2], spot_ref[3]
    for distance, piece in enumerate(pieces):
        held_ref[distance] = piece[...]
    chain = whole_chain(total_ref.shape[1])
    prefix = chain
    for place in reversed(range(8)) if backward else range(8):
        here = place == 2 * z + c
        prefix = tuple(jnp.where(here, new, old) for new, old in zip(chain, prefix))
        distance = jnp.bitwise_and(place // 2 - z + 4, 3)
        chain = extended(chain, held_ref[distance, jnp.bitwise_xor(place % 2, c)])
    total_ref[...] = jnp.concatenate(chain, axis=0)
    prefix_ref[...] = jnp.concatenate(prefix, axis=0)


def slot_carries(backward, spot_ref, pieces, prefix_ref, held_ref):
    y = spot_ref[1]
    channels = prefix_ref.shape[1]
    for distance, piece in enumerate(pieces):
        held_ref[distance] = piece[...]
    total = whole_chain(channels)
    prefix = total
    for place in reversed(range(4)) if backward else range(4):
        here = place == y
        prefix = tuple(jnp.where(here, new, old) for new, old in zip(total, prefix))
        total = extended(total, held_ref[jnp.bitwise_and(place - y + 4, 3)])
    prefix = extended(prefix, prefix_ref[...])
    current = jnp.zeros((1, channels), f32)
    carries = [None] * MEMBERS
    for _ in range(2):
        for slot in reversed(range(MEMBERS)) if backward else range(MEMBERS):
            one = slice(slot, slot + 1)
            carries[slot] = prefix[0][one] * current + prefix[1][one]
            current = total[0][one] * current + total[1][one]
    return carries


def mix_kernel(
    spot_ref,
    piece0,
    piece1,
    piece2,
    piece3,
    prefix_ref,
    local_ref,
    cum_ref,
    branch_ref,
    state_ref,
    mixed_ref,
    carry_ref,
    held_ref,
):
    pieces = (piece0, piece1, piece2, piece3)
    carries = slot_carries(False, spot_ref, pieces, prefix_ref, held_ref)
    carry_ref[...] = jnp.concatenate(carries, axis=0)

    def apply(tile, token):
        for slot in range(MEMBERS):
            rows = rows_at(slot * OWN + tile * HALO, HALO)
            states = local_ref[rows, :] + cum_ref[rows, :] * carry_ref[slot : slot + 1, :]
            state_ref[rows, :] = states
            mixed_ref[rows, :] = (states * gelu_parts(branch_ref[rows, :])[0]).astype(bf16)
        return token

    lax.fori_loop(0, OWN // HALO, apply, 0)


def local_backward_kernel(
    grad_ref,
    branch_ref,
    state_ref,
    rate_ref,
    place_ref,
    soft_ref,
    bgrad_ref,
    sgrad_ref,
    local_ref,
    cum_ref,
    edge_ref,
):
    channels = grad_ref.shape[1]
    row_ids = lax.broadcasted_iota(jnp.int32, (8, channels), 0)

    def scan(step, carry):
        ends = []
        for slot in range(MEMBERS):
            pieces = {}
            base = slot * OWN + OWN - HALO - step * HALO
            cum, after = carry[2 * slot], carry[2 * slot + 1]
            slopes = []
            for part in (1, 0):
                rows = rows_at(base + 8 * part, 8)
                gated, slope = gelu_parts(branch_ref[rows, :])
                gradient = grad_ref[rows, :]
                slopes.append(slope * gradient * state_ref[rows, :])
                sgrad = gradient * gated
                keeps = jnp.where(
                    place_ref[rows, :] == 0, 0.0, jnp.exp(-soft_ref[...] * rate_ref[rows, :])
                )
                coeff = keeps
                value = keeps * sgrad
                for distance in (1, 2, 4):
                    reach = row_ids < 8 - distance
                    value = value + coeff * jnp.where(
                        reach, pltpu.roll(value, 8 - distance, 0), 0.0
                    )
                    coeff = coeff * jnp.where(reach, pltpu.roll(coeff, 8 - distance, 0), 1.0)
                value = value + coeff * after
                coeff = coeff * cum
                sgrad_ref[rows, :] = sgrad
                local_ref[rows, :] = value
                cum_ref[rows, :] = coeff
                cum, after = coeff[0:1], value[0:1]
            bgrad_ref[rows_at(base, HALO), :] = jnp.concatenate(
                [slopes[1], slopes[0]], axis=0
            ).astype(bf16)
            ends += [cum, after]
        return tuple(ends)

    start = (jnp.ones((1, channels), f32), jnp.zeros((1, channels), f32)) * MEMBERS
    ends = lax.fori_loop(0, OWN // HALO, scan, start)
    edge_ref[...] = jnp.concatenate(ends[0::2] + ends[1::2], axis=0)


def finish_backward_kernel(
    spot_ref,
    piece0,
    piece1,
    piece2,
    piece3,
    prefix_ref,
    sgrad_ref,
    local_ref,
    cum_ref,
    state_ref,
    carry_ref,
    conv_ref,
    rate_ref,
    entry_ref,
    place_ref,
    soft_ref,
    ci_ref,
    taps_ref,
    gates_ref,
    pregrad_ref,
    igrad_ref,
    owed_ref,
    sums_ref,
    cgrad_ref,
    back_ref,
    held_ref,
):
    channels = conv_ref.shape[1]
    pieces = (piece0, piece1, piece2, piece3)
    carries = slot_carries(True, spot_ref, pieces, prefix_ref, held_ref)
    back_ref[...] = jnp.concatenate(carries, axis=0)

    row_ids = lax.broadcasted_iota(jnp.int32, (8, channels), 0)
    zero = jnp.zeros((8, channels), f32)
    logit_sum, rate_sum, entry_sum = zero, zero, zero
    for slot in range(MEMBERS):

        def gate_grads(step, carry):
            later, logit_sum, rate_sum, entry_sum = carry
            base = slot * OWN + OWN - HALO - step * HALO
            low_rate, low_entry = [], []
            for part in (1, 0):
                first = base + 8 * part
                rows = rows_at(first, 8)
                held = local_ref[rows, :] + cum_ref[rows, :] * back_ref[slot : slot + 1, :]
                following = jnp.where(row_ids == 7, later, pltpu.roll(held, 7, 0))
                adjoint = sgrad_ref[rows, :] + following
                later = held[0:1]
                ahead = state_ref[rows_at(jnp.maximum(first - 8, 0), 8), :][7:8]
                at_start = first == slot * OWN
                ahead = jnp.where(at_start, carry_ref[slot : slot + 1, :], ahead)
                previous = jnp.where(row_ids == 0, ahead, pltpu.roll(state_ref[rows, :], 1, 0))
                rates, entries, conv = rate_ref[rows, :], entry_ref[rows, :], conv_ref[rows, :]
                resets = place_ref[rows, :] == 0
                log_keep = -soft_ref[...] * rates
                squared = one_minus_exp(2.0 * log_keep)
                inverse = inverse_root(squared)
                scaling = jnp.where(resets, 1.0, squared * inverse)
                turn = jnp.where(resets, 0.0, (1.0 - squared) * inverse)
                weighed = adjoint * entries
                log_grad = held * previous - weighed * conv * turn
                rate_part = log_grad * rates
                logit_sum = logit_sum + rate_part
                rate_grad = -soft_ref[...] * rate_part * (1.0 - rates)
                direct = weighed * scaling
                entry_grad = direct * conv * (1.0 - entries)
                rate_sum = rate_sum + rate_grad
                entry_sum = entry_sum + entry_grad
                cgrad_ref[rows, :] = direct
                low_rate.append(rate_grad)
                low_entry.append(entry_grad)
            rows = rows_at(base, HALO)
            pregrad_ref[rows, :channels] = jnp.concatenate(low_rate[::-1], axis=0).astype(bf16)
            pregrad_ref[rows, channels:] = jnp.concatenate(low_entry[::-1], axis=0).astype(bf16)
            return later, logit_sum, rate_sum, entry_sum

        _, logit_sum, rate_sum, entry_sum = lax.fori_loop(
            0,
            OWN // HALO,
            gate_grads,
            (back_ref[slot : slot + 1, :], logit_sum, rate_sum, entry_sum),
        )

    def gate_back(step, carry):
        columns = pl.ds(pl.multiple_of(step * 128, 128), 128)
        cgrad_ref[:, columns] += lax.dot_general(
            pregrad_ref[...],
            gates_ref[columns, :],
            (((1,), (1,)), ((), ())),
            preferred_element_type=f32,
        )
        return carry

    lax.fori_loop(0, channels // 128, gate_back, 0)

    shift_sum = jnp.zeros((HALO, channels), f32)
    tap_sums = [shift_sum] * CONV
    for slot in range(MEMBERS):

        def spread(rows, places):
            return [rows] + [jnp.where(places >= tap, rows, 0.0) for tap in range(1, CONV)]

        def shifted_sum(current, following):
            total = taps_ref[0:1, :] * current[0]
            for tap in range(1, CONV):
                both = jnp.concatenate([current[tap], following[tap]], axis=0)
                total = total + taps_ref[tap : tap + 1, :] * pltpu.roll(both, 2 * HALO - tap, 0)[:HALO]
            return total

        def conv_back(tile, carry):
            shift_sum, tap_sums = carry
            base = slot * OWN + tile * HALO
            rows = rows_at(base, HALO)
            after = jnp.minimum(base + HALO, slot * OWN + OWN - HALO)
            next_rows = rows_at(after, HALO)
            last = jnp.where(tile == OWN // HALO - 1, 0.0, 1.0)
            grads = spread(cgrad_ref[rows, :], place_ref[rows, :])
            coming = spread(cgrad_ref[next_rows, :] * last, place_ref[next_rows, :])
            igrad_ref[rows, :] = shifted_sum(grads, coming)
            inputs = conv_rows(ci_ref, slot, tile)
            shift_sum = shift_sum + grads[0]
            sums = [tap_sums[0] + grads[0] * inputs[HALO:]]
            for tap in range(1, CONV):
                sums.append(tap_sums[tap] + grads[tap] * pltpu.roll(inputs, tap, 0)[HALO:])
            return shift_sum, sums

        shift_sum, tap_sums = lax.fori_loop(0, OWN // HALO, conv_back, (shift_sum, tap_sums))
        rows = rows_at(slot * OWN, HALO)
        first = spread(cgrad_ref[rows, :], place_ref[rows, :])
        owed_ref[slot * HALO : (slot + 1) * HALO, :] = shifted_sum(
            [jnp.zeros((HALO, channels), f32)] * CONV, first
        )

    def total_rows(values):
        return jnp.sum(values, axis=0, keepdims=True)

    sums_ref[...] = jnp.concatenate(
        [total_rows(v) for v in [shift_sum, rate_sum, entry_sum, logit_sum] + list(tap_sums)],
        axis=0,
    )


def in_vmem(kernel, outs, scratch=(), scalars=0, count=1, moved=0):
    vmem = pl.BlockSpec(memory_space=pltpu.VMEM)
    smem = pl.BlockSpec(memory_space=pltpu.SMEM)
    return pl.pallas_call(
        kernel,
        out_shape=[jax.ShapeDtypeStruct(shape, dtype) for shape, dtype in outs],
        in_specs=[smem] * scalars + [vmem] * count,
        out_specs=[vmem] * len(outs),
        scratch_shapes=[pltpu.VMEM(shape, dtype) for shape, dtype in scratch],
        compiler_params=pltpu.CompilerParams(vmem_limit_bytes=40 * 1024 * 1024),
        cost_estimate=pl.CostEstimate(flops=0, bytes_accessed=moved, transcendentals=0),
    )


def exchange_edges(edges, spots, backward):
    channels = edges.shape[1]
    near = jnp.stack([edges, hop(edges, "core", 1)])
    total, prefix = in_vmem(
        functools.partial(fold_near_kernel, backward),
        [((8, channels), f32)] * 2,
        [((4, 2, 8, channels), f32)],
        scalars=1,
        count=4,
        moved=3_000_000,
    )(spots, *direct_gather(near, "z"))
    return direct_gather(total, "y") + [prefix], near


def outer_kernel(lhs_one, lhs_two, rhs_one, rhs_two, rhs_three, out_ref):
    def settle(lhs, rhs):
        out_ref[...] = lax.dot_general(
            lhs[...], rhs[...], (((0,), (0,)), ((), ())), preferred_element_type=f32
        ).astype(bf16)

    for step, (lhs, rhs) in enumerate(
        ((lhs_one, rhs_one), (lhs_one, rhs_two), (lhs_two, rhs_three))
    ):
        pl.when(pl.program_id(0) == step)(functools.partial(settle, lhs, rhs))


def feed_outer(lhs_one, lhs_two, rhs):
    rows, features = lhs_one.shape
    columns = rhs[0].shape[1]
    height = 1024
    whole = pl.BlockSpec((rows, columns), lambda j, i: (0, 0))
    return pl.pallas_call(
        outer_kernel,
        grid=(3, features // height),
        in_specs=[
            pl.BlockSpec((rows, height), lambda j, i: (0, jnp.where(j < 2, i, 0))),
            pl.BlockSpec((rows, height), lambda j, i: (0, jnp.where(j < 2, 0, i))),
            whole,
            whole,
            whole,
        ],
        out_specs=pl.BlockSpec((height, columns), lambda j, i: (i, j)),
        out_shape=jax.ShapeDtypeStruct((features, 3 * columns), bf16),
        compiler_params=pltpu.CompilerParams(vmem_limit_bytes=40 * 1024 * 1024),
        cost_estimate=pl.CostEstimate(
            flops=6 * rows * features * columns,
            bytes_accessed=6 * features * columns,
            transcendentals=0,
        ),
    )(lhs_one, lhs_two, *rhs)


def small_kernel(cut, conv_ref, pregrad_ref, sums_ref, extra_ref, out_ref):
    channels = conv_ref.shape[1]
    width = 2 * channels
    block = cut * TOKS
    dense = lax.dot_general(
        conv_ref[...].astype(bf16),
        pregrad_ref[...],
        (((0,), (0,)), ((), ())),
        preferred_element_type=f32,
    )
    columns = lax.broadcasted_iota(jnp.int32, (block, width), 1)
    columns = jnp.where(columns >= channels, columns - channels, columns)
    gates = jnp.zeros((block, width), f32)
    for group in range(channels // block):
        inside = (columns >= group * block) & (columns < (group + 1) * block)
        gates = jnp.where(inside, dense[group * block : (group + 1) * block], gates)
    spare = jnp.zeros((SMALL - 2 * cut - 9, channels), f32)
    for tok in range(TOKS):
        rows = gates[tok * cut : (tok + 1) * cut]
        pieces = [rows[:, :channels], rows[:, channels:], sums_ref[...]]
        pieces += [extra_ref[tok : tok + 1, :], spare]
        out_ref[tok] = jnp.concatenate(pieces, axis=0).astype(bf16)


def halves_kernel(count, spot_ref, small_ref, *refs):
    core = spot_ref[3]
    mine_ref, theirs_ref = refs[2 * count :]
    chips, rows, _ = mine_ref.shape
    rows = (rows - SMALL) // count
    for which in range(count):
        sums = lax.dot_general(
            refs[which][...],
            refs[count + which][...],
            (((0,), (0,)), ((), ())),
            preferred_element_type=f32,
        )
        for chip in range(chips):
            low = sums[2 * chip * rows : (2 * chip + 1) * rows]
            high = sums[(2 * chip + 1) * rows : (2 * chip + 2) * rows]
            at = slice(which * rows, (which + 1) * rows)
            mine_ref[chip, at, :] = jnp.where(core == 0, low, high).astype(bf16)
            theirs_ref[chip, at, :] = jnp.where(core == 0, high, low).astype(bf16)
    for chip in range(chips):
        low, high = small_ref[2 * chip].astype(f32), small_ref[2 * chip + 1].astype(f32)
        at = slice(count * rows, count * rows + SMALL)
        mine_ref[chip, at, :] = jnp.where(core == 0, low, high).astype(bf16)
        theirs_ref[chip, at, :] = jnp.where(core == 0, high, low).astype(bf16)


def outer_halves(spots, small, lhs, rhs):
    count = len(lhs)
    features = lhs[0].shape[1]
    rows, columns = rhs[0].shape
    height = 1024
    chips = height // 128
    total = 64 * count + SMALL
    shape = jax.ShapeDtypeStruct((features // 128, total, columns), bf16)
    out_spec = pl.BlockSpec((chips, total, columns), lambda i: (i, 0, 0))
    return pl.pallas_call(
        functools.partial(halves_kernel, count),
        grid=(features // height,),
        in_specs=[pl.BlockSpec(memory_space=pltpu.SMEM)]
        + [pl.BlockSpec((2 * chips, SMALL, columns), lambda i: (i, 0, 0))]
        + [pl.BlockSpec((rows, height), lambda i: (0, i))] * count
        + [pl.BlockSpec((rows, columns), lambda i: (0, 0))] * count,
        out_specs=[out_spec] * 2,
        out_shape=[shape] * 2,
        compiler_params=pltpu.CompilerParams(vmem_limit_bytes=40 * 1024 * 1024),
        cost_estimate=pl.CostEstimate(
            flops=2 * count * rows * features * columns,
            bytes_accessed=20_000_000,
            transcendentals=0,
        ),
    )(spots, small, *lhs, *rhs)


def per_device(
    inputs,
    mix_scale,
    branch_mat,
    input_mat,
    conv_taps,
    conv_shift,
    rate_mat,
    rate_shift,
    entry_mat,
    entry_shift,
    decay_logit,
    out_mat,
    feed_scale,
    gate_mat,
    up_mat,
    down_mat,
    lengths,
    cotangent,
):
    blk = lax.axis_index("blk")
    tok = lax.axis_index("tok")
    spot = (tok // 8, (tok // 2) % 4, tok % 2)
    spots = jnp.stack([tok] + list(spot)).astype(jnp.int32)
    channels = branch_mat.shape[1]
    hidden_units = gate_mat.shape[1]
    slice_rows = branch_mat.shape[0]
    total_rows = MEMBERS * OWN

    groups, cut, block = rate_mat.shape
    own_channels = conv_shift.shape[0]
    vectors = [conv_taps, conv_shift[None], rate_shift[None], entry_shift[None], decay_logit[None]]
    vectors = jnp.concatenate(vectors, axis=0).reshape(-1)
    extras = jnp.concatenate([vectors, mix_scale, feed_scale])
    extras = jnp.pad(extras, (0, channels - extras.shape[0]))[None]
    smalls = [jnp.moveaxis(mats, 0, 1).reshape(cut, channels) for mats in (rate_mat, entry_mat)]
    smalls = jnp.concatenate(smalls + [extras], axis=0)
    smalls = jnp.pad(smalls, ((0, HALO - smalls.shape[0]), (0, 0)))
    input_blocks = ring_gather(inputs, spot[2])
    near = after(small_gather(smalls, (input_blocks[1], input_blocks[3])), input_blocks[2])
    for axis, place in ((2, spot[2]), (1, spot[1]), (0, spot[0])):
        near = jnp.roll(near, place, axis)
    near = near.reshape(TOKS, HALO, channels)
    mixer_all = lax.all_gather(
        jnp.concatenate([input_mat, branch_mat, out_mat.T], axis=1), "tok", axis=0, tiled=True
    )
    devices = MEMBERS * TOKS
    tail = lax.ppermute(
        inputs[OWN - HALO :], ("blk", "tok"), [(i, (i + 1) % devices) for i in range(devices)]
    )
    cotangent_blocks = ring_gather(after(cotangent, input_blocks[2]), spot[2])
    rows_all = jnp.concatenate(input_blocks + direct_gather(tail), axis=0)
    cotangent_all = jnp.concatenate(cotangent_blocks, axis=0)

    extras = near[:, 2 * cut]
    vectors = extras[:, : 8 * own_channels].reshape(TOKS, 8, own_channels).astype(f32)
    vectors = jnp.moveaxis(vectors, 0, 1).reshape(8, channels)
    gains = extras[:, 8 * own_channels : 8 * own_channels + 2 * slice_rows].astype(f32)
    mix_gain = gains[:, :slice_rows].reshape(1, -1)
    feed_gain = gains[:, slice_rows:].reshape(1, -1)
    wide_values = rows_all.astype(f32)
    wide_one = (wide_values * norm_factor(wide_values) * mix_gain).astype(bf16)
    taps, shift = vectors[:CONV], vectors[4:5]
    bias = jnp.concatenate([vectors[5:6], vectors[6:7]], axis=1)
    soft = decay_power * jax.nn.softplus(-vectors[7:8])
    blocks = [near[:, i * cut : (i + 1) * cut].reshape(block, channels) for i in range(2)]
    blocks = after(jnp.concatenate(blocks, axis=1), cotangent_blocks[2])
    feed_own = jnp.concatenate([gate_mat, up_mat, down_mat.T], axis=1)
    feed_all = lax.all_gather(after(feed_own, wide_one, blocks), "tok", axis=0, tiled=True)
    gate_up_all = feed_all[:, : 2 * hidden_units]
    down_turned = feed_all[:, 2 * hidden_units :]
    own_one = wide_one[:total_rows]
    input_all = mixer_all[:, :channels]
    branch_all = mixer_all[:, channels : 2 * channels]
    project_all = mixer_all[:, : 2 * channels]
    out_turned = mixer_all[:, 2 * channels : 3 * channels]

    slots = (blk + jnp.arange(MEMBERS, dtype=jnp.int32)) % MEMBERS
    token_ids = (
        (slots * TOKS + tok)[:, None] * OWN + jnp.arange(OWN, dtype=jnp.int32)[None, :]
    ).reshape(-1)
    starts = jnp.cumsum(lengths) - lengths
    opened = jnp.max(jnp.where(starts[None, :] <= token_ids[:, None], starts[None, :], 0), axis=1)
    places = (token_ids - opened).reshape(total_rows, 1).astype(jnp.int32)

    conv_input = product(wide_one, input_all, bf16)
    branch = product(own_one, branch_all)
    state_shape = ((total_rows, channels), f32)
    conv, rates, entries, local, cum, edges, gates = in_vmem(
        local_forward_kernel,
        [state_shape] * 5 + [((8, channels), f32), ((channels, 2 * channels), bf16)],
        [
            ((total_rows, 2 * channels), f32),
            ((total_rows, channels), bf16),
        ],
        count=7,
        moved=30_000_000,
    )(conv_input, places, taps, shift, blocks, bias, soft)
    chains, _ = exchange_edges(edges, spots, False)
    states, mixture, carried = in_vmem(
        mix_kernel,
        [state_shape, ((total_rows, channels), bf16), ((MEMBERS, channels), f32)],
        [((4, 8, channels), f32)],
        scalars=1,
        count=8,
        moved=4_500_000,
    )(spots, *chains, local, cum, branch)

    def rows_of(values):
        return [values[j * OWN : (j + 1) * OWN] for j in range(MEMBERS)]

    own_values = inputs.astype(f32)
    middle = own_values + ring_scatter(rows_of(product_back(mixture, out_turned)), spot[2])

    factor_two = norm_factor(middle)
    normed_two = (middle * factor_two * feed_gain).astype(bf16)
    hidden_grad = product(after(cotangent_all, mixture), down_turned)
    blocks_two = ring_gather(normed_two, spot[2])
    blocks_two[2] = after(blocks_two[2], hidden_grad)
    wide_two = jnp.concatenate(blocks_two, axis=0)
    gate_up = product(wide_two, gate_up_all)
    gate_pre, up_pre = gate_up[:, :hidden_units], gate_up[:, hidden_units:]
    gate_act, gate_slope = gelu_parts(gate_pre)
    hidden = (gate_act * up_pre).astype(bf16)
    gate_grad = (gate_slope * hidden_grad * up_pre).astype(bf16)
    up_grad = (gate_act * hidden_grad).astype(bf16)
    both_grads = jnp.concatenate([gate_grad, up_grad], axis=1)
    two_shares = product_back(both_grads, gate_up_all)
    two_parts = rows_of(two_shares)
    two_far, two_near = ring_open(two_parts, spot[2])
    two_grad = ring_close(two_parts, two_near, ring_pass(two_parts, two_far, spot[2]))
    middle_grad = cotangent.astype(f32) + normalize_back(two_grad, middle, factor_two, feed_gain)
    grad_feed_scale = jnp.sum(two_grad * middle * factor_two, axis=0)
    feed_shares = feed_outer(
        wide_two, cotangent_all, after((gate_grad, up_grad, hidden), two_shares)
    )
    feed_grads = lax.psum_scatter(
        after(feed_shares, two_grad), "tok", scatter_dimension=0, tiled=True
    )

    layer_shares = product_back(after(hidden, two_far), down_turned, bf16)
    middle_blocks = ring_gather(middle_grad.astype(bf16), spot[2])
    middle_blocks[2] = after(middle_blocks[2], layer_shares)
    middle_wide = jnp.concatenate(middle_blocks, axis=0)
    mixture_grad = product(middle_wide, out_turned)
    branch_grad, sgrad, local_back, cum_back, back_edges = in_vmem(
        local_backward_kernel,
        [((total_rows, channels), bf16)] + [state_shape] * 3 + [((8, channels), f32)],
        count=6,
        moved=9_500_000,
    )(mixture_grad, branch, states, rates, places, soft)
    chains_back, near_back = exchange_edges(back_edges, spots, True)
    pregrads, igrad, owed, sums = in_vmem(
        finish_backward_kernel,
        [
            ((total_rows, 2 * channels), bf16),
            state_shape,
            ((MEMBERS * HALO, channels), f32),
            ((8, channels), f32),
        ],
        [
            ((total_rows, channels), f32),
            ((MEMBERS, channels), f32),
            ((4, 8, channels), f32),
        ],
        scalars=1,
        count=18,
        moved=40_000_000,
    )(
        spots,
        *chains_back,
        sgrad,
        local_back,
        cum_back,
        states,
        carried,
        conv,
        rates,
        entries,
        places,
        soft,
        conv_input,
        taps,
        gates,
    )
    returned = lax.ppermute(
        owed.reshape(MEMBERS, HALO, channels)[:, HALO - 3 :],
        "tok",
        [(i, (i - 1) % TOKS) for i in range(TOKS)],
    )
    turned_on = jnp.concatenate([returned[1:], returned[:1]], axis=0)
    landing = jnp.where(tok == TOKS - 1, turned_on, returned)
    input_grad = igrad.reshape(MEMBERS, OWN, channels) + jnp.pad(
        landing, ((0, 0), (OWN - 3, 0), (0, 0))
    )
    input_low = input_grad.reshape(total_rows, channels).astype(bf16)
    feed_rows = jnp.pad(
        grad_feed_scale.reshape(TOKS, slice_rows), ((0, 0), (0, channels - slice_rows))
    )
    (small_rows,) = in_vmem(
        functools.partial(small_kernel, cut),
        [((TOKS, SMALL, channels), bf16)],
        count=4,
        moved=11_000_000,
    )(conv, pregrads, sums, feed_rows)

    core = spot[2]
    weight_mine, weight_theirs = outer_halves(
        spots, small_rows, (middle_wide, wide_one, wide_one), (mixture, branch_grad, input_low)
    )
    weight_other = hop(weight_theirs, "core", 1)
    late = after(input_low, weight_theirs)
    one_shares = product_back(jnp.concatenate([late, branch_grad], axis=1), project_all, bf16)
    one_parts = rows_of(one_shares)
    one_grad = ring_scatter(one_parts, core)
    factor_one = norm_factor(own_values)
    first_grad = normalize_back(one_grad, own_values, factor_one, mix_gain)
    inputs_grad = (middle_grad + first_grad).astype(bf16)
    settled = chips_sum(narrow_sum(weight_mine, weight_other))
    layer_out = middle + ring_scatter(rows_of(after(layer_shares, one_grad)), core)
    grad_out, grad_branch, grad_input = [
        settled[i * slice_rows : (i + 1) * slice_rows] for i in range(3)
    ]
    settled = settled[3 * slice_rows :]
    grad_mix_scale = jnp.sum(
        grad_branch * branch_mat.astype(f32) + grad_input * input_mat.astype(f32), axis=1
    ) / mix_scale.astype(f32)
    gains_own = jnp.concatenate([grad_mix_scale, settled[2 * cut + 8, :slice_rows]])
    gains_own = hop_sum(gains_own.reshape(1, -1), "blk")[0]
    gate_own = [
        jnp.moveaxis(settled[i * cut : (i + 1) * cut].reshape(cut, groups, block), 1, 0)
        for i in range(2)
    ]
    sums_own = lax.dynamic_slice(
        settled[2 * cut : 2 * cut + 8], (0, tok * own_channels), (8, own_channels)
    )
    own_logits = decay_logit.astype(f32)
    return (
        layer_out.astype(bf16),
        inputs_grad,
        gains_own[:slice_rows],
        grad_branch,
        grad_input,
        sums_own[4:],
        sums_own[0],
        gate_own[0],
        sums_own[1],
        gate_own[1],
        sums_own[2],
        sums_own[3] * decay_power * jax.nn.sigmoid(-own_logits),
        grad_out.T,
        gains_own[slice_rows : 2 * slice_rows],
        feed_grads[:, :hidden_units].astype(f32),
        feed_grads[:, hidden_units : 2 * hidden_units].astype(f32),
        feed_grads[:, 2 * hidden_units :].T.astype(f32),
    )


def solution(mesh):
    in_specs = (
        P(("blk", "tok"), None),
        P("tok"),
        P("tok", "blk"),
        P("tok", "blk"),
        P(None, ("blk", "tok")),
        P(("blk", "tok")),
        P("blk", "tok", None),
        P(("blk", "tok")),
        P("blk", "tok", None),
        P(("blk", "tok")),
        P(("blk", "tok")),
        P("blk", "tok"),
        P("tok"),
        P("tok", "blk"),
        P("tok", "blk"),
        P("blk", "tok"),
        P(),
        P(("blk", "tok"), None),
    )
    out_specs = (
        P(("blk", "tok"), None),
        P(("blk", "tok"), None),
        P("tok"),
        P("tok", "blk"),
        P("tok", "blk"),
        P(None, ("blk", "tok")),
        P(("blk", "tok")),
        P("blk", "tok", None),
        P(("blk", "tok")),
        P("blk", "tok", None),
        P(("blk", "tok")),
        P(("blk", "tok")),
        P("blk", "tok"),
        P("tok"),
        P("tok", "blk"),
        P("tok", "blk"),
        P("blk", "tok"),
    )
    return jax.shard_map(
        per_device, mesh=mesh, in_specs=in_specs, out_specs=out_specs, check_vma=False
    )
```

```python
import functools

import jax
import jax.numpy as jnp
from jax import lax
from jax.experimental import pallas as pl
from jax.experimental.pallas import tpu as pltpu
from jax.sharding import PartitionSpec as P

CONV = 4
MEMBERS = 4
TOKS = 32
OWN = 128
HALO = 16
SMALL = 24
FIRST = 104

eps_norm = 1e-06
decay_power = 8.0
f32 = jnp.float32
bf16 = jnp.bfloat16


def hop_blk(values, distance):
    return lax.ppermute(
        values, "blk", [(i, (i + distance) % MEMBERS) for i in range(MEMBERS)]
    )


def hop_tok(values, axis, distance):
    route = []
    for y in range(4):
        for z in range(4):
            for c in range(2):
                if axis == "y":
                    to = ((y + distance) % 4, z, c)
                elif axis == "z":
                    to = (y, (z + distance) % 4, c)
                else:
                    to = (y, z, (c + distance) % 2)
                route.append((y * 8 + z * 2 + c, to[0] * 8 + to[1] * 2 + to[2]))
    return lax.ppermute(values, "tok", route)


def hop(values, axis, distance):
    if axis == "blk":
        return hop_blk(values, distance)
    return hop_tok(values, axis, distance)


def hop_apart(values, distance, axis="blk"):
    route = []
    for b in range(MEMBERS):
        for t in range(TOKS):
            step = distance if t % 2 == 0 else -distance
            place = {"blk": b, "y": t // 8, "z": t // 2 % 4}
            place[axis] = (place[axis] + step) % 4
            to = place["blk"] * TOKS + place["y"] * 8 + place["z"] * 2 + t % 2
            route.append((b * TOKS + t, to))
    return lax.ppermute(values, ("blk", "tok"), route)


def either(core, first, second):
    return jnp.where(core == 0, first, second)


def ring_gather(values, core, before_last=()):
    behind = hop_apart(values, 1)
    ahead = hop_apart(values, -1)
    far = hop_apart(after(behind, *before_last), 1)
    return [values, either(core, ahead, behind), far, either(core, behind, ahead)]


def ring_open(parts, core, axis="blk"):
    return hop_apart(parts[2].astype(bf16), 1, axis), ring_near(parts, core, axis)


def ring_near(parts, core, axis="blk"):
    return hop_apart(either(core, parts[3], parts[1]).astype(bf16), -1, axis)


def ring_pass(parts, far, core, axis="blk"):
    onward = either(core, parts[1], parts[3]).astype(f32) + far.astype(f32)
    return hop_apart(onward.astype(bf16), 1, axis)


def ring_close(parts, near, joined):
    return parts[0].astype(f32) + near.astype(f32) + joined.astype(f32)


def ring_scatter(parts, core, axis="blk"):
    far, near = ring_open(parts, core, axis)
    return ring_close(parts, near, ring_pass(parts, far, core, axis))


def direct_scatter(parts, axis):
    total = parts[0].astype(f32)
    for distance in range(1, 4):
        total = total + hop(parts[distance], axis, distance).astype(f32)
    return total


def narrow_sum(left, right):
    return (left.astype(f32) + right.astype(f32)).astype(bf16)


def after(value, *others):
    return lax.optimization_barrier((value,) + others)[0]


def hop_sum(values, axis):
    return values + hop(values, axis, 1) + hop(values, axis, -1) + hop(values, axis, 2)


def direct_gather(values, axis="blk"):
    return [values] + [hop(values, axis, -d) for d in range(1, 4)]


def turned(values, place, axis=0):
    return [
        lax.dynamic_index_in_dim(values, (place + j) % 4, axis, keepdims=False) for j in range(4)
    ]


def swap_sum(parts, core):
    mine = lax.dynamic_index_in_dim(parts, core, 1, keepdims=False)
    theirs = lax.dynamic_index_in_dim(parts, 1 - core, 1, keepdims=False)
    return narrow_sum(mine, hop(theirs, "core", 1))


def chip_sum(values, core):
    return swap_sum(values.reshape(16, 2, -1, values.shape[1]), core)


def chips_sum(values):
    cores = [[2 * i + c for i in range(16)] for c in range(2)]
    terms = lax.all_to_all(values, "tok", 0, 0, axis_index_groups=cores, tiled=True)
    return jnp.sum(terms.astype(f32), axis=0)


def together(*values):
    return lax.optimization_barrier(values)


def small_gather(values, before_last):
    values = jnp.stack([values, hop(values, "core", 1)])
    values = jnp.stack(direct_gather(values, "z"))
    return jnp.stack(direct_gather(after(values, *before_last), "y"))


def product(operand, weight, out=f32):
    return jnp.dot(operand, weight, preferred_element_type=f32).astype(out)


def product_back(operand, weight, out=f32):
    return lax.dot_general(
        operand, weight, (((1,), (1,)), ((), ())), preferred_element_type=f32
    ).astype(out)


def product_outer(operand, weight, out=bf16):
    return lax.dot_general(
        operand, weight, (((0,), (0,)), ((), ())), preferred_element_type=f32
    ).astype(out)


def norm_factor(values):
    return lax.rsqrt(jnp.mean(values * values, axis=1, keepdims=True) + eps_norm)


def normalize_back(gradient, values, factor, gains):
    weighted = gradient * gains
    return factor * weighted - values * (factor * factor * factor) * jnp.mean(
        weighted * values, axis=1, keepdims=True
    )


def sigmoid(values):
    return 1.0 / (1.0 + jnp.exp(-values))


def one_minus_exp(values):
    series = 1.0 + values * (1.0 / 6.0)
    for order in (5.0, 4.0, 3.0, 2.0):
        series = 1.0 + values * series * (1.0 / order)
    return jnp.where(values > -0.1, -values * series, 1.0 - jnp.exp(values))


def inverse_root(values):
    return lax.rsqrt(jnp.maximum(values, 1e-37))


def gelu_parts(values):
    root = 0.7978845608028654
    square = values * values
    bent = jnp.tanh(root * values * (1.0 + 0.044715 * square))
    half = 0.5 * (1.0 + bent)
    slope = half + 0.5 * values * (1.0 - bent * bent) * root * (1.0 + 3.0 * 0.044715 * square)
    return values * half, slope


def rows_at(start, size):
    return pl.ds(pl.multiple_of(start, size), size)


def conv_rows(ci_ref, halo_ref, tile):
    before = halo_ref[...] if tile == 0 else ci_ref[(tile - 1) * HALO : tile * HALO, :]
    here = ci_ref[tile * HALO : (tile + 1) * HALO, :]
    return jnp.concatenate([before.astype(f32), here.astype(f32)], axis=0)


def local_forward_kernel(
    taps_ref,
    shift_ref,
    blocks_ref,
    bias_ref,
    soft_ref,
    ci_ref,
    halo_ref,
    place_ref,
    conv_ref,
    rate_ref,
    entry_ref,
    local_ref,
    cum_ref,
    edge_ref,
    gates_ref,
    pre_ref,
    high_ref,
):
    slot = pl.program_id(0)
    channels = conv_ref.shape[1]
    block = blocks_ref.shape[0]
    width = 2 * channels

    @pl.when(slot == 0)
    def spread_gates():
        columns = lax.broadcasted_iota(jnp.int32, (HALO, width), 1)
        columns = jnp.where(columns >= channels, columns - channels, columns)
        for group in range(channels // block):
            inside = (columns >= group * block) & (columns < (group + 1) * block)
            for step in range(0, block, HALO):
                rows = blocks_ref[step : step + HALO, :].astype(f32)
                at = group * block + step
                gates_ref[at : at + HALO, :] = jnp.where(inside, rows, 0.0).astype(bf16)

    for tile in range(OWN // HALO):
        at = slice(tile * HALO, (tile + 1) * HALO)
        rows = conv_rows(ci_ref, halo_ref, tile)
        places = place_ref[at, :]
        total = shift_ref[...] + taps_ref[0:1, :] * rows[HALO:]
        for tap in range(1, CONV):
            lagged = pltpu.roll(rows, tap, 0)[HALO:]
            total = total + taps_ref[tap : tap + 1, :] * jnp.where(places >= tap, lagged, 0.0)
        conv_ref[at, :] = total
        high_ref[at, :] = total.astype(bf16)
    for step in range(0, width, 256):
        columns = slice(step, step + 256)
        pre_ref[:, columns] = (
            jnp.dot(high_ref[...], gates_ref[:, columns], preferred_element_type=f32)
            + bias_ref[:, columns]
        )

    row_ids = lax.broadcasted_iota(jnp.int32, (8, channels), 0)

    def scan(tile, carry):
        rows = rows_at(tile * 8, 8)
        rates = sigmoid(pre_ref[rows, :channels])
        entries = 0.5 * jnp.tanh(0.5 * pre_ref[rows, channels:]) + 0.5
        log_keep = -soft_ref[...] * rates
        resets = place_ref[rows, :] == 0
        coeff = jnp.where(resets, 0.0, jnp.exp(log_keep))
        squared = one_minus_exp(2.0 * log_keep)
        scaling = jnp.where(resets, 1.0, squared * inverse_root(squared))
        value = entries * conv_ref[rows, :] * scaling
        for distance in (1, 2, 4):
            reach = row_ids >= distance
            value = value + coeff * jnp.where(reach, pltpu.roll(value, distance, 0), 0.0)
            coeff = coeff * jnp.where(reach, pltpu.roll(coeff, distance, 0), 1.0)
        value = value + coeff * carry[1]
        coeff = coeff * carry[0]
        rate_ref[rows, :] = rates
        entry_ref[rows, :] = entries
        local_ref[rows, :] = value
        cum_ref[rows, :] = coeff
        return coeff[7:8], value[7:8]

    start = (jnp.ones((1, channels), f32), jnp.zeros((1, channels), f32))
    coeff, value = lax.fori_loop(0, OWN // 8, scan, start, unroll=4)
    edge_ref[pl.ds(slot, 1), :] = coeff
    edge_ref[pl.ds(slot + MEMBERS, 1), :] = value


def extended(pair, block):
    return pair[0] * block[:4], block[:4] * pair[1] + block[4:]


def whole_chain(channels):
    return jnp.ones((4, channels), f32), jnp.zeros((4, channels), f32)


def fold_near_kernel(backward, spot_ref, *refs):
    pieces, (total_ref, prefix_ref, held_ref) = refs[:4], refs[4:]
    z, c = spot_ref[2], spot_ref[3]
    for distance, piece in enumerate(pieces):
        held_ref[distance] = piece[...]
    chain = whole_chain(total_ref.shape[1])
    prefix = chain
    for place in reversed(range(8)) if backward else range(8):
        here = place == 2 * z + c
        prefix = tuple(jnp.where(here, new, old) for new, old in zip(chain, prefix))
        distance = jnp.bitwise_and(place // 2 - z + 4, 3)
        chain = extended(chain, held_ref[distance, jnp.bitwise_xor(place % 2, c)])
    total_ref[...] = jnp.concatenate(chain, axis=0)
    prefix_ref[...] = jnp.concatenate(prefix, axis=0)


def slot_carries(backward, spot_ref, pieces, prefix_ref, held_ref):
    y = spot_ref[1]
    channels = prefix_ref.shape[1]
    for distance, piece in enumerate(pieces):
        held_ref[distance] = piece[...]
    total = whole_chain(channels)
    prefix = total
    for place in reversed(range(4)) if backward else range(4):
        here = place == y
        prefix = tuple(jnp.where(here, new, old) for new, old in zip(total, prefix))
        total = extended(total, held_ref[jnp.bitwise_and(place - y + 4, 3)])
    prefix = extended(prefix, prefix_ref[...])
    current = jnp.zeros((1, channels), f32)
    carries = [None] * MEMBERS
    for _ in range(2):
        for slot in reversed(range(MEMBERS)) if backward else range(MEMBERS):
            one = slice(slot, slot + 1)
            carries[slot] = prefix[0][one] * current + prefix[1][one]
            current = total[0][one] * current + total[1][one]
    return carries


def mix_kernel(
    spot_ref,
    piece0,
    piece1,
    piece2,
    piece3,
    prefix_ref,
    local_ref,
    cum_ref,
    branch_ref,
    state_ref,
    mixed_ref,
    carry_ref,
    held_ref,
):
    slot = pl.program_id(0)

    @pl.when(slot == 0)
    def begin():
        pieces = (piece0, piece1, piece2, piece3)
        carries = slot_carries(False, spot_ref, pieces, prefix_ref, held_ref)
        carry_ref[...] = jnp.concatenate(carries, axis=0)

    carry = carry_ref[pl.ds(slot, 1), :]

    def apply(tile, token):
        rows = rows_at(tile * HALO, HALO)
        states = local_ref[rows, :] + cum_ref[rows, :] * carry
        state_ref[rows, :] = states
        mixed_ref[rows, :] = (states * gelu_parts(branch_ref[rows, :])[0]).astype(bf16)
        return token

    lax.fori_loop(0, OWN // HALO, apply, 0, unroll=2)


def reverse_scan(rows, later, gated, grad_ref, rate_ref, place_ref, soft_ref, row_ids):
    sgrad = grad_ref[rows, :] * gated
    keeps = jnp.exp(-soft_ref[...] * rate_ref[rows, :])
    coeff = jnp.where(place_ref[rows, :] == 0, 0.0, keeps)
    value = coeff * sgrad
    for distance in (1, 2, 4):
        reach = row_ids < 8 - distance
        value = value + coeff * jnp.where(reach, pltpu.roll(value, 8 - distance, 0), 0.0)
        coeff = coeff * jnp.where(reach, pltpu.roll(coeff, 8 - distance, 0), 1.0)
    return value + coeff * later, sgrad, coeff


def local_backward_kernel(
    soft_ref,
    grad_ref,
    branch_ref,
    state_ref,
    rate_ref,
    place_ref,
    bgrad_ref,
    edge_ref,
):
    slot = pl.program_id(0)
    channels = grad_ref.shape[1]
    row_ids = lax.broadcasted_iota(jnp.int32, (8, channels), 0)

    def scan(step, carry):
        base = OWN - HALO - step * HALO
        cum, later = carry
        slopes = []
        for part in (1, 0):
            rows = rows_at(base + 8 * part, 8)
            gated, slope = gelu_parts(branch_ref[rows, :])
            slopes.append(slope * grad_ref[rows, :] * state_ref[rows, :])
            held, _, coeff = reverse_scan(
                rows, later, gated, grad_ref, rate_ref, place_ref, soft_ref, row_ids
            )
            cum, later = coeff[0:1] * cum, held[0:1]
        bgrad_ref[rows_at(base, HALO), :] = jnp.concatenate(slopes[::-1], axis=0).astype(bf16)
        return cum, later

    start = (jnp.ones((1, channels), f32), jnp.zeros((1, channels), f32))
    coeff, value = lax.fori_loop(0, OWN // HALO, scan, start, unroll=2)
    edge_ref[pl.ds(slot, 1), :] = coeff
    edge_ref[pl.ds(slot + MEMBERS, 1), :] = value


def finish_backward_kernel(
    spot_ref,
    piece0,
    piece1,
    piece2,
    piece3,
    prefix_ref,
    carry_ref,
    soft_ref,
    taps_ref,
    gates_ref,
    grad_ref,
    branch_ref,
    state_ref,
    conv_ref,
    rate_ref,
    entry_ref,
    place_ref,
    ci_ref,
    halo_ref,
    pregrad_ref,
    igrad_ref,
    owed_ref,
    sums_ref,
    cgrad_ref,
    back_ref,
    held_ref,
):
    slot = pl.program_id(0)
    channels = conv_ref.shape[1]

    @pl.when(slot == 0)
    def begin():
        pieces = (piece0, piece1, piece2, piece3)
        carries = slot_carries(True, spot_ref, pieces, prefix_ref, held_ref)
        back_ref[...] = jnp.concatenate(carries, axis=0)
        sums_ref[...] = jnp.zeros_like(sums_ref)

    row_ids = lax.broadcasted_iota(jnp.int32, (8, channels), 0)
    back = back_ref[pl.ds(slot, 1), :]
    ahead_first = carry_ref[pl.ds(slot, 1), :]

    def gate_grads(step, carry):
        later, logit_sum, rate_sum, entry_sum = carry
        base = OWN - HALO - step * HALO
        low_rate, low_entry = [], []
        for part in (1, 0):
            first = base + 8 * part
            rows = rows_at(first, 8)
            gated, _ = gelu_parts(branch_ref[rows, :])
            held, sgrad, _ = reverse_scan(
                rows, later, gated, grad_ref, rate_ref, place_ref, soft_ref, row_ids
            )
            adjoint = sgrad + jnp.where(row_ids == 7, later, pltpu.roll(held, 7, 0))
            later = held[0:1]
            ahead = state_ref[rows_at(jnp.maximum(first - 8, 0), 8), :][7:8]
            ahead = jnp.where(first == 0, ahead_first, ahead)
            previous = jnp.where(row_ids == 0, ahead, pltpu.roll(state_ref[rows, :], 1, 0))
            rates, entries, conv = rate_ref[rows, :], entry_ref[rows, :], conv_ref[rows, :]
            resets = place_ref[rows, :] == 0
            log_keep = -soft_ref[...] * rates
            squared = one_minus_exp(2.0 * log_keep)
            inverse = inverse_root(squared)
            scaling = jnp.where(resets, 1.0, squared * inverse)
            turn = jnp.where(resets, 0.0, (1.0 - squared) * inverse)
            weighed = adjoint * entries
            log_grad = held * previous - weighed * conv * turn
            rate_part = log_grad * rates
            logit_sum = logit_sum + rate_part
            rate_grad = -soft_ref[...] * rate_part * (1.0 - rates)
            direct = weighed * scaling
            entry_grad = direct * conv * (1.0 - entries)
            rate_sum = rate_sum + rate_grad
            entry_sum = entry_sum + entry_grad
            cgrad_ref[rows, :] = direct
            low_rate.append(rate_grad)
            low_entry.append(entry_grad)
        rows = rows_at(base, HALO)
        pregrad_ref[rows, :channels] = jnp.concatenate(low_rate[::-1], axis=0).astype(bf16)
        pregrad_ref[rows, channels:] = jnp.concatenate(low_entry[::-1], axis=0).astype(bf16)
        return later, logit_sum, rate_sum, entry_sum

    zero = jnp.zeros((8, channels), f32)
    _, logit_sum, rate_sum, entry_sum = lax.fori_loop(
        0, OWN // HALO, gate_grads, (back, zero, zero, zero), unroll=2
    )
    for step in range(0, channels, 128):
        columns = slice(step, step + 128)
        cgrad_ref[:, columns] += lax.dot_general(
            pregrad_ref[...],
            gates_ref[columns, :],
            (((1,), (1,)), ((), ())),
            preferred_element_type=f32,
        )

    def spread(tile):
        at = slice(tile * HALO, (tile + 1) * HALO)
        rows, places = cgrad_ref[at, :], place_ref[at, :]
        return [rows] + [jnp.where(places >= tap, rows, 0.0) for tap in range(1, CONV)]

    def shifted_sum(current, following):
        total = taps_ref[0:1, :] * current[0]
        for tap in range(1, CONV):
            both = jnp.concatenate([current[tap], following[tap]], axis=0)
            total = total + taps_ref[tap : tap + 1, :] * pltpu.roll(both, 2 * HALO - tap, 0)[:HALO]
        return total

    nothing = [jnp.zeros((HALO, channels), f32)] * CONV
    shift_sum, tap_sums = nothing[0], list(nothing)
    tiles = OWN // HALO
    coming = spread(0)
    owed_ref[...] = shifted_sum(nothing, coming)
    for tile in range(tiles):
        grads, coming = coming, spread(tile + 1) if tile + 1 < tiles else nothing
        igrad_ref[tile * HALO : (tile + 1) * HALO, :] = shifted_sum(grads, coming)
        inputs = conv_rows(ci_ref, halo_ref, tile)
        shift_sum = shift_sum + grads[0]
        tap_sums[0] = tap_sums[0] + grads[0] * inputs[HALO:]
        for tap in range(1, CONV):
            tap_sums[tap] = tap_sums[tap] + grads[tap] * pltpu.roll(inputs, tap, 0)[HALO:]

    def total_rows(values):
        return jnp.sum(values, axis=0, keepdims=True)

    sums_ref[...] += jnp.concatenate(
        [total_rows(v) for v in [shift_sum, rate_sum, entry_sum, logit_sum] + tap_sums], axis=0
    )


def in_hbm(values):
    return pltpu.with_memory_space_constraint(values, pltpu.HBM)


def by_slot(kernel, outs, ins, scratch, scalars, moved, far_outs=None):
    whole = [pl.BlockSpec(a.shape, lambda i, n=a.ndim: (0,) * n) for a in ins if not isinstance(a, tuple)]
    parts = [
        pl.BlockSpec((rows, a.shape[1]), lambda i, first=first: (first + i, 0))
        for a, rows, first in (a for a in ins if isinstance(a, tuple))
    ]
    out_specs = [
        pl.BlockSpec(shape, lambda i: (0, 0))
        if rows is None
        else pl.BlockSpec((rows, shape[1]), lambda i: (i, 0))
        for rows, shape, _ in outs
    ]
    return pl.pallas_call(
        kernel,
        grid=(MEMBERS,),
        in_specs=[pl.BlockSpec(memory_space=pltpu.SMEM)] * len(scalars) + whole + parts,
        out_specs=out_specs,
        out_shape=[
            pltpu.HBM(shape, dtype) if far else jax.ShapeDtypeStruct(shape, dtype)
            for (_, shape, dtype), far in zip(outs, far_outs or [False] * len(outs))
        ],
        scratch_shapes=[pltpu.VMEM(shape, dtype) for shape, dtype in scratch],
        compiler_params=pltpu.CompilerParams(vmem_limit_bytes=16 * 1024 * 1024),
        cost_estimate=pl.CostEstimate(flops=0, bytes_accessed=moved, transcendentals=0),
    )(*scalars, *[a[0] if isinstance(a, tuple) else a for a in ins])


def in_vmem(kernel, outs, scratch=(), scalars=0, count=1, moved=0):
    vmem = pl.BlockSpec(memory_space=pltpu.VMEM)
    smem = pl.BlockSpec(memory_space=pltpu.SMEM)
    return pl.pallas_call(
        kernel,
        out_shape=[jax.ShapeDtypeStruct(shape, dtype) for shape, dtype in outs],
        in_specs=[smem] * scalars + [vmem] * count,
        out_specs=[vmem] * len(outs),
        scratch_shapes=[pltpu.VMEM(shape, dtype) for shape, dtype in scratch],
        compiler_params=pltpu.CompilerParams(vmem_limit_bytes=16 * 1024 * 1024),
        cost_estimate=pl.CostEstimate(flops=0, bytes_accessed=moved, transcendentals=0),
    )


def exchange_edges(edges, spots, backward):
    channels = edges.shape[1]
    near = jnp.stack([edges, hop(edges, "core", 1)])
    total, prefix = in_vmem(
        functools.partial(fold_near_kernel, backward),
        [((8, channels), f32)] * 2,
        [((4, 2, 8, channels), f32)],
        scalars=1,
        count=4,
        moved=3_000_000,
    )(spots, *direct_gather(near, "z"))
    return direct_gather(total, "y") + [prefix], near


def outer_kernel(lhs_one, lhs_two, rhs_one, rhs_two, rhs_three, out_ref):
    def settle(lhs, rhs):
        out_ref[...] = lax.dot_general(
            lhs[...], rhs[...], (((0,), (0,)), ((), ())), preferred_element_type=f32
        ).astype(bf16)

    for step, (lhs, rhs) in enumerate(
        ((lhs_one, rhs_one), (lhs_one, rhs_two), (lhs_two, rhs_three))
    ):
        pl.when(pl.program_id(0) == step)(functools.partial(settle, lhs, rhs))


def feed_outer(lhs_one, lhs_two, rhs):
    rows, features = lhs_one.shape
    columns = rhs[0].shape[1]
    height = 1024
    whole = pl.BlockSpec((rows, columns), lambda j, i: (0, 0))
    return pl.pallas_call(
        outer_kernel,
        grid=(3, features // height),
        in_specs=[
            pl.BlockSpec((rows, height), lambda j, i: (0, jnp.where(j < 2, i, 0))),
            pl.BlockSpec((rows, height), lambda j, i: (0, jnp.where(j < 2, 0, i))),
            whole,
            whole,
            whole,
        ],
        out_specs=pl.BlockSpec((height, columns), lambda j, i: (i, j)),
        out_shape=jax.ShapeDtypeStruct((features, 3 * columns), bf16),
        compiler_params=pltpu.CompilerParams(vmem_limit_bytes=32 * 1024 * 1024),
        cost_estimate=pl.CostEstimate(
            flops=6 * rows * features * columns,
            bytes_accessed=6 * features * columns,
            transcendentals=0,
        ),
    )(lhs_one, lhs_two, *rhs)


def small_kernel(cut, conv_ref, pregrad_ref, sums_ref, extra_ref, out_ref):
    channels = conv_ref.shape[1]
    width = 2 * channels
    block = cut * TOKS
    dense = lax.dot_general(
        conv_ref[...].astype(bf16),
        pregrad_ref[...],
        (((0,), (0,)), ((), ())),
        preferred_element_type=f32,
    )
    columns = lax.broadcasted_iota(jnp.int32, (block, width), 1)
    columns = jnp.where(columns >= channels, columns - channels, columns)
    gates = jnp.zeros((block, width), f32)
    for group in range(channels // block):
        inside = (columns >= group * block) & (columns < (group + 1) * block)
        gates = jnp.where(inside, dense[group * block : (group + 1) * block], gates)
    spare = jnp.zeros((SMALL - 2 * cut - 9, channels), f32)
    for tok in range(TOKS):
        rows = gates[tok * cut : (tok + 1) * cut]
        pieces = [rows[:, :channels], rows[:, channels:], sums_ref[...]]
        pieces += [extra_ref[tok : tok + 1, :], spare]
        out_ref[tok] = jnp.concatenate(pieces, axis=0).astype(bf16)


def halves_kernel(count, small, spot_ref, *refs):
    core = spot_ref[3]
    small_ref, refs = (refs[0], refs[1:]) if small else (None, refs)
    mine_ref, theirs_ref = refs[2 * count :]
    chips, rows, _ = mine_ref.shape
    rows = (rows - small) // count
    for which in range(count):
        sums = lax.dot_general(
            refs[which][...],
            refs[count + which][...],
            (((0,), (0,)), ((), ())),
            preferred_element_type=f32,
        )
        for chip in range(chips):
            low = sums[2 * chip * rows : (2 * chip + 1) * rows]
            high = sums[(2 * chip + 1) * rows : (2 * chip + 2) * rows]
            at = slice(which * rows, (which + 1) * rows)
            mine_ref[chip, at, :] = jnp.where(core == 0, low, high).astype(bf16)
            theirs_ref[chip, at, :] = jnp.where(core == 0, high, low).astype(bf16)
    for chip in range(chips if small else 0):
        low, high = small_ref[2 * chip].astype(f32), small_ref[2 * chip + 1].astype(f32)
        at = slice(count * rows, count * rows + small)
        mine_ref[chip, at, :] = jnp.where(core == 0, low, high).astype(bf16)
        theirs_ref[chip, at, :] = jnp.where(core == 0, high, low).astype(bf16)


def outer_halves(spots, small, lhs, rhs):
    count = len(lhs)
    features = lhs[0].shape[1]
    rows, columns = rhs[0].shape
    height = 1024
    chips = height // 128
    extra = SMALL if small is not None else 0
    total = 64 * count + extra
    shape = jax.ShapeDtypeStruct((features // 128, total, columns), bf16)
    out_spec = pl.BlockSpec((chips, total, columns), lambda i: (i, 0, 0))
    return pl.pallas_call(
        functools.partial(halves_kernel, count, extra),
        grid=(features // height,),
        in_specs=[pl.BlockSpec(memory_space=pltpu.SMEM)]
        + [pl.BlockSpec((2 * chips, SMALL, columns), lambda i: (i, 0, 0))] * (extra > 0)
        + [pl.BlockSpec((rows, height), lambda i: (0, i))] * count
        + [pl.BlockSpec((rows, columns), lambda i: (0, 0))] * count,
        out_specs=[out_spec] * 2,
        out_shape=[shape] * 2,
        compiler_params=pltpu.CompilerParams(vmem_limit_bytes=28 * 1024 * 1024),
        cost_estimate=pl.CostEstimate(
            flops=2 * count * rows * features * columns,
            bytes_accessed=0,
            transcendentals=0,
        ),
    )(spots, *([small] if extra else []), *lhs, *rhs)


def per_device(
    inputs,
    mix_scale,
    branch_mat,
    input_mat,
    conv_taps,
    conv_shift,
    rate_mat,
    rate_shift,
    entry_mat,
    entry_shift,
    decay_logit,
    out_mat,
    feed_scale,
    gate_mat,
    up_mat,
    down_mat,
    lengths,
    cotangent,
):
    blk = lax.axis_index("blk")
    tok = lax.axis_index("tok")
    spot = (tok // 8, (tok // 2) % 4, tok % 2)
    spots = jnp.stack([tok] + list(spot)).astype(jnp.int32)
    channels = branch_mat.shape[1]
    hidden_units = gate_mat.shape[1]
    slice_rows = branch_mat.shape[0]
    total_rows = MEMBERS * OWN

    groups, cut, block = rate_mat.shape
    own_channels = conv_shift.shape[0]
    vectors = [conv_taps, conv_shift[None], rate_shift[None], entry_shift[None], decay_logit[None]]
    vectors = jnp.concatenate(vectors, axis=0).reshape(-1)
    extras = jnp.concatenate([vectors, mix_scale, feed_scale])
    extras = jnp.pad(extras, (0, channels - extras.shape[0]))[None]
    smalls = [jnp.moveaxis(mats, 0, 1).reshape(cut, channels) for mats in (rate_mat, entry_mat)]
    smalls = jnp.concatenate(smalls + [extras], axis=0)
    smalls = jnp.pad(smalls, ((0, HALO - smalls.shape[0]), (0, 0)))
    input_blocks = ring_gather(inputs, spot[2])
    near = after(small_gather(smalls, (input_blocks[1], input_blocks[3])), input_blocks[2])
    for axis, place in ((2, spot[2]), (1, spot[1]), (0, spot[0])):
        near = jnp.roll(near, place, axis)
    near = near.reshape(TOKS, HALO, channels)
    mixer_all = lax.all_gather(
        jnp.concatenate([input_mat, branch_mat, out_mat.T], axis=1), "tok", axis=0, tiled=True
    )
    devices = MEMBERS * TOKS
    tail = lax.ppermute(
        inputs[OWN - HALO :], ("blk", "tok"), [(i, (i + 1) % devices) for i in range(devices)]
    )
    cotangent_blocks = ring_gather(after(cotangent, input_blocks[2]), spot[2])
    rows_all = jnp.concatenate(input_blocks + direct_gather(tail), axis=0)
    cotangent_all = jnp.concatenate(cotangent_blocks, axis=0)

    extras = near[:, 2 * cut]
    vectors = extras[:, : 8 * own_channels].reshape(TOKS, 8, own_channels).astype(f32)
    vectors = jnp.moveaxis(vectors, 0, 1).reshape(8, channels)
    gains = extras[:, 8 * own_channels : 8 * own_channels + 2 * slice_rows].astype(f32)
    mix_gain = gains[:, :slice_rows].reshape(1, -1)
    feed_gain = gains[:, slice_rows:].reshape(1, -1)
    wide_values = rows_all.astype(f32)
    wide_one = (wide_values * norm_factor(wide_values) * mix_gain).astype(bf16)
    taps, shift = vectors[:CONV], vectors[4:5]
    bias = jnp.concatenate([vectors[5:6], vectors[6:7]], axis=1)
    soft = decay_power * jax.nn.softplus(-vectors[7:8])
    blocks = [near[:, i * cut : (i + 1) * cut].reshape(block, channels) for i in range(2)]
    blocks = after(jnp.concatenate(blocks, axis=1), cotangent_blocks[2])
    feed_own = jnp.concatenate([gate_mat, up_mat, down_mat.T], axis=1)
    feed_all = lax.all_gather(after(feed_own, wide_one, blocks), "tok", axis=0, tiled=True)
    gate_up_all = feed_all[:, : 2 * hidden_units]
    down_turned = feed_all[:, 2 * hidden_units :]
    own_one = wide_one[:total_rows]
    input_all = mixer_all[:, :channels]
    branch_all = mixer_all[:, channels : 2 * channels]
    project_all = mixer_all[:, : 2 * channels]
    out_turned = mixer_all[:, 2 * channels : 3 * channels]

    slots = (blk + jnp.arange(MEMBERS, dtype=jnp.int32)) % MEMBERS
    token_ids = (
        (slots * TOKS + tok)[:, None] * OWN + jnp.arange(OWN, dtype=jnp.int32)[None, :]
    ).reshape(-1)
    starts = jnp.cumsum(lengths) - lengths
    opened = jnp.max(jnp.where(starts[None, :] <= token_ids[:, None], starts[None, :], 0), axis=1)
    places = (token_ids - opened).reshape(total_rows, 1).astype(jnp.int32)

    conv_input = product(wide_one, input_all, bf16)
    branch = product(own_one, branch_all)
    halo_first = total_rows // HALO
    conv, rates, entries, local, cum, edges, gates = by_slot(
        local_forward_kernel,
        [(OWN, (total_rows, channels), f32)] * 5
        + [(None, (8, channels), f32), (None, (channels, 2 * channels), bf16)],
        [
            taps,
            shift,
            blocks,
            bias,
            soft,
            (conv_input, OWN, 0),
            (conv_input, HALO, halo_first),
            (places, OWN, 0),
        ],
        [((OWN, 2 * channels), f32), ((OWN, channels), bf16)],
        (),
        30_000_000,
        [True, True, True, False, False, False, True],
    )
    conv, rates, entries, gates = [in_hbm(a) for a in (conv, rates, entries, gates)]
    chains, _ = exchange_edges(edges, spots, False)
    states, mixture, carried = by_slot(
        mix_kernel,
        [
            (OWN, (total_rows, channels), f32),
            (OWN, (total_rows, channels), bf16),
            (None, (MEMBERS, channels), f32),
        ],
        [*chains] + [(a, OWN, 0) for a in (local, cum, branch)],
        [((4, 8, channels), f32)],
        (spots,),
        4_500_000,
    )

    def rows_of(values):
        return [values[j * OWN : (j + 1) * OWN] for j in range(MEMBERS)]

    own_values = inputs.astype(f32)
    middle = own_values + ring_scatter(rows_of(product_back(mixture, out_turned)), spot[2])

    factor_two = norm_factor(middle)
    normed_two = (middle * factor_two * feed_gain).astype(bf16)
    hidden_grad = product(after(cotangent_all, mixture), down_turned)
    blocks_two = ring_gather(normed_two, spot[2], (feed_all,))
    blocks_two[2] = after(blocks_two[2], hidden_grad)
    wide_two = jnp.concatenate(blocks_two, axis=0)
    gate_up = product(wide_two, gate_up_all)
    gate_pre, up_pre = gate_up[:, :hidden_units], gate_up[:, hidden_units:]
    gate_act, gate_slope = gelu_parts(gate_pre)
    hidden = (gate_act * up_pre).astype(bf16)
    gate_grad = (gate_slope * hidden_grad * up_pre).astype(bf16)
    up_grad = (gate_act * hidden_grad).astype(bf16)
    feed_shares = feed_outer(wide_two, cotangent_all, (gate_grad, up_grad, hidden))
    feed_grads = lax.psum_scatter(feed_shares, "tok", scatter_dimension=0, tiled=True)
    gate_late, up_late = after((gate_grad, up_grad), feed_shares)
    two_shares = product_back(jnp.concatenate([gate_late, up_late], axis=1), gate_up_all)
    two_parts = rows_of(two_shares)
    two_far, two_near = ring_open(two_parts, spot[2])
    two_grad = ring_close(two_parts, two_near, ring_pass(two_parts, two_far, spot[2]))
    middle_grad = cotangent.astype(f32) + normalize_back(two_grad, middle, factor_two, feed_gain)
    grad_feed_scale = jnp.sum(two_grad * middle * factor_two, axis=0)
    layer_shares = product_back(after(hidden, two_far), down_turned, bf16)
    middle_blocks = ring_gather(middle_grad.astype(bf16), spot[2])
    middle_blocks[2] = after(middle_blocks[2], layer_shares)
    middle_wide = jnp.concatenate(middle_blocks, axis=0)
    mixture_grad = product(middle_wide, out_turned)
    branch = in_hbm(branch)
    branch_grad, back_edges = by_slot(
        local_backward_kernel,
        [(OWN, (total_rows, channels), bf16), (None, (8, channels), f32)],
        [soft] + [(a, OWN, 0) for a in (mixture_grad, branch, states, rates, places)],
        (),
        (),
        9_500_000,
    )
    chains_back, near_back = exchange_edges(back_edges, spots, True)
    pregrads, igrad, owed, sums = by_slot(
        finish_backward_kernel,
        [
            (OWN, (total_rows, 2 * channels), bf16),
            (OWN, (total_rows, channels), f32),
            (HALO, (MEMBERS * HALO, channels), f32),
            (None, (8, channels), f32),
        ],
        [*chains_back, carried, soft, taps, gates]
        + [(a, OWN, 0) for a in (mixture_grad, branch, states, conv, rates, entries)]
        + [(places, OWN, 0), (conv_input, OWN, 0), (conv_input, HALO, halo_first)],
        [
            ((OWN, channels), f32),
            ((MEMBERS, channels), f32),
            ((4, 8, channels), f32),
        ],
        (spots,),
        40_000_000,
    )
    returned = lax.ppermute(
        owed.reshape(MEMBERS, HALO, channels)[:, HALO - 3 :],
        "tok",
        [(i, (i - 1) % TOKS) for i in range(TOKS)],
    )
    turned_on = jnp.concatenate([returned[1:], returned[:1]], axis=0)
    landing = jnp.where(tok == TOKS - 1, turned_on, returned)
    input_grad = igrad.reshape(MEMBERS, OWN, channels) + jnp.pad(
        landing, ((0, 0), (OWN - 3, 0), (0, 0))
    )
    input_low = input_grad.reshape(total_rows, channels).astype(bf16)
    feed_rows = jnp.pad(
        grad_feed_scale.reshape(TOKS, slice_rows), ((0, 0), (0, channels - slice_rows))
    )
    (small_rows,) = in_vmem(
        functools.partial(small_kernel, cut),
        [((TOKS, SMALL, channels), bf16)],
        count=4,
        moved=11_000_000,
    )(conv, pregrads, sums, feed_rows)

    core = spot[2]
    weight_mine, weight_theirs = outer_halves(
        spots, small_rows, (middle_wide, wide_one, wide_one), (mixture, branch_grad, input_low)
    )
    weight_other = hop(weight_theirs, "core", 1)
    late = after(input_low, weight_theirs)
    one_shares = product_back(jnp.concatenate([late, branch_grad], axis=1), project_all, bf16)
    weight_chip = narrow_sum(weight_mine, weight_other)
    one_shares = after(one_shares, weight_chip)
    one_parts = rows_of(one_shares)
    one_grad = ring_scatter(one_parts, core)
    factor_one = norm_factor(own_values)
    first_grad = normalize_back(one_grad, own_values, factor_one, mix_gain)
    inputs_grad = (middle_grad + first_grad).astype(bf16)
    settled = chips_sum(weight_chip)
    layer_out = middle + ring_scatter(rows_of(after(layer_shares, one_grad)), core)
    grad_out, grad_branch, grad_input = [
        settled[i * slice_rows : (i + 1) * slice_rows] for i in range(3)
    ]
    settled = settled[3 * slice_rows :]
    grad_mix_scale = jnp.sum(
        grad_branch * branch_mat.astype(f32) + grad_input * input_mat.astype(f32), axis=1
    ) / mix_scale.astype(f32)
    gains_own = jnp.concatenate([grad_mix_scale, settled[2 * cut + 8, :slice_rows]])
    gains_own = hop_sum(gains_own.reshape(1, -1), "blk")[0]
    gate_own = [
        jnp.moveaxis(settled[i * cut : (i + 1) * cut].reshape(cut, groups, block), 1, 0)
        for i in range(2)
    ]
    sums_own = lax.dynamic_slice(
        settled[2 * cut : 2 * cut + 8], (0, tok * own_channels), (8, own_channels)
    )
    own_logits = decay_logit.astype(f32)
    return (
        layer_out.astype(bf16),
        inputs_grad,
        gains_own[:slice_rows],
        grad_branch,
        grad_input,
        sums_own[4:],
        sums_own[0],
        gate_own[0],
        sums_own[1],
        gate_own[1],
        sums_own[2],
        sums_own[3] * decay_power * jax.nn.sigmoid(-own_logits),
        grad_out.T,
        gains_own[slice_rows : 2 * slice_rows],
        feed_grads[:, :hidden_units].astype(f32),
        feed_grads[:, hidden_units : 2 * hidden_units].astype(f32),
        feed_grads[:, 2 * hidden_units :].T.astype(f32),
    )


def solution(mesh):
    in_specs = (
        P(("blk", "tok"), None),
        P("tok"),
        P("tok", "blk"),
        P("tok", "blk"),
        P(None, ("blk", "tok")),
        P(("blk", "tok")),
        P("blk", "tok", None),
        P(("blk", "tok")),
        P("blk", "tok", None),
        P(("blk", "tok")),
        P(("blk", "tok")),
        P("blk", "tok"),
        P("tok"),
        P("tok", "blk"),
        P("tok", "blk"),
        P("blk", "tok"),
        P(),
        P(("blk", "tok"), None),
    )
    out_specs = (
        P(("blk", "tok"), None),
        P(("blk", "tok"), None),
        P("tok"),
        P("tok", "blk"),
        P("tok", "blk"),
        P(None, ("blk", "tok")),
        P(("blk", "tok")),
        P("blk", "tok", None),
        P(("blk", "tok")),
        P("blk", "tok", None),
        P(("blk", "tok")),
        P(("blk", "tok")),
        P("blk", "tok"),
        P("tok"),
        P("tok", "blk"),
        P("tok", "blk"),
        P("blk", "tok"),
    )
    return jax.shard_map(
        per_device, mesh=mesh, in_specs=in_specs, out_specs=out_specs, check_vma=False
    )
```

```python
import functools

import jax
import jax.numpy as jnp
from jax import lax
from jax.experimental import pallas as pl
from jax.experimental.pallas import tpu as pltpu
from jax.sharding import PartitionSpec as P

CONV = 4
MEMBERS = 4
TOKS = 32
OWN = 128
HALO = 16
SMALL = 16
FIRST = 104

eps_norm = 1e-06
decay_power = 8.0
f32 = jnp.float32
bf16 = jnp.bfloat16


def hop_blk(values, distance):
    return lax.ppermute(
        values, "blk", [(i, (i + distance) % MEMBERS) for i in range(MEMBERS)]
    )


def hop_tok(values, axis, distance):
    route = []
    for y in range(4):
        for z in range(4):
            for c in range(2):
                if axis == "y":
                    to = ((y + distance) % 4, z, c)
                elif axis == "z":
                    to = (y, (z + distance) % 4, c)
                else:
                    to = (y, z, (c + distance) % 2)
                route.append((y * 8 + z * 2 + c, to[0] * 8 + to[1] * 2 + to[2]))
    return lax.ppermute(values, "tok", route)


def hop(values, axis, distance):
    if axis == "blk":
        return hop_blk(values, distance)
    return hop_tok(values, axis, distance)


def hop_apart(values, distance, axis="blk"):
    route = []
    for b in range(MEMBERS):
        for t in range(TOKS):
            step = distance if t % 2 == 0 else -distance
            place = {"blk": b, "y": t // 8, "z": t // 2 % 4}
            place[axis] = (place[axis] + step) % 4
            to = place["blk"] * TOKS + place["y"] * 8 + place["z"] * 2 + t % 2
            route.append((b * TOKS + t, to))
    return lax.ppermute(values, ("blk", "tok"), route)


def either(core, first, second):
    return jnp.where(core == 0, first, second)


def ring_gather(values, core, before_last=()):
    behind = hop_apart(values, 1)
    ahead = hop_apart(values, -1)
    far = hop_apart(after(behind, *before_last), 1)
    return [values, either(core, ahead, behind), far, either(core, behind, ahead)]


def ring_open(parts, core, axis="blk"):
    return hop_apart(parts[2].astype(bf16), 1, axis), ring_near(parts, core, axis)


def ring_near(parts, core, axis="blk"):
    return hop_apart(either(core, parts[3], parts[1]).astype(bf16), -1, axis)


def ring_pass(parts, far, core, axis="blk"):
    onward = either(core, parts[1], parts[3]).astype(f32) + far.astype(f32)
    return hop_apart(onward.astype(bf16), 1, axis)


def ring_close(parts, near, joined):
    return parts[0].astype(f32) + near.astype(f32) + joined.astype(f32)


def ring_scatter(parts, core, axis="blk"):
    far, near = ring_open(parts, core, axis)
    return ring_close(parts, near, ring_pass(parts, far, core, axis))


def direct_scatter(parts, axis):
    total = parts[0].astype(f32)
    for distance in range(1, 4):
        total = total + hop(parts[distance], axis, distance).astype(f32)
    return total


def narrow_sum(left, right):
    return (left.astype(f32) + right.astype(f32)).astype(bf16)


def after(value, *others):
    return lax.optimization_barrier((value,) + others)[0]


def hop_sum(values, axis):
    return values + hop(values, axis, 1) + hop(values, axis, -1) + hop(values, axis, 2)


def direct_gather(values, axis="blk"):
    return [values] + [hop(values, axis, -d) for d in range(1, 4)]


def turned(values, place, axis=0):
    return [
        lax.dynamic_index_in_dim(values, (place + j) % 4, axis, keepdims=False) for j in range(4)
    ]


def swap_sum(parts, core):
    mine = lax.dynamic_index_in_dim(parts, core, 1, keepdims=False)
    theirs = lax.dynamic_index_in_dim(parts, 1 - core, 1, keepdims=False)
    return narrow_sum(mine, hop(theirs, "core", 1))


def chip_sum(values, core):
    return swap_sum(values.reshape(16, 2, -1, values.shape[1]), core)


def chips_sum(values):
    cores = [[2 * i + c for i in range(16)] for c in range(2)]
    terms = lax.all_to_all(values, "tok", 0, 0, axis_index_groups=cores, tiled=True)
    return jnp.sum(terms.astype(f32), axis=0)


def together(*values):
    return lax.optimization_barrier(values)


def small_gather(values, before_last):
    values = jnp.stack([values, hop(values, "core", 1)])
    values = jnp.stack(direct_gather(values, "z"))
    return jnp.stack(direct_gather(after(values, *before_last), "y"))


def product(operand, weight, out=f32):
    return jnp.dot(operand, weight, preferred_element_type=f32).astype(out)


def product_back(operand, weight, out=f32):
    return lax.dot_general(
        operand, weight, (((1,), (1,)), ((), ())), preferred_element_type=f32
    ).astype(out)


def product_outer(operand, weight, out=bf16):
    return lax.dot_general(
        operand, weight, (((0,), (0,)), ((), ())), preferred_element_type=f32
    ).astype(out)


def norm_factor(values):
    return lax.rsqrt(jnp.mean(values * values, axis=1, keepdims=True) + eps_norm)


def normalize_back(gradient, values, factor, gains):
    weighted = gradient * gains
    return factor * weighted - values * (factor * factor * factor) * jnp.mean(
        weighted * values, axis=1, keepdims=True
    )


def sigmoid(values):
    return 1.0 / (1.0 + jnp.exp(-values))


def one_minus_exp(values):
    series = 1.0 + values * (1.0 / 6.0)
    for order in (5.0, 4.0, 3.0, 2.0):
        series = 1.0 + values * series * (1.0 / order)
    return jnp.where(values > -0.1, -values * series, 1.0 - jnp.exp(values))


def inverse_root(values):
    return lax.rsqrt(jnp.maximum(values, 1e-37))


def gelu_parts(values):
    root = 0.7978845608028654
    square = values * values
    bent = jnp.tanh(root * values * (1.0 + 0.044715 * square))
    half = 0.5 * (1.0 + bent)
    slope = half + 0.5 * values * (1.0 - bent * bent) * root * (1.0 + 3.0 * 0.044715 * square)
    return values * half, slope


def rows_at(start, size):
    return pl.ds(pl.multiple_of(start, size), size)


def conv_rows(ci_ref, halo_ref, tile):
    before = halo_ref[...] if tile == 0 else ci_ref[(tile - 1) * HALO : tile * HALO, :]
    here = ci_ref[tile * HALO : (tile + 1) * HALO, :]
    return jnp.concatenate([before.astype(f32), here.astype(f32)], axis=0)


def local_forward_kernel(
    taps_ref,
    shift_ref,
    blocks_ref,
    bias_ref,
    soft_ref,
    ci_ref,
    halo_ref,
    place_ref,
    conv_ref,
    rate_ref,
    entry_ref,
    local_ref,
    cum_ref,
    edge_ref,
    gates_ref,
    pre_ref,
    exact_ref,
):
    slot = pl.program_id(0)
    channels = conv_ref.shape[1]
    block = blocks_ref.shape[0]
    width = 2 * channels

    @pl.when(slot == 0)
    def spread_gates():
        columns = lax.broadcasted_iota(jnp.int32, (HALO, width), 1)
        columns = jnp.where(columns >= channels, columns - channels, columns)
        for group in range(channels // block):
            inside = (columns >= group * block) & (columns < (group + 1) * block)
            for step in range(0, block, HALO):
                rows = blocks_ref[step : step + HALO, :].astype(f32)
                at = group * block + step
                gates_ref[at : at + HALO, :] = jnp.where(inside, rows, 0.0).astype(bf16)

    for tile in range(OWN // HALO):
        at = slice(tile * HALO, (tile + 1) * HALO)
        rows = conv_rows(ci_ref, halo_ref, tile)
        places = place_ref[at, :]
        total = shift_ref[...] + taps_ref[0:1, :] * rows[HALO:]
        for tap in range(1, CONV):
            lagged = pltpu.roll(rows, tap, 0)[HALO:]
            total = total + taps_ref[tap : tap + 1, :] * jnp.where(places >= tap, lagged, 0.0)
        exact_ref[at, :] = total
        conv_ref[at, :] = total.astype(bf16)
    for step in range(0, width, 256):
        columns = slice(step, step + 256)
        pre_ref[:, columns] = (
            jnp.dot(conv_ref[...], gates_ref[:, columns], preferred_element_type=f32)
            + bias_ref[:, columns]
        )

    row_ids = lax.broadcasted_iota(jnp.int32, (8, channels), 0)

    def scan(step, carry):
        halves = []
        for part in range(2):
            rows = rows_at(step * HALO + 8 * part, 8)
            rates = sigmoid(pre_ref[rows, :channels])
            entries = 0.5 * jnp.tanh(0.5 * pre_ref[rows, channels:]) + 0.5
            log_keep = -soft_ref[...] * rates
            resets = place_ref[rows, :] == 0
            coeff = jnp.where(resets, 0.0, jnp.exp(log_keep))
            squared = one_minus_exp(2.0 * log_keep)
            scaling = jnp.where(resets, 1.0, squared * inverse_root(squared))
            value = entries * exact_ref[rows, :] * scaling
            for distance in (1, 2, 4):
                reach = row_ids >= distance
                value = value + coeff * jnp.where(reach, pltpu.roll(value, distance, 0), 0.0)
                coeff = coeff * jnp.where(reach, pltpu.roll(coeff, distance, 0), 1.0)
            value = value + coeff * carry[1]
            coeff = coeff * carry[0]
            rate_ref[rows, :] = rates
            local_ref[rows, :] = value
            cum_ref[rows, :] = coeff
            halves.append(entries)
            carry = coeff[7:8], value[7:8]
        entry_ref[rows_at(step * HALO, HALO), :] = jnp.concatenate(halves, axis=0).astype(bf16)
        return carry

    start = (jnp.ones((1, channels), f32), jnp.zeros((1, channels), f32))
    coeff, value = lax.fori_loop(0, OWN // HALO, scan, start, unroll=2)
    edge_ref[pl.ds(slot, 1), :] = coeff
    edge_ref[pl.ds(slot + MEMBERS, 1), :] = value


def extended(pair, block):
    return pair[0] * block[:4], block[:4] * pair[1] + block[4:]


def whole_chain(channels):
    return jnp.ones((4, channels), f32), jnp.zeros((4, channels), f32)


def fold_near_kernel(backward, spot_ref, *refs):
    pieces, (total_ref, prefix_ref, held_ref) = refs[:4], refs[4:]
    z, c = spot_ref[2], spot_ref[3]
    for distance, piece in enumerate(pieces):
        held_ref[distance] = piece[...]
    chain = whole_chain(total_ref.shape[1])
    prefix = chain
    for place in reversed(range(8)) if backward else range(8):
        here = place == 2 * z + c
        prefix = tuple(jnp.where(here, new, old) for new, old in zip(chain, prefix))
        distance = jnp.bitwise_and(place // 2 - z + 4, 3)
        chain = extended(chain, held_ref[distance, jnp.bitwise_xor(place % 2, c)])
    total_ref[...] = jnp.concatenate(chain, axis=0)
    prefix_ref[...] = jnp.concatenate(prefix, axis=0)


def slot_carries(backward, spot_ref, pieces, prefix_ref, held_ref):
    y = spot_ref[1]
    channels = prefix_ref.shape[1]
    for distance, piece in enumerate(pieces):
        held_ref[distance] = piece[...]
    total = whole_chain(channels)
    prefix = total
    for place in reversed(range(4)) if backward else range(4):
        here = place == y
        prefix = tuple(jnp.where(here, new, old) for new, old in zip(total, prefix))
        total = extended(total, held_ref[jnp.bitwise_and(place - y + 4, 3)])
    prefix = extended(prefix, prefix_ref[...])
    current = jnp.zeros((1, channels), f32)
    carries = [None] * MEMBERS
    for _ in range(2):
        for slot in reversed(range(MEMBERS)) if backward else range(MEMBERS):
            one = slice(slot, slot + 1)
            carries[slot] = prefix[0][one] * current + prefix[1][one]
            current = total[0][one] * current + total[1][one]
    return carries


def mix_kernel(
    spot_ref,
    piece0,
    piece1,
    piece2,
    piece3,
    prefix_ref,
    local_ref,
    cum_ref,
    branch_ref,
    state_ref,
    mixed_ref,
    carry_ref,
    held_ref,
):
    slot = pl.program_id(0)

    @pl.when(slot == 0)
    def begin():
        pieces = (piece0, piece1, piece2, piece3)
        carries = slot_carries(False, spot_ref, pieces, prefix_ref, held_ref)
        carry_ref[...] = jnp.concatenate(carries, axis=0)

    carry = carry_ref[pl.ds(slot, 1), :]

    def apply(tile, token):
        rows = rows_at(tile * HALO, HALO)
        states = local_ref[rows, :] + cum_ref[rows, :] * carry
        state_ref[rows, :] = states.astype(bf16)
        mixed_ref[rows, :] = (states * gelu_parts(branch_ref[rows, :])[0]).astype(bf16)
        return token

    lax.fori_loop(0, OWN // HALO, apply, 0, unroll=2)


def reverse_scan(rows, later, gated, grad_ref, rate_ref, place_ref, soft_ref, row_ids):
    sgrad = grad_ref[rows, :] * gated
    keeps = jnp.exp(-soft_ref[...] * rate_ref[rows, :])
    coeff = jnp.where(place_ref[rows, :] == 0, 0.0, keeps)
    value = coeff * sgrad
    for distance in (1, 2, 4):
        reach = row_ids < 8 - distance
        value = value + coeff * jnp.where(reach, pltpu.roll(value, 8 - distance, 0), 0.0)
        coeff = coeff * jnp.where(reach, pltpu.roll(coeff, 8 - distance, 0), 1.0)
    return value + coeff * later, sgrad, coeff


def local_backward_kernel(
    soft_ref,
    grad_ref,
    branch_ref,
    state_ref,
    rate_ref,
    place_ref,
    bgrad_ref,
    edge_ref,
):
    slot = pl.program_id(0)
    channels = grad_ref.shape[1]
    row_ids = lax.broadcasted_iota(jnp.int32, (8, channels), 0)

    def scan(step, carry):
        base = OWN - HALO - step * HALO
        cum, later = carry
        slopes = []
        states = state_ref[rows_at(base, HALO), :].astype(f32)
        for part in (1, 0):
            rows = rows_at(base + 8 * part, 8)
            gated, slope = gelu_parts(branch_ref[rows, :])
            slopes.append(slope * grad_ref[rows, :] * states[8 * part : 8 * part + 8])
            held, _, coeff = reverse_scan(
                rows, later, gated, grad_ref, rate_ref, place_ref, soft_ref, row_ids
            )
            cum, later = coeff[0:1] * cum, held[0:1]
        bgrad_ref[rows_at(base, HALO), :] = jnp.concatenate(slopes[::-1], axis=0).astype(bf16)
        return cum, later

    start = (jnp.ones((1, channels), f32), jnp.zeros((1, channels), f32))
    coeff, value = lax.fori_loop(0, OWN // HALO, scan, start, unroll=2)
    edge_ref[pl.ds(slot, 1), :] = coeff
    edge_ref[pl.ds(slot + MEMBERS, 1), :] = value


def finish_backward_kernel(
    spot_ref,
    piece0,
    piece1,
    piece2,
    piece3,
    prefix_ref,
    carry_ref,
    soft_ref,
    taps_ref,
    gates_ref,
    grad_ref,
    branch_ref,
    state_ref,
    conv_ref,
    rate_ref,
    entry_ref,
    place_ref,
    ci_ref,
    halo_ref,
    pregrad_ref,
    igrad_ref,
    owed_ref,
    sums_ref,
    cgrad_ref,
    back_ref,
    held_ref,
):
    slot = pl.program_id(0)
    channels = conv_ref.shape[1]

    @pl.when(slot == 0)
    def begin():
        pieces = (piece0, piece1, piece2, piece3)
        carries = slot_carries(True, spot_ref, pieces, prefix_ref, held_ref)
        back_ref[...] = jnp.concatenate(carries, axis=0)
        sums_ref[...] = jnp.zeros_like(sums_ref)

    row_ids = lax.broadcasted_iota(jnp.int32, (8, channels), 0)
    back = back_ref[pl.ds(slot, 1), :]
    ahead_first = carry_ref[pl.ds(slot, 1), :]

    def gate_grads(step, carry):
        later, logit_sum, rate_sum, entry_sum = carry
        base = OWN - HALO - step * HALO
        low_rate, low_entry = [], []
        both = rows_at(base, HALO)
        states, convs = state_ref[both, :].astype(f32), conv_ref[both, :].astype(f32)
        all_entries = entry_ref[both, :].astype(f32)
        before = state_ref[rows_at(jnp.maximum(base - HALO, 0), HALO), :].astype(f32)[HALO - 1 :]
        before = jnp.where(base == 0, ahead_first, before)
        for part in (1, 0):
            first = base + 8 * part
            rows = rows_at(first, 8)
            gated, _ = gelu_parts(branch_ref[rows, :])
            held, sgrad, _ = reverse_scan(
                rows, later, gated, grad_ref, rate_ref, place_ref, soft_ref, row_ids
            )
            adjoint = sgrad + jnp.where(row_ids == 7, later, pltpu.roll(held, 7, 0))
            later = held[0:1]
            half = slice(8 * part, 8 * part + 8)
            ahead = states[7:8] if part else before
            previous = jnp.where(row_ids == 0, ahead, pltpu.roll(states[half], 1, 0))
            rates, entries, conv = rate_ref[rows, :], all_entries[half], convs[half]
            resets = place_ref[rows, :] == 0
            log_keep = -soft_ref[...] * rates
            squared = one_minus_exp(2.0 * log_keep)
            inverse = inverse_root(squared)
            scaling = jnp.where(resets, 1.0, squared * inverse)
            turn = jnp.where(resets, 0.0, (1.0 - squared) * inverse)
            weighed = adjoint * entries
            log_grad = held * previous - weighed * conv * turn
            rate_part = log_grad * rates
            logit_sum = logit_sum + rate_part
            rate_grad = -soft_ref[...] * rate_part * (1.0 - rates)
            direct = weighed * scaling
            entry_grad = direct * conv * (1.0 - entries)
            rate_sum = rate_sum + rate_grad
            entry_sum = entry_sum + entry_grad
            cgrad_ref[rows, :] = direct
            low_rate.append(rate_grad)
            low_entry.append(entry_grad)
        rows = rows_at(base, HALO)
        pregrad_ref[rows, :channels] = jnp.concatenate(low_rate[::-1], axis=0).astype(bf16)
        pregrad_ref[rows, channels:] = jnp.concatenate(low_entry[::-1], axis=0).astype(bf16)
        return later, logit_sum, rate_sum, entry_sum

    zero = jnp.zeros((8, channels), f32)
    _, logit_sum, rate_sum, entry_sum = lax.fori_loop(
        0, OWN // HALO, gate_grads, (back, zero, zero, zero), unroll=2
    )
    for step in range(0, channels, 128):
        columns = slice(step, step + 128)
        cgrad_ref[:, columns] += lax.dot_general(
            pregrad_ref[...],
            gates_ref[columns, :],
            (((1,), (1,)), ((), ())),
            preferred_element_type=f32,
        )

    def spread(tile):
        at = slice(tile * HALO, (tile + 1) * HALO)
        rows, places = cgrad_ref[at, :], place_ref[at, :]
        return [rows] + [jnp.where(places >= tap, rows, 0.0) for tap in range(1, CONV)]

    def shifted_sum(current, following):
        total = taps_ref[0:1, :] * current[0]
        for tap in range(1, CONV):
            both = jnp.concatenate([current[tap], following[tap]], axis=0)
            total = total + taps_ref[tap : tap + 1, :] * pltpu.roll(both, 2 * HALO - tap, 0)[:HALO]
        return total

    nothing = [jnp.zeros((HALO, channels), f32)] * CONV
    shift_sum, tap_sums = nothing[0], list(nothing)
    tiles = OWN // HALO
    coming = spread(0)
    owed_ref[...] = shifted_sum(nothing, coming)
    for tile in range(tiles):
        grads, coming = coming, spread(tile + 1) if tile + 1 < tiles else nothing
        igrad_ref[tile * HALO : (tile + 1) * HALO, :] = shifted_sum(grads, coming)
        inputs = conv_rows(ci_ref, halo_ref, tile)
        shift_sum = shift_sum + grads[0]
        tap_sums[0] = tap_sums[0] + grads[0] * inputs[HALO:]
        for tap in range(1, CONV):
            tap_sums[tap] = tap_sums[tap] + grads[tap] * pltpu.roll(inputs, tap, 0)[HALO:]

    def total_rows(values):
        return jnp.sum(values, axis=0, keepdims=True)

    sums_ref[...] += jnp.concatenate(
        [total_rows(v) for v in [shift_sum, rate_sum, entry_sum, logit_sum] + tap_sums], axis=0
    )


def in_hbm(values):
    return pltpu.with_memory_space_constraint(values, pltpu.HBM)


def by_slot(kernel, outs, ins, scratch, scalars, moved, far_outs=None):
    whole = [pl.BlockSpec(a.shape, lambda i, n=a.ndim: (0,) * n) for a in ins if not isinstance(a, tuple)]
    parts = [
        pl.BlockSpec((rows, a.shape[1]), lambda i, first=first: (first + i, 0))
        for a, rows, first in (a for a in ins if isinstance(a, tuple))
    ]
    out_specs = [
        pl.BlockSpec(shape, lambda i: (0, 0))
        if rows is None
        else pl.BlockSpec((rows, shape[1]), lambda i: (i, 0))
        for rows, shape, _ in outs
    ]
    return pl.pallas_call(
        kernel,
        grid=(MEMBERS,),
        in_specs=[pl.BlockSpec(memory_space=pltpu.SMEM)] * len(scalars) + whole + parts,
        out_specs=out_specs,
        out_shape=[
            pltpu.HBM(shape, dtype) if far else jax.ShapeDtypeStruct(shape, dtype)
            for (_, shape, dtype), far in zip(outs, far_outs or [False] * len(outs))
        ],
        scratch_shapes=[pltpu.VMEM(shape, dtype) for shape, dtype in scratch],
        compiler_params=pltpu.CompilerParams(vmem_limit_bytes=16 * 1024 * 1024),
        cost_estimate=pl.CostEstimate(flops=0, bytes_accessed=moved, transcendentals=0),
    )(*scalars, *[a[0] if isinstance(a, tuple) else a for a in ins])


def in_vmem(kernel, outs, scratch=(), scalars=0, count=1, moved=0):
    vmem = pl.BlockSpec(memory_space=pltpu.VMEM)
    smem = pl.BlockSpec(memory_space=pltpu.SMEM)
    return pl.pallas_call(
        kernel,
        out_shape=[jax.ShapeDtypeStruct(shape, dtype) for shape, dtype in outs],
        in_specs=[smem] * scalars + [vmem] * count,
        out_specs=[vmem] * len(outs),
        scratch_shapes=[pltpu.VMEM(shape, dtype) for shape, dtype in scratch],
        compiler_params=pltpu.CompilerParams(vmem_limit_bytes=16 * 1024 * 1024),
        cost_estimate=pl.CostEstimate(flops=0, bytes_accessed=moved, transcendentals=0),
    )


def exchange_edges(edges, spots, backward):
    channels = edges.shape[1]
    near = jnp.stack([edges, hop(edges, "core", 1)])
    total, prefix = in_vmem(
        functools.partial(fold_near_kernel, backward),
        [((8, channels), f32)] * 2,
        [((4, 2, 8, channels), f32)],
        scalars=1,
        count=4,
        moved=3_000_000,
    )(spots, *direct_gather(near, "z"))
    return direct_gather(total, "y") + [prefix], near


def outer_kernel(lhs_one, lhs_two, rhs_one, rhs_two, rhs_three, out_ref):
    def settle(lhs, rhs):
        out_ref[...] = lax.dot_general(
            lhs[...], rhs[...], (((0,), (0,)), ((), ())), preferred_element_type=f32
        ).astype(bf16)

    for step, (lhs, rhs) in enumerate(
        ((lhs_one, rhs_one), (lhs_one, rhs_two), (lhs_two, rhs_three))
    ):
        pl.when(pl.program_id(0) == step)(functools.partial(settle, lhs, rhs))


def feed_outer(lhs_one, lhs_two, rhs):
    rows, features = lhs_one.shape
    columns = rhs[0].shape[1]
    height = 1024
    whole = pl.BlockSpec(
        (rows, columns), lambda j, i: (0, 0), pipeline_mode=pl.Buffered(buffer_count=1)
    )
    return pl.pallas_call(
        outer_kernel,
        grid=(3, features // height),
        in_specs=[
            pl.BlockSpec((rows, height), lambda j, i: (0, jnp.where(j < 2, i, 0))),
            pl.BlockSpec((rows, height), lambda j, i: (0, jnp.where(j < 2, 0, i))),
            whole,
            whole,
            whole,
        ],
        out_specs=pl.BlockSpec((height, columns), lambda j, i: (i, j)),
        out_shape=pltpu.HBM((features, 3 * columns), bf16),
        compiler_params=pltpu.CompilerParams(vmem_limit_bytes=26 * 1024 * 1024),
        cost_estimate=pl.CostEstimate(
            flops=6 * rows * features * columns,
            bytes_accessed=6 * features * columns,
            transcendentals=0,
        ),
    )(lhs_one, lhs_two, *rhs)


def small_kernel(cut, conv_ref, pregrad_ref, sums_ref, extra_ref, out_ref):
    channels = conv_ref.shape[1]
    width = 2 * channels
    block = cut * TOKS
    dense = lax.dot_general(
        conv_ref[...],
        pregrad_ref[...],
        (((0,), (0,)), ((), ())),
        preferred_element_type=f32,
    )
    columns = lax.broadcasted_iota(jnp.int32, (block, width), 1)
    columns = jnp.where(columns >= channels, columns - channels, columns)
    gates = jnp.zeros((block, width), f32)
    for group in range(channels // block):
        inside = (columns >= group * block) & (columns < (group + 1) * block)
        gates = jnp.where(inside, dense[group * block : (group + 1) * block], gates)
    own = channels // TOKS
    sums = sums_ref[...]
    blank = jnp.zeros((4, channels - 256), f32)
    spare = jnp.zeros((SMALL - 2 * cut - 5, channels), f32)
    for tok in range(TOKS):
        rows = gates[tok * cut : (tok + 1) * cut]
        turned_sums = pltpu.roll(sums, channels - tok * own, 1) if tok else sums
        vectors = [turned_sums[:4, :128], turned_sums[4:, :128], blank]
        pieces = [rows[:, :channels], rows[:, channels:], jnp.concatenate(vectors, axis=1)]
        pieces += [extra_ref[tok : tok + 1, :], spare]
        out_ref[tok] = jnp.concatenate(pieces, axis=0).astype(bf16)


def halves_kernel(count, small, spot_ref, *refs):
    core = spot_ref[3]
    small_ref, refs = (refs[0], refs[1:]) if small else (None, refs)
    mine_ref, theirs_ref = refs[2 * count :]
    chips, rows, _ = mine_ref.shape
    rows = (rows - small) // count
    for which in range(count):
        sums = lax.dot_general(
            refs[which][...],
            refs[count + which][...],
            (((0,), (0,)), ((), ())),
            preferred_element_type=f32,
        )
        for chip in range(chips):
            low = sums[2 * chip * rows : (2 * chip + 1) * rows]
            high = sums[(2 * chip + 1) * rows : (2 * chip + 2) * rows]
            at = slice(which * rows, (which + 1) * rows)
            mine_ref[chip, at, :] = jnp.where(core == 0, low, high).astype(bf16)
            theirs_ref[chip, at, :] = jnp.where(core == 0, high, low).astype(bf16)
    for chip in range(chips if small else 0):
        low, high = small_ref[2 * chip].astype(f32), small_ref[2 * chip + 1].astype(f32)
        at = slice(count * rows, count * rows + small)
        mine_ref[chip, at, :] = jnp.where(core == 0, low, high).astype(bf16)
        theirs_ref[chip, at, :] = jnp.where(core == 0, high, low).astype(bf16)


def outer_halves(spots, small, lhs, rhs):
    count = len(lhs)
    features = lhs[0].shape[1]
    rows, columns = rhs[0].shape
    height = 1024
    chips = height // 128
    extra = SMALL if small is not None else 0
    total = 64 * count + extra
    shape = jax.ShapeDtypeStruct((features // 128, total, columns), bf16)
    out_spec = pl.BlockSpec((chips, total, columns), lambda i: (i, 0, 0))
    return pl.pallas_call(
        functools.partial(halves_kernel, count, extra),
        grid=(features // height,),
        in_specs=[pl.BlockSpec(memory_space=pltpu.SMEM)]
        + [pl.BlockSpec((2 * chips, SMALL, columns), lambda i: (i, 0, 0))] * (extra > 0)
        + [pl.BlockSpec((rows, height), lambda i: (0, i))] * count
        + [pl.BlockSpec((rows, columns), lambda i: (0, 0))] * count,
        out_specs=[out_spec] * 2,
        out_shape=[shape] * 2,
        compiler_params=pltpu.CompilerParams(vmem_limit_bytes=28 * 1024 * 1024),
        cost_estimate=pl.CostEstimate(
            flops=2 * count * rows * features * columns,
            bytes_accessed=0,
            transcendentals=0,
        ),
    )(spots, *([small] if extra else []), *lhs, *rhs)


def per_device(
    inputs,
    mix_scale,
    branch_mat,
    input_mat,
    conv_taps,
    conv_shift,
    rate_mat,
    rate_shift,
    entry_mat,
    entry_shift,
    decay_logit,
    out_mat,
    feed_scale,
    gate_mat,
    up_mat,
    down_mat,
    lengths,
    cotangent,
):
    blk = lax.axis_index("blk")
    tok = lax.axis_index("tok")
    spot = (tok // 8, (tok // 2) % 4, tok % 2)
    spots = jnp.stack([tok] + list(spot)).astype(jnp.int32)
    channels = branch_mat.shape[1]
    hidden_units = gate_mat.shape[1]
    slice_rows = branch_mat.shape[0]
    total_rows = MEMBERS * OWN

    groups, cut, block = rate_mat.shape
    own_channels = conv_shift.shape[0]
    vectors = [conv_taps, conv_shift[None], rate_shift[None], entry_shift[None], decay_logit[None]]
    vectors = jnp.concatenate(vectors, axis=0).reshape(-1)
    extras = jnp.concatenate([vectors, mix_scale, feed_scale])
    extras = jnp.pad(extras, (0, channels - extras.shape[0]))[None]
    smalls = [jnp.moveaxis(mats, 0, 1).reshape(cut, channels) for mats in (rate_mat, entry_mat)]
    smalls = jnp.concatenate(smalls + [extras], axis=0)
    smalls = jnp.pad(smalls, ((0, HALO - smalls.shape[0]), (0, 0)))
    input_blocks = ring_gather(inputs, spot[2])
    near = after(small_gather(smalls, (input_blocks[1], input_blocks[3])), input_blocks[2])
    for axis, place in ((2, spot[2]), (1, spot[1]), (0, spot[0])):
        near = jnp.roll(near, place, axis)
    near = near.reshape(TOKS, HALO, channels)
    mixer_all = lax.all_gather(
        jnp.concatenate([input_mat, branch_mat, out_mat.T], axis=1), "tok", axis=0, tiled=True
    )
    devices = MEMBERS * TOKS
    tail = lax.ppermute(
        inputs[OWN - HALO :], ("blk", "tok"), [(i, (i + 1) % devices) for i in range(devices)]
    )
    cotangent_blocks = ring_gather(after(cotangent, input_blocks[2]), spot[2])
    rows_all = jnp.concatenate(input_blocks + direct_gather(tail), axis=0)
    cotangent_all = jnp.concatenate(cotangent_blocks, axis=0)

    extras = near[:, 2 * cut]
    vectors = extras[:, : 8 * own_channels].reshape(TOKS, 8, own_channels).astype(f32)
    vectors = jnp.moveaxis(vectors, 0, 1).reshape(8, channels)
    gains = extras[:, 8 * own_channels : 8 * own_channels + 2 * slice_rows].astype(f32)
    mix_gain = gains[:, :slice_rows].reshape(1, -1)
    feed_gain = gains[:, slice_rows:].reshape(1, -1)
    wide_values = rows_all.astype(f32)
    wide_one = (wide_values * norm_factor(wide_values) * mix_gain).astype(bf16)
    taps, shift = vectors[:CONV], vectors[4:5]
    bias = jnp.concatenate([vectors[5:6], vectors[6:7]], axis=1)
    soft = decay_power * jax.nn.softplus(-vectors[7:8])
    blocks = [near[:, i * cut : (i + 1) * cut].reshape(block, channels) for i in range(2)]
    blocks = after(jnp.concatenate(blocks, axis=1), cotangent_blocks[2])
    feed_own = jnp.concatenate([gate_mat, up_mat, down_mat.T], axis=1)
    feed_all = lax.all_gather(after(feed_own, wide_one, blocks), "tok", axis=0, tiled=True)
    gate_up_all = feed_all[:, : 2 * hidden_units]
    down_turned = feed_all[:, 2 * hidden_units :]
    own_one = wide_one[:total_rows]
    input_all = mixer_all[:, :channels]
    branch_all = mixer_all[:, channels : 2 * channels]
    project_all = mixer_all[:, : 2 * channels]
    out_turned = mixer_all[:, 2 * channels : 3 * channels]

    slots = (blk + jnp.arange(MEMBERS, dtype=jnp.int32)) % MEMBERS
    token_ids = (
        (slots * TOKS + tok)[:, None] * OWN + jnp.arange(OWN, dtype=jnp.int32)[None, :]
    ).reshape(-1)
    starts = jnp.cumsum(lengths) - lengths
    opened = jnp.max(jnp.where(starts[None, :] <= token_ids[:, None], starts[None, :], 0), axis=1)
    places = (token_ids - opened).reshape(total_rows, 1).astype(jnp.int32)

    conv_input = product(wide_one, input_all, bf16)
    branch = product(own_one, branch_all)
    halo_first = total_rows // HALO
    conv, rates, entries, local, cum, edges, gates = by_slot(
        local_forward_kernel,
        [(OWN, (total_rows, channels), kind) for kind in (bf16, f32, bf16, f32, f32)]
        + [(None, (8, channels), f32), (None, (channels, 2 * channels), bf16)],
        [
            taps,
            shift,
            blocks,
            bias,
            soft,
            (conv_input, OWN, 0),
            (conv_input, HALO, halo_first),
            (places, OWN, 0),
        ],
        [((OWN, 2 * channels), f32), ((OWN, channels), f32)],
        (),
        30_000_000,
        [True, True, True, False, False, False, True],
    )
    conv, rates, entries, gates = [in_hbm(a) for a in (conv, rates, entries, gates)]
    chains, _ = exchange_edges(edges, spots, False)
    states, mixture, carried = by_slot(
        mix_kernel,
        [
            (OWN, (total_rows, channels), bf16),
            (OWN, (total_rows, channels), bf16),
            (None, (MEMBERS, channels), f32),
        ],
        [*chains] + [(a, OWN, 0) for a in (local, cum, branch)],
        [((4, 8, channels), f32)],
        (spots,),
        4_500_000,
    )

    def rows_of(values):
        return [values[j * OWN : (j + 1) * OWN] for j in range(MEMBERS)]

    own_values = inputs.astype(f32)
    middle = own_values + ring_scatter(rows_of(product_back(mixture, out_turned)), spot[2])

    factor_two = norm_factor(middle)
    normed_two = (middle * factor_two * feed_gain).astype(bf16)
    hidden_grad = product(after(cotangent_all, mixture), down_turned)
    blocks_two = ring_gather(normed_two, spot[2])
    blocks_two[2] = after(blocks_two[2], hidden_grad)
    wide_two = jnp.concatenate(blocks_two, axis=0)
    gate_up = product(wide_two, gate_up_all)
    gate_pre, up_pre = gate_up[:, :hidden_units], gate_up[:, hidden_units:]
    gate_act, gate_slope = gelu_parts(gate_pre)
    hidden = (gate_act * up_pre).astype(bf16)
    gate_grad = (gate_slope * hidden_grad * up_pre).astype(bf16)
    up_grad = (gate_act * hidden_grad).astype(bf16)
    feed_shares = feed_outer(wide_two, cotangent_all, (gate_grad, up_grad, hidden))
    feed_grads = lax.psum_scatter(feed_shares, "tok", scatter_dimension=0, tiled=True)
    gate_late, up_late = after((gate_grad, up_grad), feed_shares)
    two_shares = product_back(jnp.concatenate([gate_late, up_late], axis=1), gate_up_all)
    two_parts = rows_of(two_shares)
    two_far, two_near = ring_open(two_parts, spot[2])
    two_grad = ring_close(two_parts, two_near, ring_pass(two_parts, two_far, spot[2]))
    middle_grad = cotangent.astype(f32) + normalize_back(two_grad, middle, factor_two, feed_gain)
    grad_feed_scale = jnp.sum(two_grad * middle * factor_two, axis=0)
    layer_shares = product_back(after(hidden, two_far), down_turned, bf16)
    middle_blocks = ring_gather(middle_grad.astype(bf16), spot[2])
    middle_blocks[2] = after(middle_blocks[2], layer_shares)
    middle_wide = jnp.concatenate(middle_blocks, axis=0)
    mixture_grad = product(middle_wide, out_turned)
    branch = in_hbm(branch)
    branch_grad, back_edges = by_slot(
        local_backward_kernel,
        [(OWN, (total_rows, channels), bf16), (None, (8, channels), f32)],
        [soft] + [(a, OWN, 0) for a in (mixture_grad, branch, states, rates, places)],
        (),
        (),
        9_500_000,
    )
    chains_back, near_back = exchange_edges(back_edges, spots, True)
    pregrads, igrad, owed, sums = by_slot(
        finish_backward_kernel,
        [
            (OWN, (total_rows, 2 * channels), bf16),
            (OWN, (total_rows, channels), f32),
            (HALO, (MEMBERS * HALO, channels), f32),
            (None, (8, channels), f32),
        ],
        [*chains_back, carried, soft, taps, gates]
        + [(a, OWN, 0) for a in (mixture_grad, branch, states, conv, rates, entries)]
        + [(places, OWN, 0), (conv_input, OWN, 0), (conv_input, HALO, halo_first)],
        [
            ((OWN, channels), f32),
            ((MEMBERS, channels), f32),
            ((4, 8, channels), f32),
        ],
        (spots,),
        40_000_000,
    )
    returned = lax.ppermute(
        owed.reshape(MEMBERS, HALO, channels)[:, HALO - 3 :],
        "tok",
        [(i, (i - 1) % TOKS) for i in range(TOKS)],
    )
    turned_on = jnp.concatenate([returned[1:], returned[:1]], axis=0)
    landing = jnp.where(tok == TOKS - 1, turned_on, returned)
    input_grad = igrad.reshape(MEMBERS, OWN, channels) + jnp.pad(
        landing, ((0, 0), (OWN - 3, 0), (0, 0))
    )
    input_low = input_grad.reshape(total_rows, channels).astype(bf16)
    feed_rows = jnp.pad(
        grad_feed_scale.reshape(TOKS, slice_rows), ((0, 0), (0, channels - slice_rows))
    )
    (small_rows,) = in_vmem(
        functools.partial(small_kernel, cut),
        [((TOKS, SMALL, channels), bf16)],
        count=4,
        moved=11_000_000,
    )(conv, pregrads, sums, feed_rows)

    core = spot[2]
    weight_mine, weight_theirs = outer_halves(
        spots, small_rows, (middle_wide, wide_one, wide_one), (mixture, branch_grad, input_low)
    )
    weight_other = hop(weight_theirs, "core", 1)
    late = after(input_low, weight_theirs)
    one_shares = product_back(jnp.concatenate([late, branch_grad], axis=1), project_all, bf16)
    weight_chip = narrow_sum(weight_mine, weight_other)
    one_shares = after(one_shares, weight_chip)
    one_parts = rows_of(one_shares)
    one_grad = ring_scatter(one_parts, core)
    factor_one = norm_factor(own_values)
    first_grad = normalize_back(one_grad, own_values, factor_one, mix_gain)
    inputs_grad = (middle_grad + first_grad).astype(bf16)
    settled = chips_sum(weight_chip)
    layer_out = middle + ring_scatter(rows_of(after(layer_shares, one_grad)), core)
    grad_out, grad_branch, grad_input = [
        settled[i * slice_rows : (i + 1) * slice_rows] for i in range(3)
    ]
    settled = settled[3 * slice_rows :]
    grad_mix_scale = jnp.sum(
        grad_branch * branch_mat.astype(f32) + grad_input * input_mat.astype(f32), axis=1
    ) / mix_scale.astype(f32)
    gains_own = jnp.concatenate([grad_mix_scale, settled[2 * cut + 4, :slice_rows]])
    gains_own = hop_sum(gains_own.reshape(1, -1), "blk")[0]
    gate_own = [
        jnp.moveaxis(settled[i * cut : (i + 1) * cut].reshape(cut, groups, block), 1, 0)
        for i in range(2)
    ]
    sums_own = settled[2 * cut : 2 * cut + 4]
    taps_own = sums_own[:, 128 : 128 + own_channels]
    sums_own = sums_own[:, :own_channels]
    own_logits = decay_logit.astype(f32)
    return (
        layer_out.astype(bf16),
        inputs_grad,
        gains_own[:slice_rows],
        grad_branch,
        grad_input,
        taps_own,
        sums_own[0],
        gate_own[0],
        sums_own[1],
        gate_own[1],
        sums_own[2],
        sums_own[3] * decay_power * jax.nn.sigmoid(-own_logits),
        grad_out.T,
        gains_own[slice_rows : 2 * slice_rows],
        feed_grads[:, :hidden_units].astype(f32),
        feed_grads[:, hidden_units : 2 * hidden_units].astype(f32),
        feed_grads[:, 2 * hidden_units :].T.astype(f32),
    )


def solution(mesh):
    in_specs = (
        P(("blk", "tok"), None),
        P("tok"),
        P("tok", "blk"),
        P("tok", "blk"),
        P(None, ("blk", "tok")),
        P(("blk", "tok")),
        P("blk", "tok", None),
        P(("blk", "tok")),
        P("blk", "tok", None),
        P(("blk", "tok")),
        P(("blk", "tok")),
        P("blk", "tok"),
        P("tok"),
        P("tok", "blk"),
        P("tok", "blk"),
        P("blk", "tok"),
        P(),
        P(("blk", "tok"), None),
    )
    out_specs = (
        P(("blk", "tok"), None),
        P(("blk", "tok"), None),
        P("tok"),
        P("tok", "blk"),
        P("tok", "blk"),
        P(None, ("blk", "tok")),
        P(("blk", "tok")),
        P("blk", "tok", None),
        P(("blk", "tok")),
        P("blk", "tok", None),
        P(("blk", "tok")),
        P(("blk", "tok")),
        P("blk", "tok"),
        P("tok"),
        P("tok", "blk"),
        P("tok", "blk"),
        P("blk", "tok"),
    )
    return jax.shard_map(
        per_device, mesh=mesh, in_specs=in_specs, out_specs=out_specs, check_vma=False
    )
```

```python
import functools

import jax
import jax.numpy as jnp
from jax import lax
from jax.experimental import pallas as pl
from jax.experimental.pallas import tpu as pltpu
from jax.sharding import PartitionSpec as P

CONV = 4
MEMBERS = 4
TOKS = 32
OWN = 128
HALO = 16
SMALL = 16
FIRST = 104

eps_norm = 1e-06
decay_power = 8.0
f32 = jnp.float32
bf16 = jnp.bfloat16


def hop_blk(values, distance):
    return lax.ppermute(
        values, "blk", [(i, (i + distance) % MEMBERS) for i in range(MEMBERS)]
    )


def hop_tok(values, axis, distance):
    route = []
    for y in range(4):
        for z in range(4):
            for c in range(2):
                if axis == "y":
                    to = ((y + distance) % 4, z, c)
                elif axis == "z":
                    to = (y, (z + distance) % 4, c)
                else:
                    to = (y, z, (c + distance) % 2)
                route.append((y * 8 + z * 2 + c, to[0] * 8 + to[1] * 2 + to[2]))
    return lax.ppermute(values, "tok", route)


def hop(values, axis, distance):
    if axis == "blk":
        return hop_blk(values, distance)
    return hop_tok(values, axis, distance)


def hop_apart(values, distance, axis="blk"):
    route = []
    for b in range(MEMBERS):
        for t in range(TOKS):
            step = distance if t % 2 == 0 else -distance
            place = {"blk": b, "y": t // 8, "z": t // 2 % 4}
            place[axis] = (place[axis] + step) % 4
            to = place["blk"] * TOKS + place["y"] * 8 + place["z"] * 2 + t % 2
            route.append((b * TOKS + t, to))
    return lax.ppermute(values, ("blk", "tok"), route)


def either(core, first, second):
    return jnp.where(core == 0, first, second)


def ring_gather(values, core, before_last=()):
    behind = hop_apart(values, 1)
    ahead = hop_apart(values, -1)
    far = hop_apart(after(behind, *before_last), 1)
    return [values, either(core, ahead, behind), far, either(core, behind, ahead)]


def ring_open(parts, core, axis="blk"):
    return hop_apart(parts[2].astype(bf16), 1, axis), ring_near(parts, core, axis)


def ring_near(parts, core, axis="blk"):
    return hop_apart(either(core, parts[3], parts[1]).astype(bf16), -1, axis)


def ring_pass(parts, far, core, axis="blk"):
    onward = either(core, parts[1], parts[3]).astype(f32) + far.astype(f32)
    return hop_apart(onward.astype(bf16), 1, axis)


def ring_close(parts, near, joined):
    return parts[0].astype(f32) + near.astype(f32) + joined.astype(f32)


def ring_scatter(parts, core, axis="blk"):
    far, near = ring_open(parts, core, axis)
    return ring_close(parts, near, ring_pass(parts, far, core, axis))


def direct_scatter(parts, axis):
    total = parts[0].astype(f32)
    for distance in range(1, 4):
        total = total + hop(parts[distance], axis, distance).astype(f32)
    return total


def narrow_sum(left, right):
    return (left.astype(f32) + right.astype(f32)).astype(bf16)


def after(value, *others):
    return lax.optimization_barrier((value,) + others)[0]


def hop_sum(values, axis):
    return values + hop(values, axis, 1) + hop(values, axis, -1) + hop(values, axis, 2)


def direct_gather(values, axis="blk"):
    return [values] + [hop(values, axis, -d) for d in range(1, 4)]


def turned(values, place, axis=0):
    return [
        lax.dynamic_index_in_dim(values, (place + j) % 4, axis, keepdims=False) for j in range(4)
    ]


def swap_sum(parts, core):
    mine = lax.dynamic_index_in_dim(parts, core, 1, keepdims=False)
    theirs = lax.dynamic_index_in_dim(parts, 1 - core, 1, keepdims=False)
    return narrow_sum(mine, hop(theirs, "core", 1))


def chip_sum(values, core):
    return swap_sum(values.reshape(16, 2, -1, values.shape[1]), core)


def chips_sum(values):
    cores = [[2 * i + c for i in range(16)] for c in range(2)]
    terms = lax.all_to_all(values, "tok", 0, 0, axis_index_groups=cores, tiled=True)
    return jnp.sum(terms.astype(f32), axis=0)


def together(*values):
    return lax.optimization_barrier(values)


def small_gather(values, before_last):
    values = jnp.stack([values, hop(values, "core", 1)])
    values = jnp.stack(direct_gather(values, "z"))
    return jnp.stack(direct_gather(after(values, *before_last), "y"))


def product(operand, weight, out=f32):
    return jnp.dot(operand, weight, preferred_element_type=f32).astype(out)


def product_back(operand, weight, out=f32):
    return lax.dot_general(
        operand, weight, (((1,), (1,)), ((), ())), preferred_element_type=f32
    ).astype(out)


def product_outer(operand, weight, out=bf16):
    return lax.dot_general(
        operand, weight, (((0,), (0,)), ((), ())), preferred_element_type=f32
    ).astype(out)


def norm_factor(values):
    return lax.rsqrt(jnp.mean(values * values, axis=1, keepdims=True) + eps_norm)


def normalize_back(gradient, values, factor, gains):
    weighted = gradient * gains
    return factor * weighted - values * (factor * factor * factor) * jnp.mean(
        weighted * values, axis=1, keepdims=True
    )


def sigmoid(values):
    return 1.0 / (1.0 + jnp.exp(-values))


def one_minus_square(keeps, values):
    series = 1.0 + values * (1.0 / 6.0)
    for order in (5.0, 4.0, 3.0, 2.0):
        series = 1.0 + values * series * (1.0 / order)
    return jnp.where(values > -0.1, -values * series, 1.0 - keeps * keeps)


def inverse_root(values):
    return lax.rsqrt(jnp.maximum(values, 1e-37))


def gelu_parts(values):
    root = 0.7978845608028654
    square = values * values
    bent = jnp.tanh(root * values * (1.0 + 0.044715 * square))
    half = 0.5 * (1.0 + bent)
    slope = half + 0.5 * values * (1.0 - bent * bent) * root * (1.0 + 3.0 * 0.044715 * square)
    return values * half, slope


def rows_at(start, size):
    return pl.ds(pl.multiple_of(start, size), size)


def conv_rows(ci_ref, halo_ref, tile):
    before = halo_ref[...] if tile == 0 else ci_ref[(tile - 1) * HALO : tile * HALO, :]
    here = ci_ref[tile * HALO : (tile + 1) * HALO, :]
    return jnp.concatenate([before.astype(f32), here.astype(f32)], axis=0)


def local_forward_kernel(
    taps_ref,
    shift_ref,
    blocks_ref,
    bias_ref,
    soft_ref,
    ci_ref,
    halo_ref,
    place_ref,
    conv_ref,
    rate_ref,
    entry_ref,
    local_ref,
    cum_ref,
    edge_ref,
    gates_ref,
    pre_ref,
    exact_ref,
):
    slot = pl.program_id(0)
    channels = conv_ref.shape[1]
    block = blocks_ref.shape[0]
    width = 2 * channels

    @pl.when(slot == 0)
    def spread_gates():
        columns = lax.broadcasted_iota(jnp.int32, (HALO, width), 1)
        columns = jnp.where(columns >= channels, columns - channels, columns)
        for group in range(channels // block):
            inside = (columns >= group * block) & (columns < (group + 1) * block)
            for step in range(0, block, HALO):
                rows = blocks_ref[step : step + HALO, :].astype(f32)
                at = group * block + step
                gates_ref[at : at + HALO, :] = jnp.where(inside, rows, 0.0).astype(bf16)

    for tile in range(OWN // HALO):
        at = slice(tile * HALO, (tile + 1) * HALO)
        rows = conv_rows(ci_ref, halo_ref, tile)
        places = place_ref[at, :]
        total = shift_ref[...] + taps_ref[0:1, :] * rows[HALO:]
        for tap in range(1, CONV):
            lagged = pltpu.roll(rows, tap, 0)[HALO:]
            total = total + taps_ref[tap : tap + 1, :] * jnp.where(places >= tap, lagged, 0.0)
        exact_ref[at, :] = total
        conv_ref[at, :] = total.astype(bf16)
    for step in range(0, width, 256):
        columns = slice(step, step + 256)
        pre_ref[:, columns] = (
            jnp.dot(conv_ref[...], gates_ref[:, columns], preferred_element_type=f32)
            + bias_ref[:, columns]
        )

    row_ids = lax.broadcasted_iota(jnp.int32, (8, channels), 0)

    def scan(step, carry):
        halves = []
        for part in range(2):
            rows = rows_at(step * HALO + 8 * part, 8)
            rates = sigmoid(pre_ref[rows, :channels])
            entries = 0.5 * jnp.tanh(0.5 * pre_ref[rows, channels:]) + 0.5
            log_keep = -soft_ref[...] * rates
            resets = place_ref[rows, :] == 0
            keeps = jnp.exp(log_keep)
            coeff = jnp.where(resets, 0.0, keeps)
            squared = one_minus_square(keeps, 2.0 * log_keep)
            scaling = jnp.where(resets, 1.0, squared * inverse_root(squared))
            value = entries * exact_ref[rows, :] * scaling
            for distance in (1, 2, 4):
                reach = row_ids >= distance
                value = value + coeff * jnp.where(reach, pltpu.roll(value, distance, 0), 0.0)
                coeff = coeff * jnp.where(reach, pltpu.roll(coeff, distance, 0), 1.0)
            value = value + coeff * carry[1]
            coeff = coeff * carry[0]
            rate_ref[rows, :] = rates
            local_ref[rows, :] = value
            cum_ref[rows, :] = coeff
            halves.append(entries)
            carry = coeff[7:8], value[7:8]
        entry_ref[rows_at(step * HALO, HALO), :] = jnp.concatenate(halves, axis=0).astype(bf16)
        return carry

    start = (jnp.ones((1, channels), f32), jnp.zeros((1, channels), f32))
    coeff, value = lax.fori_loop(0, OWN // HALO, scan, start, unroll=2)
    edge_ref[pl.ds(slot, 1), :] = coeff
    edge_ref[pl.ds(slot + MEMBERS, 1), :] = value


def extended(pair, block):
    return pair[0] * block[:4], block[:4] * pair[1] + block[4:]


def whole_chain(channels):
    return jnp.ones((4, channels), f32), jnp.zeros((4, channels), f32)


def fold_near_kernel(backward, spot_ref, *refs):
    pieces, (total_ref, prefix_ref, held_ref) = refs[:4], refs[4:]
    z, c = spot_ref[2], spot_ref[3]
    for distance, piece in enumerate(pieces):
        held_ref[distance] = piece[...]
    chain = whole_chain(total_ref.shape[1])
    prefix = chain
    for place in reversed(range(8)) if backward else range(8):
        here = place == 2 * z + c
        prefix = tuple(jnp.where(here, new, old) for new, old in zip(chain, prefix))
        distance = jnp.bitwise_and(place // 2 - z + 4, 3)
        chain = extended(chain, held_ref[distance, jnp.bitwise_xor(place % 2, c)])
    total_ref[...] = jnp.concatenate(chain, axis=0)
    prefix_ref[...] = jnp.concatenate(prefix, axis=0)


def slot_carries(backward, spot_ref, pieces, prefix_ref, held_ref):
    y = spot_ref[1]
    channels = prefix_ref.shape[1]
    for distance, piece in enumerate(pieces):
        held_ref[distance] = piece[...]
    total = whole_chain(channels)
    prefix = total
    for place in reversed(range(4)) if backward else range(4):
        here = place == y
        prefix = tuple(jnp.where(here, new, old) for new, old in zip(total, prefix))
        total = extended(total, held_ref[jnp.bitwise_and(place - y + 4, 3)])
    prefix = extended(prefix, prefix_ref[...])
    current = jnp.zeros((1, channels), f32)
    carries = [None] * MEMBERS
    for _ in range(2):
        for slot in reversed(range(MEMBERS)) if backward else range(MEMBERS):
            one = slice(slot, slot + 1)
            carries[slot] = prefix[0][one] * current + prefix[1][one]
            current = total[0][one] * current + total[1][one]
    return carries


def mix_kernel(
    spot_ref,
    piece0,
    piece1,
    piece2,
    piece3,
    prefix_ref,
    local_ref,
    cum_ref,
    branch_ref,
    state_ref,
    mixed_ref,
    carry_ref,
    held_ref,
):
    slot = pl.program_id(0)

    @pl.when(slot == 0)
    def begin():
        pieces = (piece0, piece1, piece2, piece3)
        carries = slot_carries(False, spot_ref, pieces, prefix_ref, held_ref)
        carry_ref[...] = jnp.concatenate(carries, axis=0)

    carry = carry_ref[pl.ds(slot, 1), :]

    def apply(tile, token):
        rows = rows_at(tile * HALO, HALO)
        states = local_ref[rows, :] + cum_ref[rows, :] * carry
        state_ref[rows, :] = states.astype(bf16)
        mixed_ref[rows, :] = (states * gelu_parts(branch_ref[rows, :])[0]).astype(bf16)
        return token

    lax.fori_loop(0, OWN // HALO, apply, 0, unroll=2)


def reverse_scan(rows, later, gated, grad_ref, rate_ref, place_ref, soft_ref, row_ids):
    sgrad = grad_ref[rows, :] * gated
    keeps = jnp.exp(-soft_ref[...] * rate_ref[rows, :])
    coeff = jnp.where(place_ref[rows, :] == 0, 0.0, keeps)
    value = coeff * sgrad
    for distance in (1, 2, 4):
        reach = row_ids < 8 - distance
        value = value + coeff * jnp.where(reach, pltpu.roll(value, 8 - distance, 0), 0.0)
        coeff = coeff * jnp.where(reach, pltpu.roll(coeff, 8 - distance, 0), 1.0)
    return value + coeff * later, sgrad, coeff, keeps


def local_backward_kernel(
    soft_ref,
    grad_ref,
    branch_ref,
    state_ref,
    rate_ref,
    place_ref,
    bgrad_ref,
    edge_ref,
):
    slot = pl.program_id(0)
    channels = grad_ref.shape[1]
    row_ids = lax.broadcasted_iota(jnp.int32, (8, channels), 0)

    def scan(step, carry):
        base = OWN - HALO - step * HALO
        cum, later = carry
        slopes = []
        states = state_ref[rows_at(base, HALO), :].astype(f32)
        for part in (1, 0):
            rows = rows_at(base + 8 * part, 8)
            gated, slope = gelu_parts(branch_ref[rows, :])
            slopes.append(slope * grad_ref[rows, :] * states[8 * part : 8 * part + 8])
            held, _, coeff, _ = reverse_scan(
                rows, later, gated, grad_ref, rate_ref, place_ref, soft_ref, row_ids
            )
            cum, later = coeff[0:1] * cum, held[0:1]
        bgrad_ref[rows_at(base, HALO), :] = jnp.concatenate(slopes[::-1], axis=0).astype(bf16)
        return cum, later

    start = (jnp.ones((1, channels), f32), jnp.zeros((1, channels), f32))
    coeff, value = lax.fori_loop(0, OWN // HALO, scan, start, unroll=2)
    edge_ref[pl.ds(slot, 1), :] = coeff
    edge_ref[pl.ds(slot + MEMBERS, 1), :] = value


def finish_backward_kernel(
    spot_ref,
    piece0,
    piece1,
    piece2,
    piece3,
    prefix_ref,
    carry_ref,
    soft_ref,
    taps_ref,
    gates_ref,
    grad_ref,
    branch_ref,
    state_ref,
    conv_ref,
    rate_ref,
    entry_ref,
    place_ref,
    ci_ref,
    halo_ref,
    pregrad_ref,
    igrad_ref,
    owed_ref,
    sums_ref,
    cgrad_ref,
    back_ref,
    held_ref,
):
    slot = pl.program_id(0)
    channels = conv_ref.shape[1]

    @pl.when(slot == 0)
    def begin():
        pieces = (piece0, piece1, piece2, piece3)
        carries = slot_carries(True, spot_ref, pieces, prefix_ref, held_ref)
        back_ref[...] = jnp.concatenate(carries, axis=0)
        sums_ref[...] = jnp.zeros_like(sums_ref)

    row_ids = lax.broadcasted_iota(jnp.int32, (8, channels), 0)
    back = back_ref[pl.ds(slot, 1), :]
    ahead_first = carry_ref[pl.ds(slot, 1), :]

    def gate_grads(step, carry):
        later, logit_sum, rate_sum, entry_sum = carry
        base = OWN - HALO - step * HALO
        low_rate, low_entry = [], []
        both = rows_at(base, HALO)
        states, convs = state_ref[both, :].astype(f32), conv_ref[both, :].astype(f32)
        all_entries = entry_ref[both, :].astype(f32)
        before = state_ref[rows_at(jnp.maximum(base - HALO, 0), HALO), :].astype(f32)[HALO - 1 :]
        before = jnp.where(base == 0, ahead_first, before)
        for part in (1, 0):
            first = base + 8 * part
            rows = rows_at(first, 8)
            gated, _ = gelu_parts(branch_ref[rows, :])
            held, sgrad, _, keeps = reverse_scan(
                rows, later, gated, grad_ref, rate_ref, place_ref, soft_ref, row_ids
            )
            adjoint = sgrad + jnp.where(row_ids == 7, later, pltpu.roll(held, 7, 0))
            later = held[0:1]
            half = slice(8 * part, 8 * part + 8)
            ahead = states[7:8] if part else before
            previous = jnp.where(row_ids == 0, ahead, pltpu.roll(states[half], 1, 0))
            rates, entries, conv = rate_ref[rows, :], all_entries[half], convs[half]
            resets = place_ref[rows, :] == 0
            log_keep = -soft_ref[...] * rates
            squared = one_minus_square(keeps, 2.0 * log_keep)
            inverse = inverse_root(squared)
            scaling = jnp.where(resets, 1.0, squared * inverse)
            turn = jnp.where(resets, 0.0, (1.0 - squared) * inverse)
            weighed = adjoint * entries
            log_grad = held * previous - weighed * conv * turn
            rate_part = log_grad * rates
            logit_sum = logit_sum + rate_part
            rate_grad = -soft_ref[...] * rate_part * (1.0 - rates)
            direct = weighed * scaling
            entry_grad = direct * conv * (1.0 - entries)
            rate_sum = rate_sum + rate_grad
            entry_sum = entry_sum + entry_grad
            cgrad_ref[rows, :] = direct
            low_rate.append(rate_grad)
            low_entry.append(entry_grad)
        rows = rows_at(base, HALO)
        pregrad_ref[rows, :channels] = jnp.concatenate(low_rate[::-1], axis=0).astype(bf16)
        pregrad_ref[rows, channels:] = jnp.concatenate(low_entry[::-1], axis=0).astype(bf16)
        return later, logit_sum, rate_sum, entry_sum

    zero = jnp.zeros((8, channels), f32)
    _, logit_sum, rate_sum, entry_sum = lax.fori_loop(
        0, OWN // HALO, gate_grads, (back, zero, zero, zero), unroll=2
    )
    for step in range(0, channels, 128):
        columns = slice(step, step + 128)
        cgrad_ref[:, columns] += lax.dot_general(
            pregrad_ref[...],
            gates_ref[columns, :],
            (((1,), (1,)), ((), ())),
            preferred_element_type=f32,
        )

    def spread(tile):
        at = slice(tile * HALO, (tile + 1) * HALO)
        rows, places = cgrad_ref[at, :], place_ref[at, :]
        return [rows] + [jnp.where(places >= tap, rows, 0.0) for tap in range(1, CONV)]

    def shifted_sum(current, following):
        total = taps_ref[0:1, :] * current[0]
        for tap in range(1, CONV):
            both = jnp.concatenate([current[tap], following[tap]], axis=0)
            total = total + taps_ref[tap : tap + 1, :] * pltpu.roll(both, 2 * HALO - tap, 0)[:HALO]
        return total

    nothing = [jnp.zeros((HALO, channels), f32)] * CONV
    shift_sum, tap_sums = nothing[0], list(nothing)
    tiles = OWN // HALO
    coming = spread(0)
    owed_ref[...] = shifted_sum(nothing, coming)
    for tile in range(tiles):
        grads, coming = coming, spread(tile + 1) if tile + 1 < tiles else nothing
        igrad_ref[tile * HALO : (tile + 1) * HALO, :] = shifted_sum(grads, coming)
        inputs = conv_rows(ci_ref, halo_ref, tile)
        shift_sum = shift_sum + grads[0]
        tap_sums[0] = tap_sums[0] + grads[0] * inputs[HALO:]
        for tap in range(1, CONV):
            tap_sums[tap] = tap_sums[tap] + grads[tap] * pltpu.roll(inputs, tap, 0)[HALO:]

    def total_rows(values):
        return jnp.sum(values, axis=0, keepdims=True)

    sums_ref[...] += jnp.concatenate(
        [total_rows(v) for v in [shift_sum, rate_sum, entry_sum, logit_sum] + tap_sums], axis=0
    )


def in_hbm(values):
    return pltpu.with_memory_space_constraint(values, pltpu.HBM)


def by_slot(kernel, outs, ins, scratch, scalars, moved, far_outs=None):
    whole = [pl.BlockSpec(a.shape, lambda i, n=a.ndim: (0,) * n) for a in ins if not isinstance(a, tuple)]
    parts = [
        pl.BlockSpec((rows, a.shape[1]), lambda i, first=first: (first + i, 0))
        for a, rows, first in (a for a in ins if isinstance(a, tuple))
    ]
    out_specs = [
        pl.BlockSpec(shape, lambda i: (0, 0))
        if rows is None
        else pl.BlockSpec((rows, shape[1]), lambda i: (i, 0))
        for rows, shape, _ in outs
    ]
    return pl.pallas_call(
        kernel,
        grid=(MEMBERS,),
        in_specs=[pl.BlockSpec(memory_space=pltpu.SMEM)] * len(scalars) + whole + parts,
        out_specs=out_specs,
        out_shape=[
            pltpu.HBM(shape, dtype) if far else jax.ShapeDtypeStruct(shape, dtype)
            for (_, shape, dtype), far in zip(outs, far_outs or [False] * len(outs))
        ],
        scratch_shapes=[pltpu.VMEM(shape, dtype) for shape, dtype in scratch],
        compiler_params=pltpu.CompilerParams(vmem_limit_bytes=16 * 1024 * 1024),
        cost_estimate=pl.CostEstimate(flops=0, bytes_accessed=moved, transcendentals=0),
    )(*scalars, *[a[0] if isinstance(a, tuple) else a for a in ins])


def in_vmem(kernel, outs, scratch=(), scalars=0, count=1, moved=0):
    vmem = pl.BlockSpec(memory_space=pltpu.VMEM)
    smem = pl.BlockSpec(memory_space=pltpu.SMEM)
    return pl.pallas_call(
        kernel,
        out_shape=[jax.ShapeDtypeStruct(shape, dtype) for shape, dtype in outs],
        in_specs=[smem] * scalars + [vmem] * count,
        out_specs=[vmem] * len(outs),
        scratch_shapes=[pltpu.VMEM(shape, dtype) for shape, dtype in scratch],
        compiler_params=pltpu.CompilerParams(vmem_limit_bytes=16 * 1024 * 1024),
        cost_estimate=pl.CostEstimate(flops=0, bytes_accessed=moved, transcendentals=0),
    )


def exchange_edges(edges, spots, backward):
    channels = edges.shape[1]
    near = jnp.stack([edges, hop(edges, "core", 1)])
    total, prefix = in_vmem(
        functools.partial(fold_near_kernel, backward),
        [((8, channels), f32)] * 2,
        [((4, 2, 8, channels), f32)],
        scalars=1,
        count=4,
        moved=3_000_000,
    )(spots, *direct_gather(near, "z"))
    return direct_gather(total, "y") + [prefix], near


def outer_kernel(lhs_one, lhs_two, rhs_one, rhs_two, rhs_three, out_ref):
    def settle(lhs, rhs):
        out_ref[...] = lax.dot_general(
            lhs[...], rhs[...], (((0,), (0,)), ((), ())), preferred_element_type=f32
        ).astype(bf16)

    for step, (lhs, rhs) in enumerate(
        ((lhs_one, rhs_one), (lhs_one, rhs_two), (lhs_two, rhs_three))
    ):
        pl.when(pl.program_id(0) == step)(functools.partial(settle, lhs, rhs))


def feed_outer(lhs_one, lhs_two, rhs):
    rows, features = lhs_one.shape
    columns = rhs[0].shape[1]
    height = 1024
    whole = pl.BlockSpec(
        (rows, columns), lambda j, i: (0, 0), pipeline_mode=pl.Buffered(buffer_count=1)
    )
    return pl.pallas_call(
        outer_kernel,
        grid=(3, features // height),
        in_specs=[
            pl.BlockSpec((rows, height), lambda j, i: (0, jnp.where(j < 2, i, 0))),
            pl.BlockSpec((rows, height), lambda j, i: (0, jnp.where(j < 2, 0, i))),
            whole,
            whole,
            whole,
        ],
        out_specs=pl.BlockSpec((height, columns), lambda j, i: (i, j)),
        out_shape=pltpu.HBM((features, 3 * columns), bf16),
        compiler_params=pltpu.CompilerParams(vmem_limit_bytes=26 * 1024 * 1024),
        cost_estimate=pl.CostEstimate(
            flops=6 * rows * features * columns,
            bytes_accessed=6 * features * columns,
            transcendentals=0,
        ),
    )(lhs_one, lhs_two, *rhs)


def small_kernel(cut, conv_ref, pregrad_ref, sums_ref, extra_ref, out_ref):
    channels = conv_ref.shape[1]
    width = 2 * channels
    block = cut * TOKS
    dense = lax.dot_general(
        conv_ref[...],
        pregrad_ref[...],
        (((0,), (0,)), ((), ())),
        preferred_element_type=f32,
    )
    columns = lax.broadcasted_iota(jnp.int32, (block, width), 1)
    columns = jnp.where(columns >= channels, columns - channels, columns)
    gates = jnp.zeros((block, width), f32)
    for group in range(channels // block):
        inside = (columns >= group * block) & (columns < (group + 1) * block)
        gates = jnp.where(inside, dense[group * block : (group + 1) * block], gates)
    own = channels // TOKS
    sums = sums_ref[...]
    blank = jnp.zeros((4, channels - 256), f32)
    spare = jnp.zeros((SMALL - 2 * cut - 5, channels), f32)
    for tok in range(TOKS):
        rows = gates[tok * cut : (tok + 1) * cut]
        turned_sums = pltpu.roll(sums, channels - tok * own, 1) if tok else sums
        vectors = [turned_sums[:4, :128], turned_sums[4:, :128], blank]
        pieces = [rows[:, :channels], rows[:, channels:], jnp.concatenate(vectors, axis=1)]
        pieces += [extra_ref[tok : tok + 1, :], spare]
        out_ref[tok] = jnp.concatenate(pieces, axis=0).astype(bf16)


def halves_kernel(count, small, spot_ref, *refs):
    core = spot_ref[3]
    small_ref, refs = (refs[0], refs[1:]) if small else (None, refs)
    mine_ref, theirs_ref = refs[2 * count :]
    chips, rows, _ = mine_ref.shape
    rows = (rows - small) // count
    for which in range(count):
        sums = lax.dot_general(
            refs[which][...],
            refs[count + which][...],
            (((0,), (0,)), ((), ())),
            preferred_element_type=f32,
        )
        for chip in range(chips):
            low = sums[2 * chip * rows : (2 * chip + 1) * rows]
            high = sums[(2 * chip + 1) * rows : (2 * chip + 2) * rows]
            at = slice(which * rows, (which + 1) * rows)
            mine_ref[chip, at, :] = jnp.where(core == 0, low, high).astype(bf16)
            theirs_ref[chip, at, :] = jnp.where(core == 0, high, low).astype(bf16)
    for chip in range(chips if small else 0):
        low, high = small_ref[2 * chip].astype(f32), small_ref[2 * chip + 1].astype(f32)
        at = slice(count * rows, count * rows + small)
        mine_ref[chip, at, :] = jnp.where(core == 0, low, high).astype(bf16)
        theirs_ref[chip, at, :] = jnp.where(core == 0, high, low).astype(bf16)


def outer_halves(spots, small, lhs, rhs, part):
    count = len(lhs)
    rows, columns = rhs[0].shape
    height = 1024
    chips = height // 128
    extra = SMALL if small is not None else 0
    total = 64 * count + extra
    shape = jax.ShapeDtypeStruct((chips, total, columns), bf16)
    out_spec = pl.BlockSpec((chips, total, columns), lambda i: (0, 0, 0))
    return pl.pallas_call(
        functools.partial(halves_kernel, count, extra),
        grid=(1,),
        in_specs=[pl.BlockSpec(memory_space=pltpu.SMEM)]
        + [pl.BlockSpec((2 * chips, SMALL, columns), lambda i: (part, 0, 0))] * (extra > 0)
        + [pl.BlockSpec((rows, height), lambda i: (0, part))] * count
        + [pl.BlockSpec((rows, columns), lambda i: (0, 0))] * count,
        out_specs=[out_spec] * 2,
        out_shape=[shape] * 2,
        compiler_params=pltpu.CompilerParams(vmem_limit_bytes=28 * 1024 * 1024),
        cost_estimate=pl.CostEstimate(
            flops=2 * count * rows * height * columns,
            bytes_accessed=0,
            transcendentals=0,
        ),
    )(spots, *([small] if extra else []), *lhs, *rhs)


def per_device(
    inputs,
    mix_scale,
    branch_mat,
    input_mat,
    conv_taps,
    conv_shift,
    rate_mat,
    rate_shift,
    entry_mat,
    entry_shift,
    decay_logit,
    out_mat,
    feed_scale,
    gate_mat,
    up_mat,
    down_mat,
    lengths,
    cotangent,
):
    blk = lax.axis_index("blk")
    tok = lax.axis_index("tok")
    spot = (tok // 8, (tok // 2) % 4, tok % 2)
    spots = jnp.stack([tok] + list(spot)).astype(jnp.int32)
    channels = branch_mat.shape[1]
    hidden_units = gate_mat.shape[1]
    slice_rows = branch_mat.shape[0]
    total_rows = MEMBERS * OWN

    groups, cut, block = rate_mat.shape
    own_channels = conv_shift.shape[0]
    vectors = [conv_taps, conv_shift[None], rate_shift[None], entry_shift[None], decay_logit[None]]
    vectors = jnp.concatenate(vectors, axis=0).reshape(-1)
    extras = jnp.concatenate([vectors, mix_scale, feed_scale])
    extras = jnp.pad(extras, (0, channels - extras.shape[0]))[None]
    smalls = [jnp.moveaxis(mats, 0, 1).reshape(cut, channels) for mats in (rate_mat, entry_mat)]
    smalls = jnp.concatenate(smalls + [extras], axis=0)
    smalls = jnp.pad(smalls, ((0, HALO - smalls.shape[0]), (0, 0)))
    input_blocks = ring_gather(inputs, spot[2])
    near = after(small_gather(smalls, (input_blocks[1], input_blocks[3])), input_blocks[2])
    for axis, place in ((2, spot[2]), (1, spot[1]), (0, spot[0])):
        near = jnp.roll(near, place, axis)
    near = near.reshape(TOKS, HALO, channels)
    mixer_all = lax.all_gather(
        jnp.concatenate([input_mat, branch_mat, out_mat.T], axis=1), "tok", axis=0, tiled=True
    )
    devices = MEMBERS * TOKS
    tail = lax.ppermute(
        inputs[OWN - HALO :], ("blk", "tok"), [(i, (i + 1) % devices) for i in range(devices)]
    )
    cotangent_blocks = ring_gather(after(cotangent, input_blocks[2]), spot[2])
    rows_all = jnp.concatenate(input_blocks + direct_gather(tail), axis=0)
    cotangent_all = jnp.concatenate(cotangent_blocks, axis=0)

    extras = near[:, 2 * cut]
    vectors = extras[:, : 8 * own_channels].reshape(TOKS, 8, own_channels).astype(f32)
    vectors = jnp.moveaxis(vectors, 0, 1).reshape(8, channels)
    gains = extras[:, 8 * own_channels : 8 * own_channels + 2 * slice_rows].astype(f32)
    mix_gain = gains[:, :slice_rows].reshape(1, -1)
    feed_gain = gains[:, slice_rows:].reshape(1, -1)
    wide_values = rows_all.astype(f32)
    wide_one = (wide_values * norm_factor(wide_values) * mix_gain).astype(bf16)
    taps, shift = vectors[:CONV], vectors[4:5]
    bias = jnp.concatenate([vectors[5:6], vectors[6:7]], axis=1)
    soft = decay_power * jax.nn.softplus(-vectors[7:8])
    blocks = [near[:, i * cut : (i + 1) * cut].reshape(block, channels) for i in range(2)]
    blocks = after(jnp.concatenate(blocks, axis=1), cotangent_blocks[2])
    feed_own = jnp.concatenate([gate_mat, up_mat, down_mat.T], axis=1)
    feed_all = lax.all_gather(after(feed_own, wide_one, blocks), "tok", axis=0, tiled=True)
    gate_up_all = feed_all[:, : 2 * hidden_units]
    down_turned = feed_all[:, 2 * hidden_units :]
    own_one = wide_one[:total_rows]
    input_all = mixer_all[:, :channels]
    branch_all = mixer_all[:, channels : 2 * channels]
    project_all = mixer_all[:, : 2 * channels]
    out_turned = mixer_all[:, 2 * channels : 3 * channels]

    slots = (blk + jnp.arange(MEMBERS, dtype=jnp.int32)) % MEMBERS
    token_ids = (
        (slots * TOKS + tok)[:, None] * OWN + jnp.arange(OWN, dtype=jnp.int32)[None, :]
    ).reshape(-1)
    starts = jnp.cumsum(lengths) - lengths
    opened = jnp.max(jnp.where(starts[None, :] <= token_ids[:, None], starts[None, :], 0), axis=1)
    places = (token_ids - opened).reshape(total_rows, 1).astype(jnp.int32)

    conv_input = product(wide_one, input_all, bf16)
    branch = product(own_one, branch_all)
    halo_first = total_rows // HALO
    conv, rates, entries, local, cum, edges, gates = by_slot(
        local_forward_kernel,
        [(OWN, (total_rows, channels), kind) for kind in (bf16, f32, bf16, f32, f32)]
        + [(None, (8, channels), f32), (None, (channels, 2 * channels), bf16)],
        [
            taps,
            shift,
            blocks,
            bias,
            soft,
            (conv_input, OWN, 0),
            (conv_input, HALO, halo_first),
            (places, OWN, 0),
        ],
        [((OWN, 2 * channels), f32), ((OWN, channels), f32)],
        (),
        30_000_000,
        [True, True, True, False, False, False, True],
    )
    conv, rates, entries, gates = [in_hbm(a) for a in (conv, rates, entries, gates)]
    chains, _ = exchange_edges(edges, spots, False)
    states, mixture, carried = by_slot(
        mix_kernel,
        [
            (OWN, (total_rows, channels), bf16),
            (OWN, (total_rows, channels), bf16),
            (None, (MEMBERS, channels), f32),
        ],
        [*chains] + [(a, OWN, 0) for a in (local, cum, branch)],
        [((4, 8, channels), f32)],
        (spots,),
        4_500_000,
    )

    def rows_of(values):
        return [values[j * OWN : (j + 1) * OWN] for j in range(MEMBERS)]

    own_values = inputs.astype(f32)
    middle = own_values + ring_scatter(rows_of(product_back(mixture, out_turned, bf16)), spot[2])

    factor_two = norm_factor(middle)
    normed_two = (middle * factor_two * feed_gain).astype(bf16)
    hidden_grad = product(after(cotangent_all, mixture), down_turned)
    blocks_two = ring_gather(normed_two, spot[2])
    blocks_two[2] = after(blocks_two[2], hidden_grad)
    wide_two = jnp.concatenate(blocks_two, axis=0)
    gate_up = product(wide_two, gate_up_all)
    gate_pre, up_pre = gate_up[:, :hidden_units], gate_up[:, hidden_units:]
    gate_act, gate_slope = gelu_parts(gate_pre)
    hidden = (gate_act * up_pre).astype(bf16)
    gate_grad = (gate_slope * hidden_grad * up_pre).astype(bf16)
    up_grad = (gate_act * hidden_grad).astype(bf16)
    feed_shares = feed_outer(wide_two, cotangent_all, (gate_grad, up_grad, hidden))
    feed_grads = lax.psum_scatter(feed_shares, "tok", scatter_dimension=0, tiled=True)
    gate_late, up_late = after((gate_grad, up_grad), feed_shares)
    two_shares = product_back(jnp.concatenate([gate_late, up_late], axis=1), gate_up_all, bf16)
    two_parts = rows_of(two_shares)
    two_far, two_near = ring_open(two_parts, spot[2])
    two_grad = ring_close(two_parts, two_near, ring_pass(two_parts, two_far, spot[2]))
    middle_grad = cotangent.astype(f32) + normalize_back(two_grad, middle, factor_two, feed_gain)
    grad_feed_scale = jnp.sum(two_grad * middle * factor_two, axis=0)
    layer_shares = product_back(after(hidden, two_far), down_turned, bf16)
    middle_blocks = ring_gather(middle_grad.astype(bf16), spot[2])
    middle_blocks[2] = after(middle_blocks[2], layer_shares)
    middle_wide = jnp.concatenate(middle_blocks, axis=0)
    mixture_grad = product(middle_wide, out_turned)
    branch = in_hbm(branch)
    branch_grad, back_edges = by_slot(
        local_backward_kernel,
        [(OWN, (total_rows, channels), bf16), (None, (8, channels), f32)],
        [soft] + [(a, OWN, 0) for a in (mixture_grad, branch, states, rates, places)],
        (),
        (),
        9_500_000,
    )
    chains_back, near_back = exchange_edges(back_edges, spots, True)
    pregrads, igrad, owed, sums = by_slot(
        finish_backward_kernel,
        [
            (OWN, (total_rows, 2 * channels), bf16),
            (OWN, (total_rows, channels), f32),
            (HALO, (MEMBERS * HALO, channels), f32),
            (None, (8, channels), f32),
        ],
        [*chains_back, carried, soft, taps, gates]
        + [(a, OWN, 0) for a in (mixture_grad, branch, states, conv, rates, entries)]
        + [(places, OWN, 0), (conv_input, OWN, 0), (conv_input, HALO, halo_first)],
        [
            ((OWN, channels), f32),
            ((MEMBERS, channels), f32),
            ((4, 8, channels), f32),
        ],
        (spots,),
        40_000_000,
    )
    returned = lax.ppermute(
        owed.reshape(MEMBERS, HALO, channels)[:, HALO - 3 :],
        "tok",
        [(i, (i - 1) % TOKS) for i in range(TOKS)],
    )
    turned_on = jnp.concatenate([returned[1:], returned[:1]], axis=0)
    landing = jnp.where(tok == TOKS - 1, turned_on, returned)
    input_grad = igrad.reshape(MEMBERS, OWN, channels) + jnp.pad(
        landing, ((0, 0), (OWN - 3, 0), (0, 0))
    )
    input_low = input_grad.reshape(total_rows, channels).astype(bf16)
    feed_rows = jnp.pad(
        grad_feed_scale.reshape(TOKS, slice_rows), ((0, 0), (0, channels - slice_rows))
    )
    (small_rows,) = in_vmem(
        functools.partial(small_kernel, cut),
        [((TOKS, SMALL, channels), bf16)],
        count=4,
        moved=11_000_000,
    )(conv, pregrads, sums, feed_rows)

    core = spot[2]
    chips_one, chips_two = [
        outer_halves(
            spots, small_rows, (middle_wide, wide_one, wide_one), (mixture, branch_grad, low), part
        )
        for part, low in enumerate((input_low, input_low))
    ]
    other_one = hop(chips_one[1], "core", 1)
    other_two = hop(chips_two[1], "core", 1)
    late = after(input_low, chips_two[1])
    one_shares = product_back(jnp.concatenate([late, branch_grad], axis=1), project_all, bf16)
    weight_chip = jnp.concatenate(
        [narrow_sum(chips_one[0], other_one), narrow_sum(chips_two[0], other_two)], axis=0
    )
    one_shares = after(one_shares, weight_chip)
    one_parts = rows_of(one_shares)
    one_grad = ring_scatter(one_parts, core)
    factor_one = norm_factor(own_values)
    first_grad = normalize_back(one_grad, own_values, factor_one, mix_gain)
    inputs_grad = (middle_grad + first_grad).astype(bf16)
    settled = chips_sum(weight_chip)
    layer_out = middle + ring_scatter(rows_of(after(layer_shares, one_grad)), core)
    grad_out, grad_branch, grad_input = [
        settled[i * slice_rows : (i + 1) * slice_rows] for i in range(3)
    ]
    settled = settled[3 * slice_rows :]
    grad_mix_scale = jnp.sum(
        grad_branch * branch_mat.astype(f32) + grad_input * input_mat.astype(f32), axis=1
    ) / mix_scale.astype(f32)
    gains_own = jnp.concatenate([grad_mix_scale, settled[2 * cut + 4, :slice_rows]])
    gains_own = hop_sum(gains_own.reshape(1, -1), "blk")[0]
    gate_own = [
        jnp.moveaxis(settled[i * cut : (i + 1) * cut].reshape(cut, groups, block), 1, 0)
        for i in range(2)
    ]
    sums_own = settled[2 * cut : 2 * cut + 4]
    taps_own = sums_own[:, 128 : 128 + own_channels]
    sums_own = sums_own[:, :own_channels]
    own_logits = decay_logit.astype(f32)
    return (
        layer_out.astype(bf16),
        inputs_grad,
        gains_own[:slice_rows],
        grad_branch,
        grad_input,
        taps_own,
        sums_own[0],
        gate_own[0],
        sums_own[1],
        gate_own[1],
        sums_own[2],
        sums_own[3] * decay_power * jax.nn.sigmoid(-own_logits),
        grad_out.T,
        gains_own[slice_rows : 2 * slice_rows],
        feed_grads[:, :hidden_units].astype(f32),
        feed_grads[:, hidden_units : 2 * hidden_units].astype(f32),
        feed_grads[:, 2 * hidden_units :].T.astype(f32),
    )


def solution(mesh):
    in_specs = (
        P(("blk", "tok"), None),
        P("tok"),
        P("tok", "blk"),
        P("tok", "blk"),
        P(None, ("blk", "tok")),
        P(("blk", "tok")),
        P("blk", "tok", None),
        P(("blk", "tok")),
        P("blk", "tok", None),
        P(("blk", "tok")),
        P(("blk", "tok")),
        P("blk", "tok"),
        P("tok"),
        P("tok", "blk"),
        P("tok", "blk"),
        P("blk", "tok"),
        P(),
        P(("blk", "tok"), None),
    )
    out_specs = (
        P(("blk", "tok"), None),
        P(("blk", "tok"), None),
        P("tok"),
        P("tok", "blk"),
        P("tok", "blk"),
        P(None, ("blk", "tok")),
        P(("blk", "tok")),
        P("blk", "tok", None),
        P(("blk", "tok")),
        P("blk", "tok", None),
        P(("blk", "tok")),
        P(("blk", "tok")),
        P("blk", "tok"),
        P("tok"),
        P("tok", "blk"),
        P("tok", "blk"),
        P("blk", "tok"),
    )
    return jax.shard_map(
        per_device, mesh=mesh, in_specs=in_specs, out_specs=out_specs, check_vma=False
    )
```

```python
import functools

import jax
import jax.numpy as jnp
from jax import lax
from jax.experimental import pallas as pl
from jax.experimental.pallas import tpu as pltpu
from jax.sharding import PartitionSpec as P

CONV = 4
MEMBERS = 4
TOKS = 32
OWN = 128
HALO = 16
SMALL = 16
FIRST = 104

eps_norm = 1e-06
decay_power = 8.0
f32 = jnp.float32
bf16 = jnp.bfloat16


def hop_blk(values, distance):
    return lax.ppermute(
        values, "blk", [(i, (i + distance) % MEMBERS) for i in range(MEMBERS)]
    )


def hop_tok(values, axis, distance):
    route = []
    for y in range(4):
        for z in range(4):
            for c in range(2):
                if axis == "y":
                    to = ((y + distance) % 4, z, c)
                elif axis == "z":
                    to = (y, (z + distance) % 4, c)
                else:
                    to = (y, z, (c + distance) % 2)
                route.append((y * 8 + z * 2 + c, to[0] * 8 + to[1] * 2 + to[2]))
    return lax.ppermute(values, "tok", route)


def hop(values, axis, distance):
    if axis == "blk":
        return hop_blk(values, distance)
    return hop_tok(values, axis, distance)


def hop_apart(values, distance, axis="blk"):
    route = []
    for b in range(MEMBERS):
        for t in range(TOKS):
            step = distance if t % 2 == 0 else -distance
            place = {"blk": b, "y": t // 8, "z": t // 2 % 4}
            place[axis] = (place[axis] + step) % 4
            to = place["blk"] * TOKS + place["y"] * 8 + place["z"] * 2 + t % 2
            route.append((b * TOKS + t, to))
    return lax.ppermute(values, ("blk", "tok"), route)


def either(core, first, second):
    return jnp.where(core == 0, first, second)


def ring_gather(values, core, before_last=()):
    behind = hop_apart(values, 1)
    ahead = hop_apart(values, -1)
    far = hop_apart(after(behind, *before_last), 1)
    return [values, either(core, ahead, behind), far, either(core, behind, ahead)]


def ring_open(parts, core, axis="blk"):
    return hop_apart(parts[2].astype(bf16), 1, axis), ring_near(parts, core, axis)


def ring_near(parts, core, axis="blk"):
    return hop_apart(either(core, parts[3], parts[1]).astype(bf16), -1, axis)


def ring_pass(parts, far, core, axis="blk"):
    onward = either(core, parts[1], parts[3]).astype(f32) + far.astype(f32)
    return hop_apart(onward.astype(bf16), 1, axis)


def ring_close(parts, near, joined):
    return parts[0].astype(f32) + near.astype(f32) + joined.astype(f32)


def ring_scatter(parts, core, axis="blk"):
    far, near = ring_open(parts, core, axis)
    return ring_close(parts, near, ring_pass(parts, far, core, axis))


def direct_scatter(parts, axis):
    total = parts[0].astype(f32)
    for distance in range(1, 4):
        total = total + hop(parts[distance], axis, distance).astype(f32)
    return total


def narrow_sum(left, right):
    return (left.astype(f32) + right.astype(f32)).astype(bf16)


def after(value, *others):
    return lax.optimization_barrier((value,) + others)[0]


def hop_sum(values, axis):
    return values + hop(values, axis, 1) + hop(values, axis, -1) + hop(values, axis, 2)


def direct_gather(values, axis="blk"):
    return [values] + [hop(values, axis, -d) for d in range(1, 4)]


def turned(values, place, axis=0):
    return [
        lax.dynamic_index_in_dim(values, (place + j) % 4, axis, keepdims=False) for j in range(4)
    ]


def swap_sum(parts, core):
    mine = lax.dynamic_index_in_dim(parts, core, 1, keepdims=False)
    theirs = lax.dynamic_index_in_dim(parts, 1 - core, 1, keepdims=False)
    return narrow_sum(mine, hop(theirs, "core", 1))


def chip_sum(values, core):
    return swap_sum(values.reshape(16, 2, -1, values.shape[1]), core)


def chips_sum(values):
    cores = [[2 * i + c for i in range(16)] for c in range(2)]
    terms = lax.all_to_all(values, "tok", 0, 0, axis_index_groups=cores, tiled=True)
    return jnp.sum(terms.astype(f32), axis=0)


def together(*values):
    return lax.optimization_barrier(values)


def small_gather(values, before_last):
    values = jnp.stack([values, hop(values, "core", 1)])
    values = jnp.stack(direct_gather(values, "z"))
    return jnp.stack(direct_gather(after(values, *before_last), "y"))


def product(operand, weight, out=f32):
    return jnp.dot(operand, weight, preferred_element_type=f32).astype(out)


def product_back(operand, weight, out=f32):
    return lax.dot_general(
        operand, weight, (((1,), (1,)), ((), ())), preferred_element_type=f32
    ).astype(out)


def product_outer(operand, weight, out=bf16):
    return lax.dot_general(
        operand, weight, (((0,), (0,)), ((), ())), preferred_element_type=f32
    ).astype(out)


def norm_factor(values):
    return lax.rsqrt(jnp.mean(values * values, axis=1, keepdims=True) + eps_norm)


def normalize_back(gradient, values, factor, gains):
    weighted = gradient * gains
    return factor * weighted - values * (factor * factor * factor) * jnp.mean(
        weighted * values, axis=1, keepdims=True
    )


def sigmoid(values):
    return 1.0 / (1.0 + jnp.exp(-values))


def one_minus_square(keeps, values):
    series = 1.0 + values * (1.0 / 6.0)
    for order in (5.0, 4.0, 3.0, 2.0):
        series = 1.0 + values * series * (1.0 / order)
    return jnp.where(values > -0.1, -values * series, 1.0 - keeps * keeps)


def inverse_root(values):
    return lax.rsqrt(jnp.maximum(values, 1e-37))


def gelu_parts(values):
    root = 0.7978845608028654
    square = values * values
    bent = jnp.tanh(root * values * (1.0 + 0.044715 * square))
    half = 0.5 * (1.0 + bent)
    slope = half + 0.5 * values * (1.0 - bent * bent) * root * (1.0 + 3.0 * 0.044715 * square)
    return values * half, slope


def rows_at(start, size):
    return pl.ds(pl.multiple_of(start, size), size)


def conv_rows(ci_ref, halo_ref, tile):
    before = halo_ref[...] if tile == 0 else ci_ref[(tile - 1) * HALO : tile * HALO, :]
    here = ci_ref[tile * HALO : (tile + 1) * HALO, :]
    return jnp.concatenate([before.astype(f32), here.astype(f32)], axis=0)


def local_forward_kernel(
    taps_ref,
    shift_ref,
    blocks_ref,
    bias_ref,
    soft_ref,
    ci_ref,
    halo_ref,
    place_ref,
    conv_ref,
    rate_ref,
    entry_ref,
    local_ref,
    cum_ref,
    edge_ref,
    gates_ref,
    pre_ref,
    exact_ref,
):
    slot = pl.program_id(0)
    channels = conv_ref.shape[1]
    block = blocks_ref.shape[0]
    width = 2 * channels

    @pl.when(slot == 0)
    def spread_gates():
        columns = lax.broadcasted_iota(jnp.int32, (HALO, width), 1)
        columns = jnp.where(columns >= channels, columns - channels, columns)
        for group in range(channels // block):
            inside = (columns >= group * block) & (columns < (group + 1) * block)
            for step in range(0, block, HALO):
                rows = blocks_ref[step : step + HALO, :].astype(f32)
                at = group * block + step
                gates_ref[at : at + HALO, :] = jnp.where(inside, rows, 0.0).astype(bf16)

    for tile in range(OWN // HALO):
        at = slice(tile * HALO, (tile + 1) * HALO)
        rows = conv_rows(ci_ref, halo_ref, tile)
        places = place_ref[at, :]
        total = shift_ref[...] + taps_ref[0:1, :] * rows[HALO:]
        for tap in range(1, CONV):
            lagged = pltpu.roll(rows, tap, 0)[HALO:]
            total = total + taps_ref[tap : tap + 1, :] * jnp.where(places >= tap, lagged, 0.0)
        exact_ref[at, :] = total
        conv_ref[at, :] = total.astype(bf16)
    for step in range(0, width, 256):
        columns = slice(step, step + 256)
        pre_ref[:, columns] = (
            jnp.dot(conv_ref[...], gates_ref[:, columns], preferred_element_type=f32)
            + bias_ref[:, columns]
        )

    row_ids = lax.broadcasted_iota(jnp.int32, (8, channels), 0)

    def scan(step, carry):
        halves = []
        for part in range(2):
            rows = rows_at(step * HALO + 8 * part, 8)
            rates = sigmoid(pre_ref[rows, :channels])
            entries = 0.5 * jnp.tanh(0.5 * pre_ref[rows, channels:]) + 0.5
            log_keep = -soft_ref[...] * rates
            resets = place_ref[rows, :] == 0
            keeps = jnp.exp(log_keep)
            coeff = jnp.where(resets, 0.0, keeps)
            squared = one_minus_square(keeps, 2.0 * log_keep)
            scaling = jnp.where(resets, 1.0, squared * inverse_root(squared))
            value = entries * exact_ref[rows, :] * scaling
            for distance in (1, 2, 4):
                reach = row_ids >= distance
                value = value + coeff * jnp.where(reach, pltpu.roll(value, distance, 0), 0.0)
                coeff = coeff * jnp.where(reach, pltpu.roll(coeff, distance, 0), 1.0)
            value = value + coeff * carry[1]
            coeff = coeff * carry[0]
            rate_ref[rows, :] = rates
            local_ref[rows, :] = value
            cum_ref[rows, :] = coeff
            halves.append(entries)
            carry = coeff[7:8], value[7:8]
        entry_ref[rows_at(step * HALO, HALO), :] = jnp.concatenate(halves, axis=0).astype(bf16)
        return carry

    start = (jnp.ones((1, channels), f32), jnp.zeros((1, channels), f32))
    coeff, value = lax.fori_loop(0, OWN // HALO, scan, start, unroll=2)
    edge_ref[pl.ds(slot, 1), :] = coeff
    edge_ref[pl.ds(slot + MEMBERS, 1), :] = value


def extended(pair, block):
    return pair[0] * block[:4], block[:4] * pair[1] + block[4:]


def whole_chain(channels):
    return jnp.ones((4, channels), f32), jnp.zeros((4, channels), f32)


def fold_near_kernel(backward, spot_ref, *refs):
    pieces, (total_ref, prefix_ref, held_ref) = refs[:4], refs[4:]
    z, c = spot_ref[2], spot_ref[3]
    for distance, piece in enumerate(pieces):
        held_ref[distance] = piece[...]
    chain = whole_chain(total_ref.shape[1])
    prefix = chain
    for place in reversed(range(8)) if backward else range(8):
        here = place == 2 * z + c
        prefix = tuple(jnp.where(here, new, old) for new, old in zip(chain, prefix))
        distance = jnp.bitwise_and(place // 2 - z + 4, 3)
        chain = extended(chain, held_ref[distance, jnp.bitwise_xor(place % 2, c)])
    total_ref[...] = jnp.concatenate(chain, axis=0)
    prefix_ref[...] = jnp.concatenate(prefix, axis=0)


def slot_carries(backward, spot_ref, pieces, prefix_ref, held_ref):
    y = spot_ref[1]
    channels = prefix_ref.shape[1]
    for distance, piece in enumerate(pieces):
        held_ref[distance] = piece[...]
    total = whole_chain(channels)
    prefix = total
    for place in reversed(range(4)) if backward else range(4):
        here = place == y
        prefix = tuple(jnp.where(here, new, old) for new, old in zip(total, prefix))
        total = extended(total, held_ref[jnp.bitwise_and(place - y + 4, 3)])
    prefix = extended(prefix, prefix_ref[...])
    current = jnp.zeros((1, channels), f32)
    carries = [None] * MEMBERS
    for _ in range(2):
        for slot in reversed(range(MEMBERS)) if backward else range(MEMBERS):
            one = slice(slot, slot + 1)
            carries[slot] = prefix[0][one] * current + prefix[1][one]
            current = total[0][one] * current + total[1][one]
    return carries


def mix_kernel(
    spot_ref,
    piece0,
    piece1,
    piece2,
    piece3,
    prefix_ref,
    local_ref,
    cum_ref,
    branch_ref,
    state_ref,
    mixed_ref,
    carry_ref,
    held_ref,
):
    slot = pl.program_id(0)

    @pl.when(slot == 0)
    def begin():
        pieces = (piece0, piece1, piece2, piece3)
        carries = slot_carries(False, spot_ref, pieces, prefix_ref, held_ref)
        carry_ref[...] = jnp.concatenate(carries, axis=0)

    carry = carry_ref[pl.ds(slot, 1), :]

    def apply(tile, token):
        rows = rows_at(tile * HALO, HALO)
        states = local_ref[rows, :] + cum_ref[rows, :] * carry
        state_ref[rows, :] = states.astype(bf16)
        mixed_ref[rows, :] = (states * gelu_parts(branch_ref[rows, :])[0]).astype(bf16)
        return token

    lax.fori_loop(0, OWN // HALO, apply, 0, unroll=2)


def reverse_scan(rows, later, gated, grad_ref, rate_ref, place_ref, soft_ref, row_ids):
    sgrad = grad_ref[rows, :] * gated
    keeps = jnp.exp(-soft_ref[...] * rate_ref[rows, :])
    coeff = jnp.where(place_ref[rows, :] == 0, 0.0, keeps)
    value = coeff * sgrad
    for distance in (1, 2, 4):
        reach = row_ids < 8 - distance
        value = value + coeff * jnp.where(reach, pltpu.roll(value, 8 - distance, 0), 0.0)
        coeff = coeff * jnp.where(reach, pltpu.roll(coeff, 8 - distance, 0), 1.0)
    return value + coeff * later, sgrad, coeff, keeps


def local_backward_kernel(
    soft_ref,
    grad_ref,
    branch_ref,
    state_ref,
    rate_ref,
    place_ref,
    bgrad_ref,
    edge_ref,
):
    slot = pl.program_id(0)
    channels = grad_ref.shape[1]
    row_ids = lax.broadcasted_iota(jnp.int32, (8, channels), 0)

    def scan(step, carry):
        base = OWN - HALO - step * HALO
        cum, later = carry
        slopes = []
        states = state_ref[rows_at(base, HALO), :].astype(f32)
        for part in (1, 0):
            rows = rows_at(base + 8 * part, 8)
            gated, slope = gelu_parts(branch_ref[rows, :])
            slopes.append(slope * grad_ref[rows, :] * states[8 * part : 8 * part + 8])
            held, _, coeff, _ = reverse_scan(
                rows, later, gated, grad_ref, rate_ref, place_ref, soft_ref, row_ids
            )
            cum, later = coeff[0:1] * cum, held[0:1]
        bgrad_ref[rows_at(base, HALO), :] = jnp.concatenate(slopes[::-1], axis=0).astype(bf16)
        return cum, later

    start = (jnp.ones((1, channels), f32), jnp.zeros((1, channels), f32))
    coeff, value = lax.fori_loop(0, OWN // HALO, scan, start, unroll=2)
    edge_ref[pl.ds(slot, 1), :] = coeff
    edge_ref[pl.ds(slot + MEMBERS, 1), :] = value


def finish_backward_kernel(
    spot_ref,
    piece0,
    piece1,
    piece2,
    piece3,
    prefix_ref,
    carry_ref,
    soft_ref,
    taps_ref,
    gates_ref,
    grad_ref,
    branch_ref,
    state_ref,
    conv_ref,
    rate_ref,
    entry_ref,
    place_ref,
    ci_ref,
    halo_ref,
    pregrad_ref,
    igrad_ref,
    owed_ref,
    sums_ref,
    cgrad_ref,
    back_ref,
    held_ref,
):
    slot = pl.program_id(0)
    channels = conv_ref.shape[1]

    @pl.when(slot == 0)
    def begin():
        pieces = (piece0, piece1, piece2, piece3)
        carries = slot_carries(True, spot_ref, pieces, prefix_ref, held_ref)
        back_ref[...] = jnp.concatenate(carries, axis=0)
        sums_ref[...] = jnp.zeros_like(sums_ref)

    row_ids = lax.broadcasted_iota(jnp.int32, (8, channels), 0)
    back = back_ref[pl.ds(slot, 1), :]
    ahead_first = carry_ref[pl.ds(slot, 1), :]

    def gate_grads(step, carry):
        later, logit_sum, rate_sum, entry_sum = carry
        base = OWN - HALO - step * HALO
        low_rate, low_entry = [], []
        both = rows_at(base, HALO)
        states, convs = state_ref[both, :].astype(f32), conv_ref[both, :].astype(f32)
        all_entries = entry_ref[both, :].astype(f32)
        before = state_ref[rows_at(jnp.maximum(base - HALO, 0), HALO), :].astype(f32)[HALO - 1 :]
        before = jnp.where(base == 0, ahead_first, before)
        for part in (1, 0):
            first = base + 8 * part
            rows = rows_at(first, 8)
            gated, _ = gelu_parts(branch_ref[rows, :])
            held, sgrad, _, keeps = reverse_scan(
                rows, later, gated, grad_ref, rate_ref, place_ref, soft_ref, row_ids
            )
            adjoint = sgrad + jnp.where(row_ids == 7, later, pltpu.roll(held, 7, 0))
            later = held[0:1]
            half = slice(8 * part, 8 * part + 8)
            ahead = states[7:8] if part else before
            previous = jnp.where(row_ids == 0, ahead, pltpu.roll(states[half], 1, 0))
            rates, entries, conv = rate_ref[rows, :], all_entries[half], convs[half]
            resets = place_ref[rows, :] == 0
            log_keep = -soft_ref[...] * rates
            squared = one_minus_square(keeps, 2.0 * log_keep)
            inverse = inverse_root(squared)
            scaling = jnp.where(resets, 1.0, squared * inverse)
            turn = jnp.where(resets, 0.0, (1.0 - squared) * inverse)
            weighed = adjoint * entries
            log_grad = held * previous - weighed * conv * turn
            rate_part = log_grad * rates
            logit_sum = logit_sum + rate_part
            rate_grad = -soft_ref[...] * rate_part * (1.0 - rates)
            direct = weighed * scaling
            entry_grad = direct * conv * (1.0 - entries)
            rate_sum = rate_sum + rate_grad
            entry_sum = entry_sum + entry_grad
            cgrad_ref[rows, :] = direct
            low_rate.append(rate_grad)
            low_entry.append(entry_grad)
        rows = rows_at(base, HALO)
        pregrad_ref[rows, :channels] = jnp.concatenate(low_rate[::-1], axis=0).astype(bf16)
        pregrad_ref[rows, channels:] = jnp.concatenate(low_entry[::-1], axis=0).astype(bf16)
        return later, logit_sum, rate_sum, entry_sum

    zero = jnp.zeros((8, channels), f32)
    _, logit_sum, rate_sum, entry_sum = lax.fori_loop(
        0, OWN // HALO, gate_grads, (back, zero, zero, zero), unroll=2
    )
    for step in range(0, channels, 128):
        columns = slice(step, step + 128)
        cgrad_ref[:, columns] += lax.dot_general(
            pregrad_ref[...],
            gates_ref[columns, :],
            (((1,), (1,)), ((), ())),
            preferred_element_type=f32,
        )

    def spread(tile):
        at = slice(tile * HALO, (tile + 1) * HALO)
        rows, places = cgrad_ref[at, :], place_ref[at, :]
        return [rows] + [jnp.where(places >= tap, rows, 0.0) for tap in range(1, CONV)]

    def shifted_sum(current, following):
        total = taps_ref[0:1, :] * current[0]
        for tap in range(1, CONV):
            both = jnp.concatenate([current[tap], following[tap]], axis=0)
            total = total + taps_ref[tap : tap + 1, :] * pltpu.roll(both, 2 * HALO - tap, 0)[:HALO]
        return total

    nothing = [jnp.zeros((HALO, channels), f32)] * CONV
    shift_sum, tap_sums = nothing[0], list(nothing)
    tiles = OWN // HALO
    coming = spread(0)
    owed_ref[...] = shifted_sum(nothing, coming)
    for tile in range(tiles):
        grads, coming = coming, spread(tile + 1) if tile + 1 < tiles else nothing
        igrad_ref[tile * HALO : (tile + 1) * HALO, :] = shifted_sum(grads, coming)
        inputs = conv_rows(ci_ref, halo_ref, tile)
        shift_sum = shift_sum + grads[0]
        tap_sums[0] = tap_sums[0] + grads[0] * inputs[HALO:]
        for tap in range(1, CONV):
            tap_sums[tap] = tap_sums[tap] + grads[tap] * pltpu.roll(inputs, tap, 0)[HALO:]

    def total_rows(values):
        return jnp.sum(values, axis=0, keepdims=True)

    sums_ref[...] += jnp.concatenate(
        [total_rows(v) for v in [shift_sum, rate_sum, entry_sum, logit_sum] + tap_sums], axis=0
    )


def in_hbm(values):
    return pltpu.with_memory_space_constraint(values, pltpu.HBM)


def by_slot(kernel, outs, ins, scratch, scalars, moved, far_outs=None):
    whole = [pl.BlockSpec(a.shape, lambda i, n=a.ndim: (0,) * n) for a in ins if not isinstance(a, tuple)]
    parts = [
        pl.BlockSpec((rows, a.shape[1]), lambda i, first=first: (first + i, 0))
        for a, rows, first in (a for a in ins if isinstance(a, tuple))
    ]
    out_specs = [
        pl.BlockSpec(shape, lambda i: (0, 0))
        if rows is None
        else pl.BlockSpec((rows, shape[1]), lambda i: (i, 0))
        for rows, shape, _ in outs
    ]
    return pl.pallas_call(
        kernel,
        grid=(MEMBERS,),
        in_specs=[pl.BlockSpec(memory_space=pltpu.SMEM)] * len(scalars) + whole + parts,
        out_specs=out_specs,
        out_shape=[
            pltpu.HBM(shape, dtype) if far else jax.ShapeDtypeStruct(shape, dtype)
            for (_, shape, dtype), far in zip(outs, far_outs or [False] * len(outs))
        ],
        scratch_shapes=[pltpu.VMEM(shape, dtype) for shape, dtype in scratch],
        compiler_params=pltpu.CompilerParams(vmem_limit_bytes=16 * 1024 * 1024),
        cost_estimate=pl.CostEstimate(flops=0, bytes_accessed=moved, transcendentals=0),
    )(*scalars, *[a[0] if isinstance(a, tuple) else a for a in ins])


def in_vmem(kernel, outs, scratch=(), scalars=0, count=1, moved=0):
    vmem = pl.BlockSpec(memory_space=pltpu.VMEM)
    smem = pl.BlockSpec(memory_space=pltpu.SMEM)
    return pl.pallas_call(
        kernel,
        out_shape=[jax.ShapeDtypeStruct(shape, dtype) for shape, dtype in outs],
        in_specs=[smem] * scalars + [vmem] * count,
        out_specs=[vmem] * len(outs),
        scratch_shapes=[pltpu.VMEM(shape, dtype) for shape, dtype in scratch],
        compiler_params=pltpu.CompilerParams(vmem_limit_bytes=16 * 1024 * 1024),
        cost_estimate=pl.CostEstimate(flops=0, bytes_accessed=moved, transcendentals=0),
    )


def exchange_edges(edges, spots, backward):
    channels = edges.shape[1]
    near = jnp.stack([edges, hop(edges, "core", 1)])
    total, prefix = in_vmem(
        functools.partial(fold_near_kernel, backward),
        [((8, channels), f32)] * 2,
        [((4, 2, 8, channels), f32)],
        scalars=1,
        count=4,
        moved=3_000_000,
    )(spots, *direct_gather(near, "z"))
    return direct_gather(total, "y") + [prefix], near


def outer_kernel(lhs_one, lhs_two, rhs_one, rhs_two, rhs_three, out_ref):
    def settle(lhs, rhs):
        out_ref[...] = lax.dot_general(
            lhs[...], rhs[...], (((0,), (0,)), ((), ())), preferred_element_type=f32
        ).astype(bf16)

    for step, (lhs, rhs) in enumerate(
        ((lhs_one, rhs_one), (lhs_one, rhs_two), (lhs_two, rhs_three))
    ):
        pl.when(pl.program_id(0) == step)(functools.partial(settle, lhs, rhs))


def feed_outer(lhs_one, lhs_two, rhs):
    rows, features = lhs_one.shape
    columns = rhs[0].shape[1]
    height = 2048
    whole = pl.BlockSpec(
        (rows, columns), lambda j, i: (0, 0), pipeline_mode=pl.Buffered(buffer_count=1)
    )
    return pl.pallas_call(
        outer_kernel,
        grid=(3, features // height),
        in_specs=[
            pl.BlockSpec((rows, height), lambda j, i: (0, jnp.where(j < 2, i, 0))),
            pl.BlockSpec((rows, height), lambda j, i: (0, jnp.where(j < 2, 0, i))),
            whole,
            whole,
            whole,
        ],
        out_specs=pl.BlockSpec((height, columns), lambda j, i: (i, j)),
        out_shape=pltpu.HBM((features, 3 * columns), bf16),
        compiler_params=pltpu.CompilerParams(vmem_limit_bytes=44 * 1024 * 1024),
        cost_estimate=pl.CostEstimate(
            flops=6 * rows * features * columns,
            bytes_accessed=6 * features * columns,
            transcendentals=0,
        ),
    )(lhs_one, lhs_two, *rhs)


def small_kernel(cut, conv_ref, pregrad_ref, sums_ref, extra_ref, out_ref):
    channels = conv_ref.shape[1]
    width = 2 * channels
    block = cut * TOKS
    dense = lax.dot_general(
        conv_ref[...],
        pregrad_ref[...],
        (((0,), (0,)), ((), ())),
        preferred_element_type=f32,
    )
    columns = lax.broadcasted_iota(jnp.int32, (block, width), 1)
    columns = jnp.where(columns >= channels, columns - channels, columns)
    gates = jnp.zeros((block, width), f32)
    for group in range(channels // block):
        inside = (columns >= group * block) & (columns < (group + 1) * block)
        gates = jnp.where(inside, dense[group * block : (group + 1) * block], gates)
    own = channels // TOKS
    sums = sums_ref[...]
    blank = jnp.zeros((4, channels - 256), f32)
    spare = jnp.zeros((SMALL - 2 * cut - 5, channels), f32)
    for tok in range(TOKS):
        rows = gates[tok * cut : (tok + 1) * cut]
        turned_sums = pltpu.roll(sums, channels - tok * own, 1) if tok else sums
        vectors = [turned_sums[:4, :128], turned_sums[4:, :128], blank]
        pieces = [rows[:, :channels], rows[:, channels:], jnp.concatenate(vectors, axis=1)]
        pieces += [extra_ref[tok : tok + 1, :], spare]
        out_ref[tok] = jnp.concatenate(pieces, axis=0).astype(bf16)


def halves_kernel(count, small, spot_ref, *refs):
    core = spot_ref[3]
    small_ref, refs = (refs[0], refs[1:]) if small else (None, refs)
    mine_ref, theirs_ref = refs[2 * count :]
    chips, rows, _ = mine_ref.shape
    rows = (rows - small) // count
    for which in range(count):
        sums = lax.dot_general(
            refs[which][...],
            refs[count + which][...],
            (((0,), (0,)), ((), ())),
            preferred_element_type=f32,
        )
        for chip in range(chips):
            low = sums[2 * chip * rows : (2 * chip + 1) * rows]
            high = sums[(2 * chip + 1) * rows : (2 * chip + 2) * rows]
            at = slice(which * rows, (which + 1) * rows)
            mine_ref[chip, at, :] = jnp.where(core == 0, low, high).astype(bf16)
            theirs_ref[chip, at, :] = jnp.where(core == 0, high, low).astype(bf16)
    for chip in range(chips if small else 0):
        low, high = small_ref[2 * chip].astype(f32), small_ref[2 * chip + 1].astype(f32)
        at = slice(count * rows, count * rows + small)
        mine_ref[chip, at, :] = jnp.where(core == 0, low, high).astype(bf16)
        theirs_ref[chip, at, :] = jnp.where(core == 0, high, low).astype(bf16)


def outer_halves(spots, small, lhs, rhs, part):
    count = len(lhs)
    rows, columns = rhs[0].shape
    height = 1024
    chips = height // 128
    extra = SMALL if small is not None else 0
    total = 64 * count + extra
    shape = jax.ShapeDtypeStruct((chips, total, columns), bf16)
    out_spec = pl.BlockSpec((chips, total, columns), lambda i: (0, 0, 0))
    return pl.pallas_call(
        functools.partial(halves_kernel, count, extra),
        grid=(1,),
        in_specs=[pl.BlockSpec(memory_space=pltpu.SMEM)]
        + [pl.BlockSpec((2 * chips, SMALL, columns), lambda i: (part, 0, 0))] * (extra > 0)
        + [pl.BlockSpec((rows, height), lambda i: (0, part))] * count
        + [pl.BlockSpec((rows, columns), lambda i: (0, 0))] * count,
        out_specs=[out_spec] * 2,
        out_shape=[shape] * 2,
        compiler_params=pltpu.CompilerParams(vmem_limit_bytes=28 * 1024 * 1024),
        cost_estimate=pl.CostEstimate(
            flops=2 * count * rows * height * columns,
            bytes_accessed=0,
            transcendentals=0,
        ),
    )(spots, *([small] if extra else []), *lhs, *rhs)


def per_device(
    inputs,
    mix_scale,
    branch_mat,
    input_mat,
    conv_taps,
    conv_shift,
    rate_mat,
    rate_shift,
    entry_mat,
    entry_shift,
    decay_logit,
    out_mat,
    feed_scale,
    gate_mat,
    up_mat,
    down_mat,
    lengths,
    cotangent,
):
    blk = lax.axis_index("blk")
    tok = lax.axis_index("tok")
    spot = (tok // 8, (tok // 2) % 4, tok % 2)
    spots = jnp.stack([tok] + list(spot)).astype(jnp.int32)
    channels = branch_mat.shape[1]
    hidden_units = gate_mat.shape[1]
    slice_rows = branch_mat.shape[0]
    total_rows = MEMBERS * OWN

    groups, cut, block = rate_mat.shape
    own_channels = conv_shift.shape[0]
    vectors = [conv_taps, conv_shift[None], rate_shift[None], entry_shift[None], decay_logit[None]]
    vectors = jnp.concatenate(vectors, axis=0).reshape(-1)
    extras = jnp.concatenate([vectors, mix_scale, feed_scale])
    extras = jnp.pad(extras, (0, channels - extras.shape[0]))[None]
    smalls = [jnp.moveaxis(mats, 0, 1).reshape(cut, channels) for mats in (rate_mat, entry_mat)]
    smalls = jnp.concatenate(smalls + [extras], axis=0)
    smalls = jnp.pad(smalls, ((0, HALO - smalls.shape[0]), (0, 0)))
    input_blocks = ring_gather(inputs, spot[2])
    near = after(small_gather(smalls, (input_blocks[1], input_blocks[3])), input_blocks[2])
    for axis, place in ((2, spot[2]), (1, spot[1]), (0, spot[0])):
        near = jnp.roll(near, place, axis)
    near = near.reshape(TOKS, HALO, channels)
    mixer_all = lax.all_gather(
        jnp.concatenate([input_mat, branch_mat, out_mat.T], axis=1), "tok", axis=0, tiled=True
    )
    devices = MEMBERS * TOKS
    tail = lax.ppermute(
        inputs[OWN - HALO :], ("blk", "tok"), [(i, (i + 1) % devices) for i in range(devices)]
    )
    cotangent_blocks = ring_gather(after(cotangent, input_blocks[2]), spot[2])
    rows_all = jnp.concatenate(input_blocks + direct_gather(tail), axis=0)
    cotangent_all = jnp.concatenate(cotangent_blocks, axis=0)

    extras = near[:, 2 * cut]
    vectors = extras[:, : 8 * own_channels].reshape(TOKS, 8, own_channels).astype(f32)
    vectors = jnp.moveaxis(vectors, 0, 1).reshape(8, channels)
    gains = extras[:, 8 * own_channels : 8 * own_channels + 2 * slice_rows].astype(f32)
    mix_gain = gains[:, :slice_rows].reshape(1, -1)
    feed_gain = gains[:, slice_rows:].reshape(1, -1)
    wide_values = rows_all.astype(f32)
    wide_one = (wide_values * norm_factor(wide_values) * mix_gain).astype(bf16)
    taps, shift = vectors[:CONV], vectors[4:5]
    bias = jnp.concatenate([vectors[5:6], vectors[6:7]], axis=1)
    soft = decay_power * jax.nn.softplus(-vectors[7:8])
    blocks = [near[:, i * cut : (i + 1) * cut].reshape(block, channels) for i in range(2)]
    blocks = after(jnp.concatenate(blocks, axis=1), cotangent_blocks[2])
    feed_own = jnp.concatenate([gate_mat, up_mat, down_mat.T], axis=1)
    feed_all = lax.all_gather(after(feed_own, wide_one, blocks), "tok", axis=0, tiled=True)
    gate_up_all = feed_all[:, : 2 * hidden_units]
    down_turned = feed_all[:, 2 * hidden_units :]
    own_one = wide_one[:total_rows]
    input_all = mixer_all[:, :channels]
    branch_all = mixer_all[:, channels : 2 * channels]
    project_all = mixer_all[:, : 2 * channels]
    out_turned = mixer_all[:, 2 * channels : 3 * channels]

    slots = (blk + jnp.arange(MEMBERS, dtype=jnp.int32)) % MEMBERS
    token_ids = (
        (slots * TOKS + tok)[:, None] * OWN + jnp.arange(OWN, dtype=jnp.int32)[None, :]
    ).reshape(-1)
    starts = jnp.cumsum(lengths) - lengths
    opened = jnp.max(jnp.where(starts[None, :] <= token_ids[:, None], starts[None, :], 0), axis=1)
    places = (token_ids - opened).reshape(total_rows, 1).astype(jnp.int32)

    conv_input = product(wide_one, input_all, bf16)
    branch = product(own_one, branch_all)
    halo_first = total_rows // HALO
    conv, rates, entries, local, cum, edges, gates = by_slot(
        local_forward_kernel,
        [(OWN, (total_rows, channels), kind) for kind in (bf16, f32, bf16, f32, f32)]
        + [(None, (8, channels), f32), (None, (channels, 2 * channels), bf16)],
        [
            taps,
            shift,
            blocks,
            bias,
            soft,
            (conv_input, OWN, 0),
            (conv_input, HALO, halo_first),
            (places, OWN, 0),
        ],
        [((OWN, 2 * channels), f32), ((OWN, channels), f32)],
        (),
        30_000_000,
        [True, True, True, False, False, False, True],
    )
    conv, rates, entries, gates = [in_hbm(a) for a in (conv, rates, entries, gates)]
    chains, _ = exchange_edges(edges, spots, False)
    states, mixture, carried = by_slot(
        mix_kernel,
        [
            (OWN, (total_rows, channels), bf16),
            (OWN, (total_rows, channels), bf16),
            (None, (MEMBERS, channels), f32),
        ],
        [*chains] + [(a, OWN, 0) for a in (local, cum, branch)],
        [((4, 8, channels), f32)],
        (spots,),
        4_500_000,
    )

    def rows_of(values):
        return [values[j * OWN : (j + 1) * OWN] for j in range(MEMBERS)]

    own_values = inputs.astype(f32)
    middle = own_values + ring_scatter(rows_of(product_back(mixture, out_turned, bf16)), spot[2])

    factor_two = norm_factor(middle)
    normed_two = (middle * factor_two * feed_gain).astype(bf16)
    hidden_grad = product(after(cotangent_all, mixture), down_turned)
    blocks_two = ring_gather(normed_two, spot[2])
    blocks_two[2] = after(blocks_two[2], hidden_grad)
    wide_two = jnp.concatenate(blocks_two, axis=0)
    gate_up = product(wide_two, gate_up_all)
    gate_pre, up_pre = gate_up[:, :hidden_units], gate_up[:, hidden_units:]
    gate_act, gate_slope = gelu_parts(gate_pre)
    hidden = (gate_act * up_pre).astype(bf16)
    gate_grad = (gate_slope * hidden_grad * up_pre).astype(bf16)
    up_grad = (gate_act * hidden_grad).astype(bf16)
    feed_shares = feed_outer(wide_two, cotangent_all, (gate_grad, up_grad, hidden))
    feed_grads = lax.psum_scatter(feed_shares, "tok", scatter_dimension=0, tiled=True)
    gate_late, up_late = after((gate_grad, up_grad), feed_shares)
    two_shares = product_back(jnp.concatenate([gate_late, up_late], axis=1), gate_up_all, bf16)
    two_parts = rows_of(two_shares)
    two_far, two_near = ring_open(two_parts, spot[2])
    two_grad = ring_close(two_parts, two_near, ring_pass(two_parts, two_far, spot[2]))
    middle_grad = cotangent.astype(f32) + normalize_back(two_grad, middle, factor_two, feed_gain)
    grad_feed_scale = jnp.sum(two_grad * middle * factor_two, axis=0)
    layer_shares = product_back(after(hidden, two_far), down_turned, bf16)
    middle_blocks = ring_gather(middle_grad.astype(bf16), spot[2])
    middle_blocks[2] = after(middle_blocks[2], layer_shares)
    middle_wide = jnp.concatenate(middle_blocks, axis=0)
    mixture_grad = product(middle_wide, out_turned)
    branch = in_hbm(branch)
    branch_grad, back_edges = by_slot(
        local_backward_kernel,
        [(OWN, (total_rows, channels), bf16), (None, (8, channels), f32)],
        [soft] + [(a, OWN, 0) for a in (mixture_grad, branch, states, rates, places)],
        (),
        (),
        9_500_000,
    )
    chains_back, near_back = exchange_edges(back_edges, spots, True)
    pregrads, igrad, owed, sums = by_slot(
        finish_backward_kernel,
        [
            (OWN, (total_rows, 2 * channels), bf16),
            (OWN, (total_rows, channels), f32),
            (HALO, (MEMBERS * HALO, channels), f32),
            (None, (8, channels), f32),
        ],
        [*chains_back, carried, soft, taps, gates]
        + [(a, OWN, 0) for a in (mixture_grad, branch, states, conv, rates, entries)]
        + [(places, OWN, 0), (conv_input, OWN, 0), (conv_input, HALO, halo_first)],
        [
            ((OWN, channels), f32),
            ((MEMBERS, channels), f32),
            ((4, 8, channels), f32),
        ],
        (spots,),
        40_000_000,
    )
    returned = lax.ppermute(
        owed.reshape(MEMBERS, HALO, channels)[:, HALO - 3 :],
        "tok",
        [(i, (i - 1) % TOKS) for i in range(TOKS)],
    )
    turned_on = jnp.concatenate([returned[1:], returned[:1]], axis=0)
    landing = jnp.where(tok == TOKS - 1, turned_on, returned)
    input_grad = igrad.reshape(MEMBERS, OWN, channels) + jnp.pad(
        landing, ((0, 0), (OWN - 3, 0), (0, 0))
    )
    input_low = input_grad.reshape(total_rows, channels).astype(bf16)
    feed_rows = jnp.pad(
        grad_feed_scale.reshape(TOKS, slice_rows), ((0, 0), (0, channels - slice_rows))
    )
    (small_rows,) = in_vmem(
        functools.partial(small_kernel, cut),
        [((TOKS, SMALL, channels), bf16)],
        count=4,
        moved=11_000_000,
    )(conv, pregrads, sums, feed_rows)

    core = spot[2]
    chips_one, chips_two = [
        outer_halves(
            spots, small_rows, (middle_wide, wide_one, wide_one), (mixture, branch_grad, low), part
        )
        for part, low in enumerate((input_low, input_low))
    ]
    other_one = hop(chips_one[1], "core", 1)
    other_two = hop(chips_two[1], "core", 1)
    late = after(input_low, chips_two[1])
    one_shares = product_back(jnp.concatenate([late, branch_grad], axis=1), project_all, bf16)
    weight_chip = jnp.concatenate(
        [narrow_sum(chips_one[0], other_one), narrow_sum(chips_two[0], other_two)], axis=0
    )
    one_shares = after(one_shares, weight_chip)
    one_parts = rows_of(one_shares)
    one_grad = ring_scatter(one_parts, core)
    factor_one = norm_factor(own_values)
    first_grad = normalize_back(one_grad, own_values, factor_one, mix_gain)
    inputs_grad = (middle_grad + first_grad).astype(bf16)
    settled = chips_sum(weight_chip)
    layer_out = middle + ring_scatter(rows_of(after(layer_shares, one_grad)), core)
    grad_out, grad_branch, grad_input = [
        settled[i * slice_rows : (i + 1) * slice_rows] for i in range(3)
    ]
    settled = settled[3 * slice_rows :]
    grad_mix_scale = jnp.sum(
        grad_branch * branch_mat.astype(f32) + grad_input * input_mat.astype(f32), axis=1
    ) / mix_scale.astype(f32)
    gains_own = jnp.concatenate([grad_mix_scale, settled[2 * cut + 4, :slice_rows]])
    gains_own = hop_sum(gains_own.reshape(1, -1), "blk")[0]
    gate_own = [
        jnp.moveaxis(settled[i * cut : (i + 1) * cut].reshape(cut, groups, block), 1, 0)
        for i in range(2)
    ]
    sums_own = settled[2 * cut : 2 * cut + 4]
    taps_own = sums_own[:, 128 : 128 + own_channels]
    sums_own = sums_own[:, :own_channels]
    own_logits = decay_logit.astype(f32)
    return (
        layer_out.astype(bf16),
        inputs_grad,
        gains_own[:slice_rows],
        grad_branch,
        grad_input,
        taps_own,
        sums_own[0],
        gate_own[0],
        sums_own[1],
        gate_own[1],
        sums_own[2],
        sums_own[3] * decay_power * jax.nn.sigmoid(-own_logits),
        grad_out.T,
        gains_own[slice_rows : 2 * slice_rows],
        feed_grads[:, :hidden_units].astype(f32),
        feed_grads[:, hidden_units : 2 * hidden_units].astype(f32),
        feed_grads[:, 2 * hidden_units :].T.astype(f32),
    )


def solution(mesh):
    in_specs = (
        P(("blk", "tok"), None),
        P("tok"),
        P("tok", "blk"),
        P("tok", "blk"),
        P(None, ("blk", "tok")),
        P(("blk", "tok")),
        P("blk", "tok", None),
        P(("blk", "tok")),
        P("blk", "tok", None),
        P(("blk", "tok")),
        P(("blk", "tok")),
        P("blk", "tok"),
        P("tok"),
        P("tok", "blk"),
        P("tok", "blk"),
        P("blk", "tok"),
        P(),
        P(("blk", "tok"), None),
    )
    out_specs = (
        P(("blk", "tok"), None),
        P(("blk", "tok"), None),
        P("tok"),
        P("tok", "blk"),
        P("tok", "blk"),
        P(None, ("blk", "tok")),
        P(("blk", "tok")),
        P("blk", "tok", None),
        P(("blk", "tok")),
        P("blk", "tok", None),
        P(("blk", "tok")),
        P(("blk", "tok")),
        P("blk", "tok"),
        P("tok"),
        P("tok", "blk"),
        P("tok", "blk"),
        P("blk", "tok"),
    )
    return jax.shard_map(
        per_device, mesh=mesh, in_specs=in_specs, out_specs=out_specs, check_vma=False
    )
```
